32 devices in a mesh: dp: 16 (over z, y, x), tensor: 2 (over core).
Axes of the slice: x: 2, y: 2, z: 4, core: 2. Of those that a mesh axis runs over, the one named last changes fastest.
Arguments:
- features: bfloat16 [16384, 2048], P('dp'), may hold values from -24 to 24
- keep_mask: int32 [16384], P('dp'), may hold values from 0 to 1, as said below
- proj_up: float32 [2048, 4096], P('dp', 'tensor'), may hold values from -0.125 to 0.125
- proj_down: float32 [256, 4096], P('dp', 'tensor'), may hold values from -0.09375 to 0.09375
- proj_norm: float32 [2, 4096], P(None, 'tensor'), may hold values from -1 to 1.4, as said below
- pred_up: float32 [256, 4096], P('dp', 'tensor'), may hold values from -0.375 to 0.375
- pred_down: float32 [256, 4096], P('dp', 'tensor'), may hold values from -0.09375 to 0.09375
- pred_norm: float32 [2, 4096], P(None, 'tensor'), may hold values from -1 to 1.4, as said below
- moment_proj_up: float32 [2048, 4096], P('dp', 'tensor'), may hold values from -0.00015258789 to 0.00015258789
- moment_proj_down: float32 [256, 4096], P('dp', 'tensor'), may hold values from -0.0008544922 to 0.0008544922
- moment_proj_norm: float32 [2, 4096], P(None, 'tensor'), may hold values from -0.00015258789 to 0.00015258789
- moment_pred_up: float32 [256, 4096], P('dp', 'tensor'), may hold values from -0.00024414062 to 0.00024414062
- moment_pred_down: float32 [256, 4096], P('dp', 'tensor'), may hold values from -0.0012207031 to 0.0012207031
- moment_pred_norm: float32 [2, 4096], P(None, 'tensor'), may hold values from -0.000328125 to 0.000328125
- target_up: float32 [2048, 4096], P('dp', 'tensor'), may hold values from -0.125 to 0.125
- target_down: float32 [256, 4096], P('dp', 'tensor'), may hold values from -0.09375 to 0.09375
- target_norm: float32 [2, 4096], P(None, 'tensor'), may hold values from -1 to 1.4, as said below
Outputs:
- loss: float32 [], replicated
- input_grad: float32 [16384, 2048], P('dp', 'tensor')
- proj_up_grad: float32 [2048, 4096], P('dp', 'tensor')
- proj_up_moment: float32 [2048, 4096], P('dp', 'tensor')
- proj_up_next: float32 [2048, 4096], P('dp', 'tensor')
- proj_down_grad: float32 [256, 4096], P('dp', 'tensor')
- proj_down_moment: float32 [256, 4096], P('dp', 'tensor')
- proj_down_next: float32 [256, 4096], P('dp', 'tensor')
- proj_norm_grad: float32 [2, 4096], P(None, 'tensor')
- proj_norm_moment: float32 [2, 4096], P(None, 'tensor')
- proj_norm_next: float32 [2, 4096], P(None, 'tensor')
- pred_up_grad: float32 [256, 4096], P('dp', 'tensor')
- pred_up_moment: float32 [256, 4096], P('dp', 'tensor')
- pred_up_next: float32 [256, 4096], P('dp', 'tensor')
- pred_down_grad: float32 [256, 4096], P('dp', 'tensor')
- pred_down_moment: float32 [256, 4096], P('dp', 'tensor')
- pred_down_next: float32 [256, 4096], P('dp', 'tensor')
- pred_norm_grad: float32 [2, 4096], P(None, 'tensor')
- pred_norm_moment: float32 [2, 4096], P(None, 'tensor')
- pred_norm_next: float32 [2, 4096], P(None, 'tensor')
- target_up_next: float32 [2048, 4096], P('dp', 'tensor')
- target_down_next: float32 [256, 4096], P('dp', 'tensor')
- target_norm_next: float32 [2, 4096], P(None, 'tensor')
The draws below stay inside these ranges and needn't reach their ends.
Inputs may be any that keep to these rules, and one draw needn't show every extreme that they name: `keep_mask`: 1 marks a view whose loss term counts; the last view always counts. `proj_norm`: row 0 positive. `pred_norm`: row 0 positive. `target_norm`: row 0 positive.
All inputs are finite; a program needn't handle non-finite values.
Results may differ from the reference program's by a relative error of at most 0.022.
Values may be sent and summed in bfloat16 or wider, within the bound.
A program may use at most 192 MiB of HBM per device.

```python
import math
import jax
import jax.numpy as jnp
from jax import lax

D_IN = 2048
HID = 4096
OUT = 256
VIEWS = 16384


def draw_features(key, part):
    key = jax.random.fold_in(key, 11)
    base_key, mean_key, factor_key, load_key = jax.random.split(key, 4)
    place = jnp.arange(VIEWS, dtype=jnp.float32) / (VIEWS - 1)
    offset = 0.5 * jax.random.uniform(mean_key, (D_IN,), jnp.float32)
    directions = jax.random.normal(factor_key, (8, D_IN), jnp.float32)
    loads = jax.random.normal(load_key, (VIEWS, 8), jnp.float32)
    common = jnp.zeros((VIEWS, D_IN), jnp.float32)
    for factor in range(8):
        common = common + loads[:, factor:factor + 1] * directions[factor][None, :]
    scale = 1.0 + 2.0 * place
    base = jax.random.truncated_normal(base_key, -4.0, 4.0, (VIEWS, D_IN), jnp.float32)
    values = scale[:, None] * (base + offset[None, :] + 0.45 * common)
    return jnp.clip(values, -24.0, 24.0).astype(jnp.bfloat16)


def draw_keep_mask(key, part):
    key = jax.random.fold_in(key, 12)
    place = jnp.arange(VIEWS, dtype=jnp.int32)
    limit = 300 + 600 * place // VIEWS
    value = jax.random.randint(key, (VIEWS,), 0, 1000, jnp.int32)
    kept = jnp.where(value < limit, 1, 0).astype(jnp.int32)
    return jnp.where(place == VIEWS - 1, 1, kept).astype(jnp.int32)


def draw_proj_norm(key, part):
    key = jax.random.fold_in(key, 13)
    gain_key, shift_key = jax.random.split(key)
    gain = 1.0 + 0.1 * jax.random.truncated_normal(gain_key, -3.0, 3.0, (HID,), jnp.float32)
    shift = 0.25 * jax.random.truncated_normal(shift_key, -4.0, 4.0, (HID,), jnp.float32)
    return jnp.stack([gain, shift]).astype(jnp.float32)


def draw_pred_norm(key, part):
    key = jax.random.fold_in(key, 14)
    gain_key, shift_key = jax.random.split(key)
    gain = 1.0 + 0.1 * jax.random.truncated_normal(gain_key, -3.0, 3.0, (HID,), jnp.float32)
    shift = 0.25 * jax.random.truncated_normal(shift_key, -4.0, 4.0, (HID,), jnp.float32)
    return jnp.stack([gain, shift]).astype(jnp.float32)


def draw_target_norm(key, part):
    key = jax.random.fold_in(key, 15)
    gain_key, shift_key = jax.random.split(key)
    gain = 1.0 + 0.1 * jax.random.truncated_normal(gain_key, -3.0, 3.0, (HID,), jnp.float32)
    shift = 0.25 * jax.random.truncated_normal(shift_key, -4.0, 4.0, (HID,), jnp.float32)
    return jnp.stack([gain, shift]).astype(jnp.float32)


def draw_moment_pred_norm(key, part):
    key = jax.random.fold_in(key, 16)
    factor = 1.0 / float(VIEWS) ** 0.5
    values = 0.014 * jax.random.truncated_normal(key, -3.0, 3.0, (2, HID), jnp.float32)
    return (values * factor).astype(jnp.float32)


def steps_of(stream_key, shape, cuts, smallest, largest):
    loudness, own = 1.0, jax.random.fold_in(stream_key, 6)
    for position, blocks in cuts:
        heights = jnp.exp(jax.random.uniform(jax.random.fold_in(own, position), (blocks,), jnp.float32, smallest / len(cuts), largest / len(cuts)))
        loudness = loudness * jnp.repeat(heights, shape[position] // blocks).reshape([-1 if axis == position else 1 for axis in range(len(shape))])
    return loudness


def noise(stream_key, extent, scale, most, pieces=(), kind=jnp.bfloat16):
    level = steps_of(stream_key, extent, pieces, -0.22, 0.18) if pieces else 1.0
    array = jax.random.normal(stream_key, extent, jnp.float32) * scale * level
    return jnp.minimum(jnp.maximum(array, -most), most).astype(kind)


def setup_inputs(seed: int = 0) -> dict:
    arg_keys = jax.random.split(jax.random.key(seed), 18)
    return {
        "features": draw_features(jax.random.fold_in(arg_keys[17], 71), 0),
        "keep_mask": draw_keep_mask(jax.random.fold_in(arg_keys[17], 71), 0),
        "proj_up": noise(arg_keys[2], (D_IN, HID), D_IN ** -0.5, 0.125, ((0, 16), (1, 2)), jnp.float32),
        "proj_down": noise(arg_keys[3], (OUT, HID), HID ** -0.5, 0.09375, ((0, 16), (1, 2)), jnp.float32),
        "proj_norm": draw_proj_norm(jax.random.fold_in(arg_keys[17], 71), 0),
        "pred_up": noise(arg_keys[5], (OUT, HID), OUT ** -0.5, 0.375, ((0, 16), (1, 2)), jnp.float32),
        "pred_down": noise(arg_keys[6], (OUT, HID), HID ** -0.5, 0.09375, ((0, 16), (1, 2)), jnp.float32),
        "pred_norm": draw_pred_norm(jax.random.fold_in(arg_keys[17], 71), 0),
        "moment_proj_up": noise(arg_keys[8], (D_IN, HID), (0.0014 / VIEWS ** 0.5), 0.00015258789, ((0, 16), (1, 2)), jnp.float32),
        "moment_proj_down": noise(arg_keys[9], (OUT, HID), (0.0076 / VIEWS ** 0.5), 0.0008544922, ((0, 16), (1, 2)), jnp.float32),
        "moment_proj_norm": noise(arg_keys[10], (2, HID), (0.0014 / VIEWS ** 0.5), 0.00015258789, ((1, 2),), jnp.float32),
        "moment_pred_up": noise(arg_keys[11], (OUT, HID), (0.002 / VIEWS ** 0.5), 0.00024414062, ((0, 16), (1, 2)), jnp.float32),
        "moment_pred_down": noise(arg_keys[12], (OUT, HID), (0.010 / VIEWS ** 0.5), 0.0012207031, ((0, 16), (1, 2)), jnp.float32),
        "moment_pred_norm": draw_moment_pred_norm(jax.random.fold_in(arg_keys[17], 71), 0),
        "target_up": noise(arg_keys[14], (D_IN, HID), D_IN ** -0.5, 0.125, ((0, 16), (1, 2)), jnp.float32),
        "target_down": noise(arg_keys[15], (OUT, HID), HID ** -0.5, 0.09375, ((0, 16), (1, 2)), jnp.float32),
        "target_norm": draw_target_norm(jax.random.fold_in(arg_keys[17], 71), 0),
    }


NORM_EPS = 1e-05
UNIT_EPS = 1e-06
RATE_PROJ_UP = 9.0
RATE_PROJ_DOWN = 1.2
RATE_PROJ_NORM = 40.0
RATE_PRED_UP = 18.0
RATE_PRED_DOWN = 0.9
RATE_PRED_NORM = 30.0

@jax.custom_vjp
def low(v):
    return lax.optimization_barrier(v.astype(jnp.bfloat16)).astype(jnp.float32)

@jax.custom_vjp
def low_back(v):
    return v

def low_keep(v):
    return (low(v), None)

def low_pass(kept, grad):
    return (grad,)

def back_keep(v):
    return (v, None)

def back_low(kept, grad):
    return (low(grad),)
low.defvjp(low_keep, low_pass)
low_back.defvjp(back_keep, back_low)

def forward_mul(matrix, weight):
    return jnp.dot(matrix, weight, precision=lax.Precision.HIGHEST, preferred_element_type=jnp.float32)

def across(matrix, weight):
    return lax.dot_general(matrix, weight, (((1,), (1,)), ((), ())), precision=lax.Precision.HIGHEST, preferred_element_type=jnp.float32)

def batch_norm(hidden, params):
    middle_mean = lax.optimization_barrier(jnp.mean(hidden, 0))
    spread = lax.optimization_barrier(jnp.mean(hidden * hidden, 0)) - middle_mean * middle_mean
    return (hidden - middle_mean) * lax.rsqrt(spread + NORM_EPS) * params[0] + params[1]

def unit_rows(values):
    return values * lax.rsqrt(lax.optimization_barrier(jnp.sum(values * values, 1, keepdims=True)) + UNIT_EPS)

def partner(values):
    width = values.shape[1]
    return values.reshape(-1, 2, width)[:, ::-1, :].reshape(-1, width)

def target_branch(inputs, weight_up, weight_down, params):
    hidden = forward_mul(inputs, low(weight_up))
    action = low(jax.nn.gelu(batch_norm(hidden, params)))
    return across(action, low(weight_down))

def online_branch(inputs, proj_up, proj_down, proj_norm, pred_up, pred_down, pred_norm):
    hidden1 = low_back(forward_mul(inputs, low(proj_up)))
    action1 = low(jax.nn.gelu(batch_norm(hidden1, proj_norm)))
    middle = low(low_back(across(action1, low(proj_down))))
    hidden2 = low_back(forward_mul(middle, low(pred_up)))
    action2 = low(jax.nn.gelu(batch_norm(hidden2, pred_norm)))
    return low_back(across(action2, low(pred_down)))

def nesterov(weight, moment, grad, rate):
    fresh = 0.5 * moment + grad
    return (fresh, weight - rate * (grad + 0.5 * fresh))

def reference(features, keep_mask, proj_up, proj_down, proj_norm, pred_up, pred_down, pred_norm, moment_proj_up, moment_proj_down, moment_proj_norm, moment_pred_up, moment_pred_down, moment_pred_norm, target_up, target_down, target_norm):
    inputs = features.astype(jnp.float32)
    target_out = target_branch(inputs, target_up, target_down, target_norm)
    goal = partner(unit_rows(target_out))
    weights = keep_mask.astype(jnp.float32)
    count = jnp.sum(weights)

    def loss_fn(inputs, proj_up, proj_down, proj_norm, pred_up, pred_down, pred_norm):
        query = online_branch(inputs, proj_up, proj_down, proj_norm, pred_up, pred_down, pred_norm)
        cosine = lax.optimization_barrier(jnp.sum(unit_rows(query) * goal, 1))
        return jnp.sum(weights * (2.0 - 2.0 * cosine)) / count
    loss, pull = jax.vjp(loss_fn, inputs, proj_up, proj_down, proj_norm, pred_up, pred_down, pred_norm)
    grads = pull(jnp.ones((), jnp.float32))
    input_grad, g_pu, g_pd, g_pn, g_qu, g_qd, g_qn = grads
    scale = math.sqrt(VIEWS)
    m_pu, n_pu = nesterov(proj_up, moment_proj_up, g_pu, RATE_PROJ_UP * scale)
    m_pd, n_pd = nesterov(proj_down, moment_proj_down, g_pd, RATE_PROJ_DOWN * scale)
    m_pn, n_pn = nesterov(proj_norm, moment_proj_norm, g_pn, RATE_PROJ_NORM * scale)
    m_qu, n_qu = nesterov(pred_up, moment_pred_up, g_qu, RATE_PRED_UP * scale)
    m_qd, n_qd = nesterov(pred_down, moment_pred_down, g_qd, RATE_PRED_DOWN * scale)
    m_qn, n_qn = nesterov(pred_norm, moment_pred_norm, g_qn, RATE_PRED_NORM * scale)
    t_up = 0.5 * target_up + 0.5 * n_pu
    t_down = 0.5 * target_down + 0.5 * n_pd
    t_norm = 0.5 * target_norm + 0.5 * n_pn
    return (loss, input_grad, g_pu, m_pu, n_pu, g_pd, m_pd, n_pd, g_pn, m_pn, n_pn, g_qu, m_qu, n_qu, g_qd, m_qd, n_qd, g_qn, m_qn, n_qn, t_up, t_down, t_norm)
```

```python
import math

import jax
import jax.numpy as jnp
from jax import lax
from jax.sharding import PartitionSpec as P

NORM_EPS = 1e-05
UNIT_EPS = 1e-06
RATE_PROJ_UP = 9.0
RATE_PROJ_DOWN = 1.2
RATE_PROJ_NORM = 40.0
RATE_PRED_UP = 18.0
RATE_PRED_DOWN = 0.9
RATE_PRED_NORM = 30.0


def across(matrix, weight):
    return lax.dot_general(
        matrix, weight, (((1,), (1,)), ((), ())), preferred_element_type=jnp.float32
    )


def outer_sum(first_op, second_op):
    return lax.dot_general(
        first_op, second_op, (((0,), (0,)), ((), ())), preferred_element_type=jnp.float32
    )


def standard(hidden, col_sum, col_square, total_views):
    middle_mean = col_sum / total_views
    inverse = lax.rsqrt(col_square / total_views - middle_mean * middle_mean + NORM_EPS)
    return ((hidden - middle_mean) * inverse, inverse)


def norm_back(grad_out, scaled, inverse, params, sum_grad, sum_cross, total_views):
    return (
        params[0]
        * inverse
        * (grad_out - sum_grad / total_views - scaled * (sum_cross / total_views))
    )


def unit_rows(values):
    return values * lax.rsqrt(jnp.sum(values * values, 1, keepdims=True) + UNIT_EPS)


def partner(values):
    width = values.shape[1]
    return values.reshape(-1, 2, width)[:, ::-1, :].reshape(-1, width)


def nesterov(weight, moment, grad, rate):
    fresh = 0.5 * moment + grad
    return (fresh, weight - rate * (grad + 0.5 * fresh))


def body(
    features,
    keep_mask,
    proj_up,
    proj_down,
    proj_norm,
    pred_up,
    pred_down,
    pred_norm,
    moment_proj_up,
    moment_proj_down,
    moment_proj_norm,
    moment_pred_up,
    moment_pred_down,
    moment_pred_norm,
    target_up,
    target_down,
    target_norm,
):
    total_views = float(features.shape[0] * lax.axis_size("dp"))
    width = proj_up.shape[1]

    def gathered(parts):
        low = jnp.stack([part.astype(jnp.bfloat16) for part in parts])
        full = lax.all_gather(low, "dp", axis=1, tiled=True)
        return tuple(full[i] for i in range(len(parts)))

    (up_full, tup_full) = gathered((proj_up, target_up))
    (down_full, pup_full, pdown_full, tdown_full) = gathered(
        (proj_down, pred_up, pred_down, target_down)
    )
    keep_float = keep_mask.astype(jnp.float32)
    hidden1 = jnp.dot(features, up_full, preferred_element_type=jnp.float32)
    target_hidden = jnp.dot(features, tup_full, preferred_element_type=jnp.float32)
    sums = lax.psum(
        jnp.stack(
            [
                jnp.sum(hidden1, 0),
                jnp.sum(hidden1 * hidden1, 0),
                jnp.sum(target_hidden, 0),
                jnp.sum(target_hidden * target_hidden, 0),
                jnp.full((width,), jnp.sum(keep_float)),
            ]
        ),
        "dp",
    )
    sum_one, square_one, sum_target, square_target = sums[0], sums[1], sums[2], sums[3]
    count = sums[4, 0]
    scaled1, inverse1 = standard(hidden1, sum_one, square_one, total_views)
    action1, gelu_back1 = jax.vjp(jax.nn.gelu, scaled1 * proj_norm[0] + proj_norm[1])
    action1 = action1.astype(jnp.bfloat16)
    target_scaled, target_inverse = standard(target_hidden, sum_target, square_target, total_views)
    target_action = jax.nn.gelu(target_scaled * target_norm[0] + target_norm[1]).astype(
        jnp.bfloat16
    )
    middle, target_out = (
        lax.psum(across(action1, down_full).astype(jnp.bfloat16), "tensor").astype(jnp.float32),
        lax.psum(across(target_action, tdown_full).astype(jnp.bfloat16), "tensor").astype(
            jnp.float32
        ),
    )
    middle_low = middle.astype(jnp.bfloat16)
    hidden2 = jnp.dot(middle_low, pup_full, preferred_element_type=jnp.float32)
    sum_two, square_two = lax.psum(
        jnp.stack([jnp.sum(hidden2, 0), jnp.sum(hidden2 * hidden2, 0)]), "dp"
    )
    scaled2, inverse2 = standard(hidden2, sum_two, square_two, total_views)
    action2, gelu_back2 = jax.vjp(jax.nn.gelu, scaled2 * pred_norm[0] + pred_norm[1])
    action2 = action2.astype(jnp.bfloat16)
    query = lax.psum(across(action2, pdown_full).astype(jnp.bfloat16), "tensor").astype(jnp.float32)
    goal = partner(unit_rows(target_out))

    def loss_terms(values):
        return jnp.sum(keep_float * (2.0 - 2.0 * jnp.sum(unit_rows(values) * goal, 1)))

    local_loss, loss_back = jax.vjp(loss_terms, query)
    (grad_query,) = loss_back(1.0 / count)
    grad_query = grad_query.astype(jnp.bfloat16)
    grad_pred_down = outer_sum(grad_query, action2)
    (grad_norm2,) = gelu_back2(jnp.dot(grad_query, pdown_full, preferred_element_type=jnp.float32))
    back_sum2, back_cross2, loss_row = lax.psum(
        jnp.stack(
            [
                jnp.sum(grad_norm2, 0),
                jnp.sum(grad_norm2 * scaled2, 0),
                jnp.full((width,), local_loss),
            ]
        ),
        "dp",
    )
    loss_total = loss_row[0]
    grad_hidden2 = norm_back(
        grad_norm2, scaled2, inverse2, pred_norm, back_sum2, back_cross2, total_views
    ).astype(jnp.bfloat16)
    grad_pred_norm = jnp.stack([back_cross2, back_sum2])
    grad_pred_up = outer_sum(middle_low, grad_hidden2)
    grad_middle = lax.psum(across(grad_hidden2, pup_full).astype(jnp.bfloat16), "tensor")
    grad_proj_down = outer_sum(grad_middle, action1)
    (grad_norm1,) = gelu_back1(jnp.dot(grad_middle, down_full, preferred_element_type=jnp.float32))
    back_sum1, back_cross1 = lax.psum(
        jnp.stack([jnp.sum(grad_norm1, 0), jnp.sum(grad_norm1 * scaled1, 0)]), "dp"
    )
    grad_hidden1 = norm_back(
        grad_norm1, scaled1, inverse1, proj_norm, back_sum1, back_cross1, total_views
    ).astype(jnp.bfloat16)
    grad_proj_norm = jnp.stack([back_cross1, back_sum1])
    grad_proj_up = outer_sum(features, grad_hidden1)
    input_grad = lax.psum_scatter(
        across(grad_hidden1, up_full).astype(jnp.bfloat16),
        "tensor",
        scatter_dimension=1,
        tiled=True,
    ).astype(jnp.float32)
    shard_proj_up = lax.psum_scatter(
        grad_proj_up.astype(jnp.bfloat16), "dp", scatter_dimension=0, tiled=True
    ).astype(jnp.float32)
    small = lax.psum_scatter(
        jnp.stack([grad_proj_down, grad_pred_up, grad_pred_down]).astype(jnp.bfloat16),
        "dp",
        scatter_dimension=1,
        tiled=True,
    ).astype(jnp.float32)
    shard_proj_down, shard_pred_up, shard_pred_down = small[0], small[1], small[2]
    loss = loss_total / count
    scale = math.sqrt(total_views)
    mom_pu, next_pu = nesterov(proj_up, moment_proj_up, shard_proj_up, RATE_PROJ_UP * scale)
    mom_pd, next_pd = nesterov(proj_down, moment_proj_down, shard_proj_down, RATE_PROJ_DOWN * scale)
    mom_pn, next_pn = nesterov(proj_norm, moment_proj_norm, grad_proj_norm, RATE_PROJ_NORM * scale)
    mom_qu, next_qu = nesterov(pred_up, moment_pred_up, shard_pred_up, RATE_PRED_UP * scale)
    mom_qd, next_qd = nesterov(pred_down, moment_pred_down, shard_pred_down, RATE_PRED_DOWN * scale)
    mom_qn, next_qn = nesterov(pred_norm, moment_pred_norm, grad_pred_norm, RATE_PRED_NORM * scale)
    target_up_next = 0.5 * target_up + 0.5 * next_pu
    target_down_next = 0.5 * target_down + 0.5 * next_pd
    target_norm_next = 0.5 * target_norm + 0.5 * next_pn
    return (
        loss,
        input_grad,
        shard_proj_up,
        mom_pu,
        next_pu,
        shard_proj_down,
        mom_pd,
        next_pd,
        grad_proj_norm,
        mom_pn,
        next_pn,
        shard_pred_up,
        mom_qu,
        next_qu,
        shard_pred_down,
        mom_qd,
        next_qd,
        grad_pred_norm,
        mom_qn,
        next_qn,
        target_up_next,
        target_down_next,
        target_norm_next,
    )


def solution(mesh):
    placed = (
        P("dp", None),
        P("dp"),
        P("dp", "tensor"),
        P("dp", "tensor"),
        P(None, "tensor"),
        P("dp", "tensor"),
        P("dp", "tensor"),
        P(None, "tensor"),
        P("dp", "tensor"),
        P("dp", "tensor"),
        P(None, "tensor"),
        P("dp", "tensor"),
        P("dp", "tensor"),
        P(None, "tensor"),
        P("dp", "tensor"),
        P("dp", "tensor"),
        P(None, "tensor"),
    )
    return jax.shard_map(
        body,
        mesh=mesh,
        in_specs=placed,
        out_specs=(
            P(),
            P("dp", "tensor"),
            P("dp", "tensor"),
            P("dp", "tensor"),
            P("dp", "tensor"),
            P("dp", "tensor"),
            P("dp", "tensor"),
            P("dp", "tensor"),
            P(None, "tensor"),
            P(None, "tensor"),
            P(None, "tensor"),
            P("dp", "tensor"),
            P("dp", "tensor"),
            P("dp", "tensor"),
            P("dp", "tensor"),
            P("dp", "tensor"),
            P("dp", "tensor"),
            P(None, "tensor"),
            P(None, "tensor"),
            P(None, "tensor"),
            P("dp", "tensor"),
            P("dp", "tensor"),
            P(None, "tensor"),
        ),
        check_vma=False,
    )
```

```python
import functools
import math

import jax
import jax.numpy as jnp
from jax import lax
from jax.experimental import pallas as pl
from jax.experimental.pallas import tpu as pltpu
from jax.sharding import PartitionSpec as P

NORM_EPS = 1e-05
UNIT_EPS = 1e-06
RATE_PROJ_UP = 9.0
RATE_PROJ_DOWN = 1.2
RATE_PROJ_NORM = 40.0
RATE_PRED_UP = 18.0
RATE_PRED_DOWN = 0.9
RATE_PRED_NORM = 30.0


def across(matrix, weight):
    return lax.dot_general(
        matrix, weight, (((1,), (1,)), ((), ())), preferred_element_type=jnp.float32
    )


def outer_sum(first_op, second_op):
    return lax.dot_general(
        first_op, second_op, (((0,), (0,)), ((), ())), preferred_element_type=jnp.float32
    )


def standard(hidden, col_sum, col_square, total_views):
    middle_mean = col_sum / total_views
    inverse = lax.rsqrt(col_square / total_views - middle_mean * middle_mean + NORM_EPS)
    return ((hidden - middle_mean) * inverse, inverse)


def norm_back(grad_out, scaled, inverse, params, sum_grad, sum_cross, total_views):
    return (
        params[0]
        * inverse
        * (grad_out - sum_grad / total_views - scaled * (sum_cross / total_views))
    )


def unit_rows(values):
    return values * lax.rsqrt(jnp.sum(values * values, 1, keepdims=True) + UNIT_EPS)


def partner(values):
    width = values.shape[1]
    return values.reshape(-1, 2, width)[:, ::-1, :].reshape(-1, width)


def nesterov(weight, moment, grad, rate):
    fresh = 0.5 * moment + grad
    return (fresh, weight - rate * (grad + 0.5 * fresh))


def finish(
    total_views,
    args,
    loss,
    input_grad,
    shard_proj_up,
    shard_proj_down,
    grad_proj_norm,
    shard_pred_up,
    shard_pred_down,
    grad_pred_norm,
):
    (proj_up, proj_down, proj_norm, pred_up, pred_down, pred_norm) = args[2:8]
    (
        moment_proj_up,
        moment_proj_down,
        moment_proj_norm,
        moment_pred_up,
        moment_pred_down,
        moment_pred_norm,
        target_up,
        target_down,
        target_norm,
    ) = args[8:]
    scale = math.sqrt(total_views)
    mom_pu, next_pu = nesterov(proj_up, moment_proj_up, shard_proj_up, RATE_PROJ_UP * scale)
    mom_pd, next_pd = nesterov(proj_down, moment_proj_down, shard_proj_down, RATE_PROJ_DOWN * scale)
    mom_pn, next_pn = nesterov(proj_norm, moment_proj_norm, grad_proj_norm, RATE_PROJ_NORM * scale)
    mom_qu, next_qu = nesterov(pred_up, moment_pred_up, shard_pred_up, RATE_PRED_UP * scale)
    mom_qd, next_qd = nesterov(pred_down, moment_pred_down, shard_pred_down, RATE_PRED_DOWN * scale)
    mom_qn, next_qn = nesterov(pred_norm, moment_pred_norm, grad_pred_norm, RATE_PRED_NORM * scale)
    target_up_next = 0.5 * target_up + 0.5 * next_pu
    target_down_next = 0.5 * target_down + 0.5 * next_pd
    target_norm_next = 0.5 * target_norm + 0.5 * next_pn
    return (
        loss,
        input_grad,
        shard_proj_up,
        mom_pu,
        next_pu,
        shard_proj_down,
        mom_pd,
        next_pd,
        grad_proj_norm,
        mom_pn,
        next_pn,
        shard_pred_up,
        mom_qu,
        next_qu,
        shard_pred_down,
        mom_qd,
        next_qd,
        grad_pred_norm,
        mom_qn,
        next_qn,
        target_up_next,
        target_down_next,
        target_norm_next,
    )


def plain_body(
    features,
    keep_mask,
    proj_up,
    proj_down,
    proj_norm,
    pred_up,
    pred_down,
    pred_norm,
    moment_proj_up,
    moment_proj_down,
    moment_proj_norm,
    moment_pred_up,
    moment_pred_down,
    moment_pred_norm,
    target_up,
    target_down,
    target_norm,
):
    total_views = float(features.shape[0] * lax.axis_size("dp"))
    width = proj_up.shape[1]

    def gathered(parts):
        low = jnp.stack([part.astype(jnp.bfloat16) for part in parts])
        full = lax.all_gather(low, "dp", axis=1, tiled=True)
        return tuple(full[i] for i in range(len(parts)))

    (up_full, tup_full) = gathered((proj_up, target_up))
    (down_full, pup_full, pdown_full, tdown_full) = gathered(
        (proj_down, pred_up, pred_down, target_down)
    )
    keep_float = keep_mask.astype(jnp.float32)
    hidden1 = jnp.dot(features, up_full, preferred_element_type=jnp.float32)
    target_hidden = jnp.dot(features, tup_full, preferred_element_type=jnp.float32)
    sums = lax.psum(
        jnp.stack(
            [
                jnp.sum(hidden1, 0),
                jnp.sum(hidden1 * hidden1, 0),
                jnp.sum(target_hidden, 0),
                jnp.sum(target_hidden * target_hidden, 0),
                jnp.full((width,), jnp.sum(keep_float)),
            ]
        ),
        "dp",
    )
    sum_one, square_one, sum_target, square_target = sums[0], sums[1], sums[2], sums[3]
    count = sums[4, 0]
    scaled1, inverse1 = standard(hidden1, sum_one, square_one, total_views)
    action1, gelu_back1 = jax.vjp(jax.nn.gelu, scaled1 * proj_norm[0] + proj_norm[1])
    action1 = action1.astype(jnp.bfloat16)
    target_scaled, target_inverse = standard(target_hidden, sum_target, square_target, total_views)
    target_action = jax.nn.gelu(target_scaled * target_norm[0] + target_norm[1]).astype(
        jnp.bfloat16
    )
    middle, target_out = (
        lax.psum(across(action1, down_full).astype(jnp.bfloat16), "tensor").astype(jnp.float32),
        lax.psum(across(target_action, tdown_full).astype(jnp.bfloat16), "tensor").astype(
            jnp.float32
        ),
    )
    middle_low = middle.astype(jnp.bfloat16)
    hidden2 = jnp.dot(middle_low, pup_full, preferred_element_type=jnp.float32)
    sum_two, square_two = lax.psum(
        jnp.stack([jnp.sum(hidden2, 0), jnp.sum(hidden2 * hidden2, 0)]), "dp"
    )
    scaled2, inverse2 = standard(hidden2, sum_two, square_two, total_views)
    action2, gelu_back2 = jax.vjp(jax.nn.gelu, scaled2 * pred_norm[0] + pred_norm[1])
    action2 = action2.astype(jnp.bfloat16)
    query = lax.psum(across(action2, pdown_full).astype(jnp.bfloat16), "tensor").astype(jnp.float32)
    goal = partner(unit_rows(target_out))

    def loss_terms(values):
        return jnp.sum(keep_float * (2.0 - 2.0 * jnp.sum(unit_rows(values) * goal, 1)))

    local_loss, loss_back = jax.vjp(loss_terms, query)
    (grad_query,) = loss_back(1.0 / count)
    grad_query = grad_query.astype(jnp.bfloat16)
    grad_pred_down = outer_sum(grad_query, action2)
    (grad_norm2,) = gelu_back2(jnp.dot(grad_query, pdown_full, preferred_element_type=jnp.float32))
    back_sum2, back_cross2, loss_row = lax.psum(
        jnp.stack(
            [
                jnp.sum(grad_norm2, 0),
                jnp.sum(grad_norm2 * scaled2, 0),
                jnp.full((width,), local_loss),
            ]
        ),
        "dp",
    )
    loss_total = loss_row[0]
    grad_hidden2 = norm_back(
        grad_norm2, scaled2, inverse2, pred_norm, back_sum2, back_cross2, total_views
    ).astype(jnp.bfloat16)
    grad_pred_norm = jnp.stack([back_cross2, back_sum2])
    grad_pred_up = outer_sum(middle_low, grad_hidden2)
    grad_middle = lax.psum(across(grad_hidden2, pup_full).astype(jnp.bfloat16), "tensor")
    grad_proj_down = outer_sum(grad_middle, action1)
    (grad_norm1,) = gelu_back1(jnp.dot(grad_middle, down_full, preferred_element_type=jnp.float32))
    back_sum1, back_cross1 = lax.psum(
        jnp.stack([jnp.sum(grad_norm1, 0), jnp.sum(grad_norm1 * scaled1, 0)]), "dp"
    )
    grad_hidden1 = norm_back(
        grad_norm1, scaled1, inverse1, proj_norm, back_sum1, back_cross1, total_views
    ).astype(jnp.bfloat16)
    grad_proj_norm = jnp.stack([back_cross1, back_sum1])
    grad_proj_up = outer_sum(features, grad_hidden1)
    input_grad = lax.psum_scatter(
        across(grad_hidden1, up_full).astype(jnp.bfloat16),
        "tensor",
        scatter_dimension=1,
        tiled=True,
    ).astype(jnp.float32)
    shard_proj_up = lax.psum_scatter(
        grad_proj_up.astype(jnp.bfloat16), "dp", scatter_dimension=0, tiled=True
    ).astype(jnp.float32)
    small = lax.psum_scatter(
        jnp.stack([grad_proj_down, grad_pred_up, grad_pred_down]).astype(jnp.bfloat16),
        "dp",
        scatter_dimension=1,
        tiled=True,
    ).astype(jnp.float32)
    shard_proj_down, shard_pred_up, shard_pred_down = small[0], small[1], small[2]
    loss = loss_total / count
    return finish(
        total_views,
        (
            features,
            keep_mask,
            proj_up,
            proj_down,
            proj_norm,
            pred_up,
            pred_down,
            pred_norm,
            moment_proj_up,
            moment_proj_down,
            moment_proj_norm,
            moment_pred_up,
            moment_pred_down,
            moment_pred_norm,
            target_up,
            target_down,
            target_norm,
        ),
        loss,
        input_grad,
        shard_proj_up,
        shard_proj_down,
        grad_proj_norm,
        shard_pred_up,
        shard_pred_down,
        grad_pred_norm,
    )


MESH = pl.DeviceIdType.MESH
GRIDS = {16: (4, 2, 2)}
TILE = 256
GELU_A = math.sqrt(2.0 / math.pi)
GELU_B = 0.044715
ALONG_LAST = (0, ((0, 2, 1), (0, 1, 2)))
ACROSS_FIRST = (1, ((2, 1, 0), (1, 2, 0)))
Z_AHEAD = 2
VMEM_LIMIT = 63 * 1024 * 1024


def loop(count, step):
    def one(i, carry):
        step(i)
        return carry

    lax.fori_loop(0, count, one, 0)


def nt_dot(first_op, second_op):
    return lax.dot_general(
        first_op, second_op, (((1,), (1,)), ((), ())), preferred_element_type=jnp.float32
    )


def tn_dot(first_op, second_op):
    return lax.dot_general(
        first_op, second_op, (((0,), (0,)), ((), ())), preferred_element_type=jnp.float32
    )


def gelu_tanh(value):
    return jnp.tanh(GELU_A * (value + GELU_B * value * value * value))


def step_kernel(
    grid,
    total_views,
    x_hbm,
    pu_hbm,
    tu_hbm,
    pd_hbm,
    qu_hbm,
    qd_hbm,
    td_hbm,
    proj_norm,
    pred_norm,
    target_norm,
    keep,
    ig_hbm,
    gu_out,
    gs_out,
    proj_stat,
    pred_stat,
    loss_out,
    feats,
    up,
    tup,
    small,
    act1,
    hat1,
    act2,
    hat2,
    wide,
    tact,
    acc,
    ex,
    exr,
    sr1,
    sr2,
    sr3,
    inv1,
    inv2,
    pa,
    pb,
    qa,
    qb,
    load_sem,
    ag_s,
    ag_r,
    ps_s,
    ps_r,
    qs_s,
    qs_r,
    ex_s,
    ex_r,
    rs_s,
    rs_r,
    ss_s,
    ss_r,
    ig_s,
    ig_r,
    ready,
):
    n0, n1, n2 = grid
    plane = n1 * n2
    views, width = wide.shape
    rows = up.shape[3]
    small_rows = small.shape[4]
    blocks = views // rows
    chunk = width // 4
    half = width // 2
    dp = lax.axis_index("dp")
    core = lax.axis_index("tensor")
    me = (dp // plane, (dp // n2) % n1, dp % n2)
    mp = dp % plane
    other = (dp, 1 - core)

    def place(index):
        return ((index[0] * n1 + index[1]) * n2 + index[2], core)

    def moved(axis, k):
        target = list(me)
        target[axis] = (me[axis] + k) % grid[axis]
        return tuple(target)

    barrier = pltpu.get_barrier_semaphore()
    greet = [place(moved(0, k)) for k in range(1, n0)]
    greet += [(me[0] * plane + (mp + k) % plane, core) for k in range(1, plane)]
    greet.append(other)
    for device in greet:
        pl.semaphore_signal(barrier, inc=1, device_id=device, device_id_type=MESH)

    loads = [
        pltpu.make_async_copy(src, wide.at[pl.ds(start, src.shape[0])], load_sem.at[i])
        for i, (src, start) in enumerate(
            (
                (pd_hbm, 2 * rows),
                (qu_hbm, 2 * rows + small_rows),
                (qd_hbm, 2 * rows + 2 * small_rows),
                (td_hbm, 2 * rows + 3 * small_rows),
                (pu_hbm, 0),
                (tu_hbm, rows),
            )
        )
    ]
    loads.append(pltpu.make_async_copy(x_hbm, feats, load_sem.at[6]))
    for load in loads:
        load.start()
    for load in loads[:4]:
        load.wait()
    for w in range(4):
        small[w, me[0], me[1], me[2]] = wide[
            pl.ds(2 * rows + w * small_rows, small_rows), :
        ].astype(jnp.bfloat16)
    loads[4].wait()
    up[me[0], me[1], me[2]] = wide[pl.ds(0, rows), :].astype(jnp.bfloat16)
    loads[5].wait()
    tup[me[0], me[1], me[2]] = wide[pl.ds(rows, rows), :].astype(jnp.bfloat16)
    pl.semaphore_wait(barrier, len(greet))

    base = (0, n0 - 1, n0 - 1 + n1 - 1)
    chunks = [("small", 0, ALONG_LAST)]
    chunks += [("up", i, ALONG_LAST) for i in range(4)]
    chunks += [("small", 1, ACROSS_FIRST)]
    chunks += [("target", i, ALONG_LAST) for i in range(4)]

    def gather_copies(c, lane, phase):
        kind, index, (_, orders) = chunks[c]
        order = orders[lane]
        axis = order[phase]
        sel = [slice(None) if b in order[:phase] else me[b] for b in range(3)]
        if kind == "small":
            ref = small.at[
                pl.ds(2 * index, 2), sel[0], sel[1], sel[2], :, pl.ds(lane * half, half)
            ]
        else:
            buffer = up if kind == "up" else tup
            ref = buffer.at[
                sel[0], sel[1], sel[2], :, pl.ds(index * chunk + lane * TILE, TILE)
            ]
        return [
            pltpu.make_async_remote_copy(
                src_ref=ref,
                dst_ref=ref,
                send_sem=ag_s.at[c, lane, base[axis] + k - 1],
                recv_sem=ag_r.at[c, lane, base[axis] + k - 1],
                device_id=place(moved(axis, k)),
                device_id_type=MESH,
            )
            for k in range(1, grid[axis])
        ]

    def gather_start(c, phase):
        for lane in range(2):
            if phase:
                for copy in gather_copies(c, lane, phase - 1):
                    copy.wait_recv()
            for copy in gather_copies(c, lane, phase):
                copy.start()

    def gather_end(c):
        for lane in range(2):
            for copy in gather_copies(c, lane, 2):
                copy.wait_recv()

    def sum_copies(buffers, i, stage):
        first, second, send, recv = buffers
        if stage == 0:
            ref = first.at[i, mp]
            return [
                pltpu.make_async_remote_copy(
                    src_ref=ref,
                    dst_ref=ref,
                    send_sem=send.at[i, k - 1],
                    recv_sem=recv.at[i, k - 1],
                    device_id=(me[0] * plane + (mp + k) % plane, core),
                    device_id_type=MESH,
                )
                for k in range(1, plane)
            ]
        ref = second.at[i, me[0]]
        return [
            pltpu.make_async_remote_copy(
                src_ref=ref,
                dst_ref=ref,
                send_sem=send.at[i, plane - 1 + k - 1],
                recv_sem=recv.at[i, plane - 1 + k - 1],
                device_id=place(moved(0, k)),
                device_id_type=MESH,
            )
            for k in range(1, n0)
        ]

    narrow_sum = (pa, pb, ps_s, ps_r)
    whole_sum = (qa, qb, qs_s, qs_r)

    def sum_start(buffers, i):
        for copy in sum_copies(buffers, i, 0):
            copy.start()

    def sum_middle(buffers, i):
        for copy in sum_copies(buffers, i, 0):
            copy.wait()
        first, second = buffers[:2]
        total = first[i, 0]
        for j in range(1, plane):
            total = total + first[i, j]
        second[i, me[0]] = total
        for copy in sum_copies(buffers, i, 1):
            copy.start()

    def sum_end(buffers, i):
        for copy in sum_copies(buffers, i, 1):
            copy.wait()
        second = buffers[1]
        total = second[i, 0]
        for j in range(1, n0):
            total = total + second[i, j]
        return total

    def swap(i):
        return pltpu.make_async_remote_copy(
            src_ref=ex.at[i],
            dst_ref=exr.at[i],
            send_sem=ex_s.at[i],
            recv_sem=ex_r.at[i],
            device_id=other,
            device_id_type=MESH,
        )

    def swap_end(i):
        swap(i).wait()

        def add(b):
            part = pl.ds(pl.multiple_of(b * rows, rows), rows)
            ex[i, part, :] = (
                ex[i, part, :].astype(jnp.float32) + exr[i, part, :].astype(jnp.float32)
            ).astype(jnp.bfloat16)

        loop(blocks, add)

    def weight(w, columns):
        return small[w, :, :, :, :, columns].reshape(plane * n0 * small_rows, columns.size)

    def columns_at(start, size):
        return pl.ds(pl.multiple_of(start, TILE), size)

    def hidden_chunk(weights, i, slot):
        def one(lane):
            columns = columns_at(i * chunk + lane * TILE, TILE)
            matrix = weights[:, :, :, :, columns].reshape(n0 * plane * rows, TILE)
            values = jnp.dot(feats[...], matrix, preferred_element_type=jnp.float32)
            wide[:, columns] = values
            spot = columns_at(lane * TILE, TILE)
            pa[slot, mp, 0:1, spot] = jnp.sum(values, 0, keepdims=True)
            pa[slot, mp, 1:2, spot] = jnp.sum(values * values, 0, keepdims=True)

        loop(2, one)
        pa[slot, mp, 2:4, :] = jnp.broadcast_to(jnp.sum(keep[...], 0, keepdims=True), (2, chunk))

    def spread(total):
        mean = total[0:1] / total_views
        return mean, lax.rsqrt(total[1:2] / total_views - mean * mean + NORM_EPS)

    def act_tiles(start, count, mean, inverse, norm, act_ref, hat_ref, act_start):
        for n in range(count):
            columns = pl.ds(start + n * TILE, TILE)
            targets = pl.ds(act_start + n * TILE, TILE)
            here = slice(n * TILE, (n + 1) * TILE)
            mean_n, inverse_n = mean[:, here], inverse[:, here]
            gain, shift = norm[0:1, columns], norm[1:2, columns]

            def one(b):
                part = pl.ds(pl.multiple_of(b * rows, rows), rows)
                hat = (wide[part, columns] - mean_n) * inverse_n
                value = hat * gain + shift
                action = 0.5 * value * (1.0 + gelu_tanh(value))
                act_ref[b // 2, b % 2, :, targets] = action.astype(jnp.bfloat16)
                if hat_ref is not None:
                    hat_ref[b // 2, b % 2, :, targets] = hat.astype(jnp.bfloat16)

            loop(blocks, one)

    def act_chunk(slot, i, norm, act_ref, hat_ref, inv_ref, w, act_start):
        total = sum_end(narrow_sum, slot)
        mean, inverse = spread(total)
        if inv_ref is not None:
            inv_ref[:, pl.ds(i * chunk, chunk)] = inverse
        act_tiles(i * chunk, chunk // TILE, mean, inverse, norm, act_ref, hat_ref, act_start)
        action = act_ref[:, :, :, pl.ds(act_start, chunk)].reshape(views, chunk)
        product = nt_dot(action, weight(w, pl.ds(i * chunk, chunk)))
        if i == 0:
            acc[...] = product
        else:
            acc[...] += product
        return total

    count = [None]

    def online_middle():
        ex[0] = acc[...].astype(jnp.bfloat16)
        swap(0).start()
        swap_end(0)

        def one(n):
            columns = columns_at(n * TILE, TILE)
            values = jnp.dot(ex[0], weight(1, columns), preferred_element_type=jnp.float32)
            wide[:, columns] = values
            qa[0, mp, 0:1, columns] = jnp.sum(values, 0, keepdims=True)
            qa[0, mp, 1:2, columns] = jnp.sum(values * values, 0, keepdims=True)

        loop(width // TILE, one)
        qa[0, mp, 2:4, :] = jnp.zeros((2, width), jnp.float32)
        sum_start(whole_sum, 0)

    def online_query():
        total = sum_end(whole_sum, 0)
        mean, inverse = spread(total)
        inv2[...] = inverse
        act_tiles(0, width // TILE, mean, inverse, pred_norm, act2, hat2, 0)
        ex[1] = nt_dot(
            act2[...].reshape(views, width), weight(2, pl.ds(0, width))
        ).astype(jnp.bfloat16)
        swap(1).start()

    def compute(c):
        if c == 1:
            loads[6].wait()
        if 1 <= c <= 4:
            i = c - 1
            if i:
                sum_middle(narrow_sum, i - 1)
            hidden_chunk(up, i, i)
            sum_start(narrow_sum, i)
            if i:
                total = act_chunk(i - 1, i - 1, proj_norm, act1, hat1, inv1, 0, (i - 1) * chunk)
                if i == 1:
                    count[0] = total[2:3, 0:1]
        if c == 5:
            sum_middle(narrow_sum, 3)
            act_chunk(3, 3, proj_norm, act1, hat1, inv1, 0, 3 * chunk)
            online_middle()
        if c == 6:
            sum_middle(whole_sum, 0)
            online_query()
        if 6 <= c <= 9:
            i = c - 6
            if i:
                sum_middle(narrow_sum, 4 + i - 1)
            hidden_chunk(tup, i, 4 + i)
            sum_start(narrow_sum, 4 + i)
            if i:
                act_chunk(4 + i - 1, i - 1, target_norm, tact, None, None, 3, 0)
            if c == 6:
                swap_end(1)

    total_chunks = len(chunks)
    for c in range(Z_AHEAD):
        gather_start(c, 0)
    for tick in range(total_chunks + 2):
        if tick < total_chunks:
            gather_start(tick, 1)
        if tick + Z_AHEAD < total_chunks:
            gather_start(tick + Z_AHEAD, 0)
        if 1 <= tick <= total_chunks:
            gather_start(tick - 1, 2)
        if tick >= 2:
            gather_end(tick - 2)
            compute(tick - 2)
    for c in range(total_chunks):
        for lane in range(2):
            for phase in range(3):
                for copy in gather_copies(c, lane, phase):
                    copy.wait_send()
    sum_middle(narrow_sum, 7)
    act_chunk(7, 3, target_norm, tact, None, None, 3, 0)
    ex[2] = acc[...].astype(jnp.bfloat16)
    swap(2).start()
    swap(2).wait()

    scale = -2.0 / count[0]

    def unit_scale(values):
        return lax.rsqrt(jnp.sum(values * values, 1, keepdims=True) + UNIT_EPS)

    even = (lax.broadcasted_iota(jnp.int32, (rows, acc.shape[1]), 0) % 2) == 0

    def loss_tile(b, carry):
        part = pl.ds(pl.multiple_of(b * rows, rows), rows)
        query = ex[1, part, :].astype(jnp.float32)
        target = ex[2, part, :].astype(jnp.float32) + exr[2, part, :].astype(jnp.float32)
        target = target * unit_scale(target)
        goal = jnp.where(even, pltpu.roll(target, rows - 1, 0), pltpu.roll(target, 1, 0))
        back = unit_scale(query)
        unit = query * back
        cosine = jnp.sum(unit * goal, 1, keepdims=True)
        kept = keep[part, :]
        ex[1, part, :] = ((scale * kept * back) * (goal - cosine * unit)).astype(jnp.bfloat16)
        return carry + kept * (2.0 - 2.0 * cosine)

    loss_rows = lax.fori_loop(0, blocks, loss_tile, jnp.zeros((rows, 1), jnp.float32))
    local_loss = jnp.sum(loss_rows, 0, keepdims=True)

    def back_norm(i, w, grads, hat_ref, norm, extra):
        def one(n):
            columns = columns_at(n * TILE, TILE)
            wide[:, columns] = jnp.dot(
                ex[grads], weight(w, columns), preferred_element_type=jnp.float32
            )
            gain, shift = norm[0:1, columns], norm[1:2, columns]

            def tile(b, carry):
                part = pl.ds(pl.multiple_of(b * rows, rows), rows)
                hat = hat_ref[b // 2, b % 2, :, columns].astype(jnp.float32)
                value = hat * gain + shift
                bent = gelu_tanh(value)
                slope = 0.5 * (1.0 + bent) + (0.5 * GELU_A) * value * (1.0 - bent * bent) * (
                    1.0 + (3.0 * GELU_B) * value * value
                )
                grad = wide[part, columns] * slope
                wide[part, columns] = grad
                cross = grad * hat
                return (
                    carry[0] + jnp.sum(grad.reshape(rows // 8, 8, TILE), 0),
                    carry[1] + jnp.sum(cross.reshape(rows // 8, 8, TILE), 0),
                )

            zero = jnp.zeros((8, TILE), jnp.float32)
            sums = lax.fori_loop(0, blocks, tile, (zero, zero))
            qa[i, mp, 0:1, columns] = jnp.sum(sums[0], 0, keepdims=True)
            qa[i, mp, 1:2, columns] = jnp.sum(sums[1], 0, keepdims=True)

        loop(width // TILE, one)
        qa[i, mp, 2:4, :] = jnp.broadcast_to(extra, (2, width))
        sum_start(whole_sum, i)

    def grad_hidden(stat, hat_ref, norm, inv_ref, columns):
        gain = norm[0:1, columns] * inv_ref[:, columns]
        shift = stat[0:1, columns] / total_views
        slope = stat[1:2, columns] / total_views

        def tile(b):
            part = pl.ds(pl.multiple_of(b * rows, rows), rows)
            hat = hat_ref[b // 2, b % 2, :, columns].astype(jnp.float32)
            hat_ref[b // 2, b % 2, :, columns] = (
                gain * (wide[part, columns] - shift - hat * slope)
            ).astype(jnp.bfloat16)

        loop(blocks, tile)

    def small_grad(w, grads, act_ref):
        def one(n):
            columns = columns_at(n * TILE, TILE)
            right = act_ref[:, :, :, columns].reshape(views, TILE)
            value = tn_dot(ex[grads], right).astype(jnp.bfloat16)
            small[w, :, :, :, :, columns] = value.reshape(n0, n1, n2, small_rows, TILE)

        loop(width // TILE, one)

    def reduce_copies(kind, g, lane, phase):
        axis, second = ((1, 2), (2, 1))[lane]
        if kind == "up":
            columns = pl.ds(g * chunk + lane * TILE, TILE)
            send, recv = rs_s, rs_r
            source = lambda sel: tup.at[sel[0], sel[1], sel[2], :, columns]
            lands = (
                act2.at[:, :, :, columns],
                hat2.at[:, 0, :, columns],
                hat2.at[me[0], 1, :, columns],
            )
        else:
            columns = pl.ds(lane * half, half)
            send, recv = ss_s, ss_r
            source = lambda sel: small.at[3 - g, sel[0], sel[1], sel[2], :, columns]
            lands = (
                sr1.at[g, :, :, :, columns],
                sr2.at[g, :, :, columns],
                sr3.at[g, me[0], :, columns],
            )
        copies = []
        moves = range(1, n0) if phase == 2 else (1,)
        for k in moves:
            axis_now = (axis, second, 0)[phase]
            target = moved(axis_now, k)
            sel = [slice(None)] * 3
            if phase > 0:
                sel[axis] = me[axis]
            if phase > 1:
                sel[second] = me[second]
            sel[axis_now] = target[axis_now]
            copies.append(
                pltpu.make_async_remote_copy(
                    src_ref=source(sel),
                    dst_ref=lands[phase],
                    send_sem=send.at[g, lane, phase + k - 1],
                    recv_sem=recv.at[g, lane, phase + k - 1],
                    device_id=place(target),
                    device_id_type=MESH,
                )
            )
        return copies

    def reduce_step(kind, g, phase):
        for lane in range(2):
            if phase:
                for copy in reduce_copies(kind, g, lane, phase - 1):
                    copy.wait()
                reduce_add(kind, g, lane, phase)
            if phase < 3:
                for copy in reduce_copies(kind, g, lane, phase):
                    copy.start()

    def plus(first_op, second_op):
        return (first_op.astype(jnp.float32) + second_op.astype(jnp.float32)).astype(jnp.bfloat16)

    def reduce_add(kind, g, lane, phase):
        big = kind == "up"
        if big:
            columns = pl.ds(g * chunk + lane * TILE, TILE)
        else:
            columns = pl.ds(lane * half, half)
        if phase == 1:

            def add(j):
                z, i = j // 2, j % 2
                y, x = (me[1], i) if lane == 0 else (i, me[2])
                if big:
                    tup[z, y, x, :, columns] = plus(
                        tup[z, y, x, :, columns], act2[z, i, :, columns]
                    )
                else:
                    small[3 - g, z, y, x, :, columns] = plus(
                        small[3 - g, z, y, x, :, columns], sr1[g, z, i, :, columns]
                    )

            loop(n0 * 2, add)
        elif phase == 2:

            def add(z):
                if big:
                    tup[z, me[1], me[2], :, columns] = plus(
                        tup[z, me[1], me[2], :, columns], hat2[z, 0, :, columns]
                    )
                else:
                    small[3 - g, z, me[1], me[2], :, columns] = plus(
                        small[3 - g, z, me[1], me[2], :, columns], sr2[g, z, :, columns]
                    )

            loop(n0, add)
        else:
            if big:
                total = tup[me[0], me[1], me[2], :, columns].astype(jnp.float32)
                for k in range(1, n0):
                    total = total + hat2[(me[0] + k) % n0, 1, :, columns].astype(jnp.float32)
                gu_out[:, columns] = total
            else:
                total = small[3 - g, me[0], me[1], me[2], :, columns].astype(jnp.float32)
                for k in range(1, n0):
                    total = total + sr3[g, (me[0] + k) % n0, :, columns].astype(jnp.float32)
                gs_out[g, :, columns] = total

    back_norm(1, 2, 1, hat2, pred_norm, local_loss)
    small_grad(3, 1, act2)
    reduce_step("small", 0, 0)
    sum_middle(whole_sum, 1)
    pred_stat[...] = sum_end(whole_sum, 1)
    loss_out[...] = jnp.broadcast_to(pred_stat[2:3, 0:1] / count[0], loss_out.shape)
    loop(
        width // TILE,
        lambda n: grad_hidden(pred_stat, hat2, pred_norm, inv2, columns_at(n * TILE, TILE)),
    )
    ex[3] = nt_dot(hat2[...].reshape(views, width), weight(1, pl.ds(0, width))).astype(jnp.bfloat16)
    swap(3).start()
    small_grad(2, 0, hat2)
    reduce_step("small", 1, 0)
    reduce_step("small", 0, 1)
    swap_end(3)
    back_norm(2, 0, 3, hat1, proj_norm, jnp.zeros((1, 1), jnp.float32))
    small_grad(1, 3, act1)
    pl.semaphore_signal(ready, inc=1, device_id=other, device_id_type=MESH)
    reduce_step("small", 2, 0)
    reduce_step("small", 1, 1)
    reduce_step("small", 0, 2)
    sum_middle(whole_sum, 2)
    proj_stat[...] = sum_end(whole_sum, 2)

    def up_grad(g):
        for n in range(2):
            grad_hidden(proj_stat, hat1, proj_norm, inv1, pl.ds(g * chunk + n * TILE, TILE))
        columns = pl.ds(g * chunk, chunk)

        def one(z):
            left = feats[:, columns_at(z * plane * rows, plane * rows)]
            value = tn_dot(left, hat1[:, :, :, columns].reshape(views, chunk))
            tup[z, :, :, :, columns] = value.astype(jnp.bfloat16).reshape(n1, n2, rows, chunk)

        loop(n0, one)
        reduce_step("up", g, 0)

    parts = ig_s.shape[0]

    def input_copy(q):
        return pltpu.make_async_remote_copy(
            src_ref=act1.at[:, :, :, pl.ds(q * TILE, TILE)],
            dst_ref=act1.at[:, :, :, pl.ds((parts + q) * TILE, TILE)],
            send_sem=ig_s.at[q],
            recv_sem=ig_r.at[q],
            device_id=other,
            device_id_type=MESH,
        )

    def input_product(q, side):
        first = side * (n0 // 2) + q // n1
        matrix = up[first, q % n1].reshape(n2 * rows, width)
        return nt_dot(hat1[...].reshape(views, width), matrix)

    for g in range(4):
        up_grad(g)
        if g == 0:
            reduce_step("small", 2, 1)
            reduce_step("small", 1, 2)
        else:
            reduce_step("up", g - 1, 1)
        if g == 1:
            reduce_step("small", 0, 3)
            reduce_step("small", 2, 2)
        if g >= 2:
            reduce_step("up", g - 2, 2)
    pl.semaphore_wait(ready, 1)

    def send_part(q):
        act1[:, :, :, pl.ds(q * TILE, TILE)] = (
            input_product(q, 1 - core).astype(jnp.bfloat16).reshape(n0, 2, rows, TILE)
        )
        input_copy(q).start()

    def own_part(q):
        wide[:, pl.ds(q * TILE, TILE)] = input_product(q, core)

    for q in range(2):
        send_part(q)
    reduce_step("up", 3, 1)
    reduce_step("up", 2, 2)
    for q in range(2, parts):
        send_part(q)
    for q in range(parts):
        own_part(q)
    reduce_step("up", 3, 2)
    out_copies = []
    for q in range(parts):
        input_copy(q).wait()

        def add(b, q=q):
            part = pl.ds(pl.multiple_of(b * rows, rows), rows)
            wide[part, pl.ds(q * TILE, TILE)] += act1[
                b // 2, b % 2, :, pl.ds((parts + q) * TILE, TILE)
            ].astype(jnp.float32)

        loop(blocks, add)
    out_copy = pltpu.make_async_copy(
        wide.at[:, pl.ds(0, parts * TILE)], ig_hbm, load_sem.at[0]
    )
    out_copy.start()
    for g in (1, 2):
        reduce_step("small", g, 3)
    for g in range(4):
        reduce_step("up", g, 3)
    out_copy.wait()


def kernel_step(grid, total_views, features, keep, ups, downs, norms):
    n0, n1, n2 = grid
    plane = n1 * n2
    views, depth = features.shape
    rows, width = ups[0].shape
    small_rows = downs[0].shape[0]
    out = small_rows * n0 * plane
    parts = depth // 2 // TILE
    low, full = jnp.bfloat16, jnp.float32
    vm = pltpu.VMEM
    dma = pltpu.SemaphoreType.DMA
    anywhere = pl.BlockSpec(memory_space=pl.ANY)
    inside = pl.BlockSpec(memory_space=pltpu.VMEM)
    spread_shape = (n0, 2, rows, width)
    moves = n0 - 1 + n1 - 1 + n2 - 1
    sum_moves = plane - 1 + n0 - 1
    return pl.pallas_call(
        functools.partial(step_kernel, grid, total_views),
        out_shape=(
            jax.ShapeDtypeStruct((views, depth // 2), full),
            jax.ShapeDtypeStruct((rows, width), full),
            jax.ShapeDtypeStruct((3, small_rows, width), full),
            jax.ShapeDtypeStruct((4, width), full),
            jax.ShapeDtypeStruct((4, width), full),
            jax.ShapeDtypeStruct((8, 128), full),
        ),
        in_specs=[anywhere] * 7 + [inside] * 4,
        out_specs=(anywhere,) + (inside,) * 5,
        scratch_shapes=[
            vm((views, depth), low),
            vm((n0, n1, n2, rows, width), low),
            vm((n0, n1, n2, rows, width), low),
            vm((4, n0, n1, n2, small_rows, width), low),
            vm(spread_shape, low),
            vm(spread_shape, low),
            vm(spread_shape, low),
            vm(spread_shape, low),
            vm((views, width), full),
            vm((n0, 2, rows, width // 4), low),
            vm((views, out), full),
            vm((4, views, out), low),
            vm((4, views, out), low),
            vm((3, n0, 2, small_rows, width), low),
            vm((3, n0, small_rows, width), low),
            vm((3, n0, small_rows, width), low),
            vm((1, width), full),
            vm((1, width), full),
            vm((8, plane, 4, width // 4), full),
            vm((8, n0, 4, width // 4), full),
            vm((3, plane, 4, width), full),
            vm((3, n0, 4, width), full),
            dma((7,)),
            dma((10, 2, moves)),
            dma((10, 2, moves)),
            dma((8, sum_moves)),
            dma((8, sum_moves)),
            dma((3, sum_moves)),
            dma((3, sum_moves)),
            dma((4,)),
            dma((4,)),
            dma((4, 2, n0 + 1)),
            dma((4, 2, n0 + 1)),
            dma((3, 2, n0 + 1)),
            dma((3, 2, n0 + 1)),
            dma((parts,)),
            dma((parts,)),
            pltpu.SemaphoreType.REGULAR,
        ],
        compiler_params=pltpu.CompilerParams(
            collective_id=0, has_side_effects=True, vmem_limit_bytes=VMEM_LIMIT
        ),
    )(features, *ups, *downs, *norms, keep)


def step_body(grid, *args):
    (
        features,
        keep_mask,
        proj_up,
        proj_down,
        proj_norm,
        pred_up,
        pred_down,
        pred_norm,
        moment_proj_up,
        moment_proj_down,
        moment_proj_norm,
        moment_pred_up,
        moment_pred_down,
        moment_pred_norm,
        target_up,
        target_down,
        target_norm,
    ) = args
    if grid is None:
        return plain_body(*args)
    total_views = float(features.shape[0] * lax.axis_size("dp"))
    input_grad, shard_proj_up, shard_small, proj_stat, pred_stat, loss = kernel_step(
        grid,
        total_views,
        features,
        keep_mask.astype(jnp.float32).reshape(-1, 1),
        (proj_up, target_up),
        (proj_down, pred_up, pred_down, target_down),
        (proj_norm, pred_norm, target_norm),
    )
    shard_pred_down, shard_pred_up, shard_proj_down = shard_small[0], shard_small[1], shard_small[2]
    grad_proj_norm = proj_stat[1::-1]
    grad_pred_norm = pred_stat[1::-1]
    return finish(
        total_views,
        args,
        loss[0, 0],
        input_grad,
        shard_proj_up,
        shard_proj_down,
        grad_proj_norm,
        shard_pred_up,
        shard_pred_down,
        grad_pred_norm,
    )


def solution(mesh):
    placed = (
        P("dp", None),
        P("dp"),
        P("dp", "tensor"),
        P("dp", "tensor"),
        P(None, "tensor"),
        P("dp", "tensor"),
        P("dp", "tensor"),
        P(None, "tensor"),
        P("dp", "tensor"),
        P("dp", "tensor"),
        P(None, "tensor"),
        P("dp", "tensor"),
        P("dp", "tensor"),
        P(None, "tensor"),
        P("dp", "tensor"),
        P("dp", "tensor"),
        P(None, "tensor"),
    )
    return jax.shard_map(
        functools.partial(step_body, GRIDS.get(mesh.shape["dp"])),
        mesh=mesh,
        in_specs=placed,
        out_specs=(
            P(),
            P("dp", "tensor"),
            P("dp", "tensor"),
            P("dp", "tensor"),
            P("dp", "tensor"),
            P("dp", "tensor"),
            P("dp", "tensor"),
            P("dp", "tensor"),
            P(None, "tensor"),
            P(None, "tensor"),
            P(None, "tensor"),
            P("dp", "tensor"),
            P("dp", "tensor"),
            P("dp", "tensor"),
            P("dp", "tensor"),
            P("dp", "tensor"),
            P("dp", "tensor"),
            P(None, "tensor"),
            P(None, "tensor"),
            P(None, "tensor"),
            P("dp", "tensor"),
            P("dp", "tensor"),
            P(None, "tensor"),
        ),
        check_vma=False,
    )
```

```python
import functools
import math

import jax
import jax.numpy as jnp
from jax import lax
from jax.experimental import pallas as pl
from jax.experimental.pallas import tpu as pltpu
from jax.sharding import PartitionSpec as P

NORM_EPS = 1e-05
UNIT_EPS = 1e-06
RATE_PROJ_UP = 9.0
RATE_PROJ_DOWN = 1.2
RATE_PROJ_NORM = 40.0
RATE_PRED_UP = 18.0
RATE_PRED_DOWN = 0.9
RATE_PRED_NORM = 30.0


def across(matrix, weight):
    return lax.dot_general(
        matrix, weight, (((1,), (1,)), ((), ())), preferred_element_type=jnp.float32
    )


def outer_sum(first_op, second_op):
    return lax.dot_general(
        first_op, second_op, (((0,), (0,)), ((), ())), preferred_element_type=jnp.float32
    )


def standard(hidden, col_sum, col_square, total_views):
    middle_mean = col_sum / total_views
    inverse = lax.rsqrt(col_square / total_views - middle_mean * middle_mean + NORM_EPS)
    return ((hidden - middle_mean) * inverse, inverse)


def norm_back(grad_out, scaled, inverse, params, sum_grad, sum_cross, total_views):
    return (
        params[0]
        * inverse
        * (grad_out - sum_grad / total_views - scaled * (sum_cross / total_views))
    )


def unit_rows(values):
    return values * lax.rsqrt(jnp.sum(values * values, 1, keepdims=True) + UNIT_EPS)


def partner(values):
    width = values.shape[1]
    return values.reshape(-1, 2, width)[:, ::-1, :].reshape(-1, width)


def nesterov(weight, moment, grad, rate):
    fresh = 0.5 * moment + grad
    return (fresh, weight - rate * (grad + 0.5 * fresh))


def finish(
    total_views,
    args,
    loss,
    input_grad,
    shard_proj_up,
    shard_proj_down,
    grad_proj_norm,
    shard_pred_up,
    shard_pred_down,
    grad_pred_norm,
):
    (proj_up, proj_down, proj_norm, pred_up, pred_down, pred_norm) = args[2:8]
    (
        moment_proj_up,
        moment_proj_down,
        moment_proj_norm,
        moment_pred_up,
        moment_pred_down,
        moment_pred_norm,
        target_up,
        target_down,
        target_norm,
    ) = args[8:]
    scale = math.sqrt(total_views)
    mom_pu, next_pu = nesterov(proj_up, moment_proj_up, shard_proj_up, RATE_PROJ_UP * scale)
    mom_pd, next_pd = nesterov(proj_down, moment_proj_down, shard_proj_down, RATE_PROJ_DOWN * scale)
    mom_pn, next_pn = nesterov(proj_norm, moment_proj_norm, grad_proj_norm, RATE_PROJ_NORM * scale)
    mom_qu, next_qu = nesterov(pred_up, moment_pred_up, shard_pred_up, RATE_PRED_UP * scale)
    mom_qd, next_qd = nesterov(pred_down, moment_pred_down, shard_pred_down, RATE_PRED_DOWN * scale)
    mom_qn, next_qn = nesterov(pred_norm, moment_pred_norm, grad_pred_norm, RATE_PRED_NORM * scale)
    target_up_next = 0.5 * target_up + 0.5 * next_pu
    target_down_next = 0.5 * target_down + 0.5 * next_pd
    target_norm_next = 0.5 * target_norm + 0.5 * next_pn
    return (
        loss,
        input_grad,
        shard_proj_up,
        mom_pu,
        next_pu,
        shard_proj_down,
        mom_pd,
        next_pd,
        grad_proj_norm,
        mom_pn,
        next_pn,
        shard_pred_up,
        mom_qu,
        next_qu,
        shard_pred_down,
        mom_qd,
        next_qd,
        grad_pred_norm,
        mom_qn,
        next_qn,
        target_up_next,
        target_down_next,
        target_norm_next,
    )


def plain_body(
    features,
    keep_mask,
    proj_up,
    proj_down,
    proj_norm,
    pred_up,
    pred_down,
    pred_norm,
    moment_proj_up,
    moment_proj_down,
    moment_proj_norm,
    moment_pred_up,
    moment_pred_down,
    moment_pred_norm,
    target_up,
    target_down,
    target_norm,
):
    total_views = float(features.shape[0] * lax.axis_size("dp"))
    width = proj_up.shape[1]

    def gathered(parts):
        low = jnp.stack([part.astype(jnp.bfloat16) for part in parts])
        full = lax.all_gather(low, "dp", axis=1, tiled=True)
        return tuple(full[i] for i in range(len(parts)))

    (up_full, tup_full) = gathered((proj_up, target_up))
    (down_full, pup_full, pdown_full, tdown_full) = gathered(
        (proj_down, pred_up, pred_down, target_down)
    )
    keep_float = keep_mask.astype(jnp.float32)
    hidden1 = jnp.dot(features, up_full, preferred_element_type=jnp.float32)
    target_hidden = jnp.dot(features, tup_full, preferred_element_type=jnp.float32)
    sums = lax.psum(
        jnp.stack(
            [
                jnp.sum(hidden1, 0),
                jnp.sum(hidden1 * hidden1, 0),
                jnp.sum(target_hidden, 0),
                jnp.sum(target_hidden * target_hidden, 0),
                jnp.full((width,), jnp.sum(keep_float)),
            ]
        ),
        "dp",
    )
    sum_one, square_one, sum_target, square_target = sums[0], sums[1], sums[2], sums[3]
    count = sums[4, 0]
    scaled1, inverse1 = standard(hidden1, sum_one, square_one, total_views)
    action1, gelu_back1 = jax.vjp(jax.nn.gelu, scaled1 * proj_norm[0] + proj_norm[1])
    action1 = action1.astype(jnp.bfloat16)
    target_scaled, target_inverse = standard(target_hidden, sum_target, square_target, total_views)
    target_action = jax.nn.gelu(target_scaled * target_norm[0] + target_norm[1]).astype(
        jnp.bfloat16
    )
    middle, target_out = (
        lax.psum(across(action1, down_full).astype(jnp.bfloat16), "tensor").astype(jnp.float32),
        lax.psum(across(target_action, tdown_full).astype(jnp.bfloat16), "tensor").astype(
            jnp.float32
        ),
    )
    middle_low = middle.astype(jnp.bfloat16)
    hidden2 = jnp.dot(middle_low, pup_full, preferred_element_type=jnp.float32)
    sum_two, square_two = lax.psum(
        jnp.stack([jnp.sum(hidden2, 0), jnp.sum(hidden2 * hidden2, 0)]), "dp"
    )
    scaled2, inverse2 = standard(hidden2, sum_two, square_two, total_views)
    action2, gelu_back2 = jax.vjp(jax.nn.gelu, scaled2 * pred_norm[0] + pred_norm[1])
    action2 = action2.astype(jnp.bfloat16)
    query = lax.psum(across(action2, pdown_full).astype(jnp.bfloat16), "tensor").astype(jnp.float32)
    goal = partner(unit_rows(target_out))

    def loss_terms(values):
        return jnp.sum(keep_float * (2.0 - 2.0 * jnp.sum(unit_rows(values) * goal, 1)))

    local_loss, loss_back = jax.vjp(loss_terms, query)
    (grad_query,) = loss_back(1.0 / count)
    grad_query = grad_query.astype(jnp.bfloat16)
    grad_pred_down = outer_sum(grad_query, action2)
    (grad_norm2,) = gelu_back2(jnp.dot(grad_query, pdown_full, preferred_element_type=jnp.float32))
    back_sum2, back_cross2, loss_row = lax.psum(
        jnp.stack(
            [
                jnp.sum(grad_norm2, 0),
                jnp.sum(grad_norm2 * scaled2, 0),
                jnp.full((width,), local_loss),
            ]
        ),
        "dp",
    )
    loss_total = loss_row[0]
    grad_hidden2 = norm_back(
        grad_norm2, scaled2, inverse2, pred_norm, back_sum2, back_cross2, total_views
    ).astype(jnp.bfloat16)
    grad_pred_norm = jnp.stack([back_cross2, back_sum2])
    grad_pred_up = outer_sum(middle_low, grad_hidden2)
    grad_middle = lax.psum(across(grad_hidden2, pup_full).astype(jnp.bfloat16), "tensor")
    grad_proj_down = outer_sum(grad_middle, action1)
    (grad_norm1,) = gelu_back1(jnp.dot(grad_middle, down_full, preferred_element_type=jnp.float32))
    back_sum1, back_cross1 = lax.psum(
        jnp.stack([jnp.sum(grad_norm1, 0), jnp.sum(grad_norm1 * scaled1, 0)]), "dp"
    )
    grad_hidden1 = norm_back(
        grad_norm1, scaled1, inverse1, proj_norm, back_sum1, back_cross1, total_views
    ).astype(jnp.bfloat16)
    grad_proj_norm = jnp.stack([back_cross1, back_sum1])
    grad_proj_up = outer_sum(features, grad_hidden1)
    input_grad = lax.psum_scatter(
        across(grad_hidden1, up_full).astype(jnp.bfloat16),
        "tensor",
        scatter_dimension=1,
        tiled=True,
    ).astype(jnp.float32)
    shard_proj_up = lax.psum_scatter(
        grad_proj_up.astype(jnp.bfloat16), "dp", scatter_dimension=0, tiled=True
    ).astype(jnp.float32)
    small = lax.psum_scatter(
        jnp.stack([grad_proj_down, grad_pred_up, grad_pred_down]).astype(jnp.bfloat16),
        "dp",
        scatter_dimension=1,
        tiled=True,
    ).astype(jnp.float32)
    shard_proj_down, shard_pred_up, shard_pred_down = small[0], small[1], small[2]
    loss = loss_total / count
    return finish(
        total_views,
        (
            features,
            keep_mask,
            proj_up,
            proj_down,
            proj_norm,
            pred_up,
            pred_down,
            pred_norm,
            moment_proj_up,
            moment_proj_down,
            moment_proj_norm,
            moment_pred_up,
            moment_pred_down,
            moment_pred_norm,
            target_up,
            target_down,
            target_norm,
        ),
        loss,
        input_grad,
        shard_proj_up,
        shard_proj_down,
        grad_proj_norm,
        shard_pred_up,
        shard_pred_down,
        grad_pred_norm,
    )


MESH = pl.DeviceIdType.MESH
GRIDS = {16: (4, 2, 2)}
TILE = 256
GELU_A = math.sqrt(2.0 / math.pi)
GELU_B = 0.044715
LATE_PER_TICK = 2
VMEM_LIMIT = 63 * 1024 * 1024


def loop(count, step):
    def one(i, carry):
        step(i)
        return carry

    lax.fori_loop(0, count, one, 0)


def nt_dot(first_op, second_op):
    return lax.dot_general(
        first_op, second_op, (((1,), (1,)), ((), ())), preferred_element_type=jnp.float32
    )


def tn_dot(first_op, second_op):
    return lax.dot_general(
        first_op, second_op, (((0,), (0,)), ((), ())), preferred_element_type=jnp.float32
    )


def gelu_tanh(value):
    return jnp.tanh(GELU_A * (value + GELU_B * value * value * value))


def step_kernel(
    grid,
    total_views,
    x_hbm,
    pu_hbm,
    tu_hbm,
    pd_hbm,
    qu_hbm,
    qd_hbm,
    td_hbm,
    proj_norm,
    pred_norm,
    target_norm,
    keep,
    ig_hbm,
    gu_out,
    gs_out,
    proj_stat,
    pred_stat,
    loss_out,
    feats,
    up,
    tup,
    small,
    act1,
    hat1,
    act2,
    hat2,
    wide,
    tact,
    acc,
    ex,
    exr,
    sr1,
    sr2,
    sr3,
    inv1,
    inv2,
    means,
    pa,
    pb,
    qa,
    qb,
    ta,
    tb,
    load_sem,
    ag_s,
    ag_r,
    ps_s,
    ps_r,
    qs_s,
    qs_r,
    ts_s,
    ts_r,
    ex_s,
    ex_r,
    rs_s,
    rs_r,
    ss_s,
    ss_r,
    ig_s,
    ig_r,
    ready,
):
    n0, n1, n2 = grid
    plane = n1 * n2
    views, width = wide.shape
    rows = up.shape[3]
    small_rows = small.shape[4]
    blocks = views // rows
    chunk = width // 4
    half = width // 2
    dp = lax.axis_index("dp")
    core = lax.axis_index("tensor")
    me = (dp // plane, (dp // n2) % n1, dp % n2)
    mp = dp % plane
    other = (dp, 1 - core)

    def place(index):
        return ((index[0] * n1 + index[1]) * n2 + index[2], core)

    def moved(axis, k):
        target = list(me)
        target[axis] = (me[axis] + k) % grid[axis]
        return tuple(target)

    barrier = pltpu.get_barrier_semaphore()
    greet = [place(moved(0, k)) for k in range(1, n0)]
    greet += [(me[0] * plane + (mp + k) % plane, core) for k in range(1, plane)]
    greet.append(other)
    for device in greet:
        pl.semaphore_signal(barrier, inc=1, device_id=device, device_id_type=MESH)

    loads = [
        pltpu.make_async_copy(src, wide.at[pl.ds(start, src.shape[0])], load_sem.at[i])
        for i, (src, start) in enumerate(
            (
                (pd_hbm, 2 * rows),
                (qu_hbm, 2 * rows + small_rows),
                (qd_hbm, 2 * rows + 2 * small_rows),
                (td_hbm, 2 * rows + 3 * small_rows),
                (pu_hbm, 0),
                (tu_hbm, rows),
            )
        )
    ]
    loads.append(pltpu.make_async_copy(x_hbm, feats, load_sem.at[6]))
    for load in loads:
        load.start()
    for load in loads[:4]:
        load.wait()
    for w in range(4):
        small[w, me[0], me[1], me[2]] = wide[
            pl.ds(2 * rows + w * small_rows, small_rows), :
        ].astype(jnp.bfloat16)
    pl.semaphore_wait(barrier, len(greet))

    def take(load, buffer, start):
        load.wait()
        buffer[me[0], me[1], me[2]] = wide[pl.ds(start, rows), :].astype(jnp.bfloat16)

    hops = n0 - 1
    kinds = [("small", 0)] + [("up", i) for i in range(4)]
    kinds += [("target", i) for i in (0, 1, 3)]
    main = len(kinds)
    kinds += [("target", 2), ("small", 1)]
    late = [main + 1, main]

    def piece(c, lane, sel):
        kind, index = kinds[c]
        if kind == "small":
            return small.at[
                pl.ds(2 * index, 2), sel[0], sel[1], sel[2], :, pl.ds(lane * half, half)
            ]
        buffer = up if kind == "up" else tup
        return buffer.at[sel[0], sel[1], sel[2], :, pl.ds(index * chunk + lane * TILE, TILE)]

    def gather_copy(c, lane, ref, sem, target):
        return pltpu.make_async_remote_copy(
            src_ref=ref,
            dst_ref=ref,
            send_sem=ag_s.at[c, lane, sem],
            recv_sem=ag_r.at[c, lane, sem],
            device_id=place(target),
            device_id_type=MESH,
        )

    def inside_line(index):
        return jnp.logical_and(index >= 0, index < n0)

    def line_each(c, lane, hop, way, act):
        sel = [None, slice(None), slice(None)] if c in late else [None, me[1], me[2]]
        for bit, turn in enumerate((1, -1)):
            block = me[0] - turn * (hop if way == "send" else hop + 1)
            fits = inside_line(block)
            if way == "send":
                fits = jnp.logical_and(fits, inside_line(me[0] + turn))

            @pl.when(fits)
            def _(bit=bit, turn=turn, block=block):
                ref = piece(c, lane, [block] + sel[1:])
                target = (me[0] + (turn if way == "send" else -turn), me[1], me[2])
                act(gather_copy(c, lane, ref, 2 * hop + bit, target))

    def line_hop(c, lane, hop):
        if hop:
            line_each(c, lane, hop - 1, "recv", lambda copy: copy.wait_recv())
        line_each(c, lane, hop, "send", lambda copy: copy.start())

    def side_copy(c, lane, phase):
        axis, second = ((2, 1), (1, 2))[lane]
        sel = [me[0] if c in late else slice(None), me[1], me[2]]
        if phase:
            sel[axis] = slice(None)
        return gather_copy(
            c, lane, piece(c, lane, sel), 2 * hops + phase, moved((axis, second)[phase], 1)
        )

    def gather_line(c, hop):
        for lane in range(2):
            line_hop(c, lane, hop)

    def gather_side(c, phase):
        for lane in range(2):
            if phase:
                side_copy(c, lane, 0).wait_recv()
            elif c not in late:
                line_each(c, lane, hops - 1, "recv", lambda copy: copy.wait_recv())
            side_copy(c, lane, phase).start()

    def gather_end(c):
        for lane in range(2):
            if c in late:
                line_each(c, lane, hops - 1, "recv", lambda copy: copy.wait_recv())
            else:
                side_copy(c, lane, 1).wait_recv()

    late_items = [(c, lane, hop) for hop in range(hops) for c in late for lane in range(2)]

    def late_next():
        if late_items:
            c, lane, hop = late_items.pop(0)
            if hop == 0:
                side_copy(c, lane, 1).wait_recv()
            line_hop(c, lane, hop)

    def gather_sent():
        for c in range(len(kinds)):
            for lane in range(2):
                for hop in range(hops):
                    line_each(c, lane, hop, "send", lambda copy: copy.wait_send())
                for phase in range(2):
                    side_copy(c, lane, phase).wait_send()

    def sum_copies(buffers, i, stage):
        first, second, send, recv = buffers
        if stage == 0:
            ref = first.at[i, mp]
            return [
                pltpu.make_async_remote_copy(
                    src_ref=ref,
                    dst_ref=ref,
                    send_sem=send.at[i, k - 1],
                    recv_sem=recv.at[i, k - 1],
                    device_id=(me[0] * plane + (mp + k) % plane, core),
                    device_id_type=MESH,
                )
                for k in range(1, plane)
            ]
        ref = second.at[i, me[0]]
        return [
            pltpu.make_async_remote_copy(
                src_ref=ref,
                dst_ref=ref,
                send_sem=send.at[i, plane - 1 + k - 1],
                recv_sem=recv.at[i, plane - 1 + k - 1],
                device_id=place(moved(0, k)),
                device_id_type=MESH,
            )
            for k in range(1, n0)
        ]

    narrow_sum = (pa, pb, ps_s, ps_r)
    whole_sum = (qa, qb, qs_s, qs_r)
    scalar_sum = (ta, tb, ts_s, ts_r)

    def sum_start(buffers, i):
        for copy in sum_copies(buffers, i, 0):
            copy.start()

    def sum_middle(buffers, i):
        for copy in sum_copies(buffers, i, 0):
            copy.wait()
        first, second = buffers[:2]
        total = first[i, 0]
        for j in range(1, plane):
            total = total + first[i, j]
        second[i, me[0]] = total
        for copy in sum_copies(buffers, i, 1):
            copy.start()

    def sum_end(buffers, i):
        for copy in sum_copies(buffers, i, 1):
            copy.wait()
        second = buffers[1]
        total = second[i, 0]
        for j in range(1, n0):
            total = total + second[i, j]
        return total

    def swap(i):
        return pltpu.make_async_remote_copy(
            src_ref=ex.at[i],
            dst_ref=exr.at[i],
            send_sem=ex_s.at[i],
            recv_sem=ex_r.at[i],
            device_id=other,
            device_id_type=MESH,
        )

    def swap_end(i):
        swap(i).wait()

        def add(b):
            part = pl.ds(pl.multiple_of(b * rows, rows), rows)
            ex[i, part, :] = (
                ex[i, part, :].astype(jnp.float32) + exr[i, part, :].astype(jnp.float32)
            ).astype(jnp.bfloat16)

        loop(blocks, add)

    def weight(w, columns):
        return small[w, :, :, :, :, columns].reshape(plane * n0 * small_rows, columns.size)

    def columns_at(start, size):
        return pl.ds(pl.multiple_of(start, TILE), size)

    def hidden_chunk(weights, i, slot):
        def one(lane):
            columns = columns_at(i * chunk + lane * TILE, TILE)
            matrix = weights[:, :, :, :, columns].reshape(n0 * plane * rows, TILE)
            values = jnp.dot(feats[...], matrix, preferred_element_type=jnp.float32)
            wide[:, columns] = values
            spot = columns_at(lane * TILE, TILE)
            pa[slot, mp, 0:1, spot] = jnp.sum(values, 0, keepdims=True)
            pa[slot, mp, 1:2, spot] = jnp.sum(values * values, 0, keepdims=True)

        loop(2, one)

    def spread(total):
        mean = total[0:1] / total_views
        return mean, lax.rsqrt(total[1:2] / total_views - mean * mean + NORM_EPS)

    def act_tiles(start, count, mean, inverse, norm, act_ref, hat_ref, act_start):
        for n in range(count):
            columns = pl.ds(start + n * TILE, TILE)
            targets = pl.ds(act_start + n * TILE, TILE)
            here = slice(n * TILE, (n + 1) * TILE)
            mean_n, inverse_n = mean[:, here], inverse[:, here]
            gain, shift = norm[0:1, columns], norm[1:2, columns]

            def one(b):
                part = pl.ds(pl.multiple_of(b * rows, rows), rows)
                hat = (wide[part, columns] - mean_n) * inverse_n
                value = hat * gain + shift
                action = 0.5 * value * (1.0 + gelu_tanh(value))
                act_ref[b // 2, b % 2, :, targets] = action.astype(jnp.bfloat16)
                if hat_ref is not None:
                    hat_ref[b // 2, b % 2, :, targets] = hat.astype(jnp.bfloat16)

            loop(blocks, one)

    def act_chunk(slot, i, norm, act_ref, hat_ref, inv_ref, w, act_start):
        total = sum_end(narrow_sum, slot)
        mean, inverse = spread(total)
        if inv_ref is not None:
            inv_ref[:, pl.ds(i * chunk, chunk)] = inverse
        act_tiles(i * chunk, chunk // TILE, mean, inverse, norm, act_ref, hat_ref, act_start)
        action = act_ref[:, :, :, pl.ds(act_start, chunk)].reshape(views, chunk)
        product = nt_dot(action, weight(w, pl.ds(i * chunk, chunk)))
        if i == 0:
            acc[...] = product
        else:
            acc[...] += product
        return total

    count = []

    def middle_stats():
        swap_end(0)

        def one(n):
            columns = columns_at(n * TILE, TILE)
            values = jnp.dot(ex[0], weight(1, columns), preferred_element_type=jnp.float32)
            qa[0, mp, 0:1, columns] = jnp.sum(values, 0, keepdims=True)
            qa[0, mp, 1:2, columns] = jnp.sum(values * values, 0, keepdims=True)

        loop(width // TILE, one)
        sum_start(whole_sum, 0)

    def online_query():
        mean, inverse = spread(sum_end(whole_sum, 0))
        inv2[...] = inverse
        means[...] = mean

        def one(n):
            columns = columns_at(n * TILE, TILE)
            wide[:, pl.ds(3 * chunk, TILE)] = jnp.dot(
                ex[0], weight(1, columns), preferred_element_type=jnp.float32
            )
            mean_n, inverse_n = means[:, columns], inv2[:, columns]
            gain, shift = pred_norm[0:1, columns], pred_norm[1:2, columns]

            def tile(b):
                part = pl.ds(pl.multiple_of(b * rows, rows), rows)
                hat = (wide[part, pl.ds(3 * chunk, TILE)] - mean_n) * inverse_n
                value = hat * gain + shift
                action = 0.5 * value * (1.0 + gelu_tanh(value))
                act2[b // 2, b % 2, :, columns] = action.astype(jnp.bfloat16)
                hat2[b // 2, b % 2, :, columns] = hat.astype(jnp.bfloat16)

            loop(blocks, tile)

        loop(width // TILE, one)
        ex[1] = nt_dot(
            act2[...].reshape(views, width), weight(2, pl.ds(0, width))
        ).astype(jnp.bfloat16)
        swap(1).start()

    def early(c):
        slot = c - 3
        if 0 <= slot <= 3:
            act_chunk(slot, slot, proj_norm, act1, hat1, inv1, 0, slot * chunk)
        elif slot >= 4:
            act_chunk(slot, slot - 4, target_norm, tact, None, None, 3, 0)
        if slot == 3:
            ex[0] = acc[...].astype(jnp.bfloat16)
            swap(0).start()
            middle_stats()
        if slot == 5:
            online_query()

    def between(c):
        if c >= 2:
            sum_middle(narrow_sum, c - 2)
        if c == 7:
            sum_middle(whole_sum, 0)
        if c == 3:
            sum_middle(scalar_sum, 0)

    def compute(c):
        if c == 0:
            loads[6].wait()
            ta[0, mp] = jnp.broadcast_to(jnp.sum(keep[...], 0, keepdims=True), (8, 128))
            sum_start(scalar_sum, 0)
        else:
            i = c - 1
            hidden_chunk(up if i < 4 else tup, i % 4, i)
            sum_start(narrow_sum, i)
        if c == 4:
            count.append(sum_end(scalar_sum, 0))

    gather_line(0, 0)
    gather_side(late[0], 0)
    take(loads[5], tup, rows)
    gather_side(late[1], 0)
    take(loads[4], up, 0)
    gather_line(1, 0)
    gather_line(0, 1)
    gather_line(2, 0)
    gather_line(1, 1)
    gather_line(0, 2)
    for c in late:
        gather_side(c, 1)
    for tick in range(main + 2):
        if tick < main:
            gather_side(tick, 0)
        for ahead, hop in ((1, 2), (2, 1), (3, 0)):
            if tick + ahead < main:
                gather_line(tick + ahead, hop)
        if tick >= 1:
            for _ in range(LATE_PER_TICK):
                late_next()
        if 1 <= tick <= main:
            gather_side(tick - 1, 1)
        if 2 <= tick <= main:
            early(tick - 2)
            between(tick - 2)
            gather_end(tick - 2)
            compute(tick - 2)
    gather_end(main + 1)
    early(main - 1)
    between(main - 1)
    gather_end(main)
    compute(main - 1)
    early(main)
    between(main)
    gather_end(main - 1)
    compute(main)
    early(main + 1)
    sum_middle(narrow_sum, 7)
    act_chunk(7, 3, target_norm, tact, None, None, 3, 0)
    ex[2] = acc[...].astype(jnp.bfloat16)
    swap(2).start()
    gather_sent()
    swap_end(1)
    swap(2).wait()

    scale = -2.0 / count[0][0:1, 0:1]

    def unit_scale(values):
        return lax.rsqrt(jnp.sum(values * values, 1, keepdims=True) + UNIT_EPS)

    even = (lax.broadcasted_iota(jnp.int32, (rows, acc.shape[1]), 0) % 2) == 0

    def loss_tile(b, carry):
        part = pl.ds(pl.multiple_of(b * rows, rows), rows)
        query = ex[1, part, :].astype(jnp.float32)
        target = ex[2, part, :].astype(jnp.float32) + exr[2, part, :].astype(jnp.float32)
        target = target * unit_scale(target)
        goal = jnp.where(even, pltpu.roll(target, rows - 1, 0), pltpu.roll(target, 1, 0))
        back = unit_scale(query)
        unit = query * back
        cosine = jnp.sum(unit * goal, 1, keepdims=True)
        kept = keep[part, :]
        ex[1, part, :] = ((scale * kept * back) * (goal - cosine * unit)).astype(jnp.bfloat16)
        return carry + kept * (2.0 - 2.0 * cosine)

    loss_rows = lax.fori_loop(0, blocks, loss_tile, jnp.zeros((rows, 1), jnp.float32))
    ta[1, mp] = jnp.broadcast_to(jnp.sum(loss_rows, 0, keepdims=True), (8, 128))
    sum_start(scalar_sum, 1)

    def back_norm(i, w, grads, hat_ref, norm):
        def one(n):
            columns = columns_at(n * TILE, TILE)
            wide[:, columns] = jnp.dot(
                ex[grads], weight(w, columns), preferred_element_type=jnp.float32
            )
            gain, shift = norm[0:1, columns], norm[1:2, columns]

            def tile(b, carry):
                part = pl.ds(pl.multiple_of(b * rows, rows), rows)
                hat = hat_ref[b // 2, b % 2, :, columns].astype(jnp.float32)
                value = hat * gain + shift
                bent = gelu_tanh(value)
                slope = 0.5 * (1.0 + bent) + (0.5 * GELU_A) * value * (1.0 - bent * bent) * (
                    1.0 + (3.0 * GELU_B) * value * value
                )
                grad = wide[part, columns] * slope
                wide[part, columns] = grad
                cross = grad * hat
                return (
                    carry[0] + jnp.sum(grad.reshape(rows // 8, 8, TILE), 0),
                    carry[1] + jnp.sum(cross.reshape(rows // 8, 8, TILE), 0),
                )

            zero = jnp.zeros((8, TILE), jnp.float32)
            sums = lax.fori_loop(0, blocks, tile, (zero, zero))
            qa[i, mp, 0:1, columns] = jnp.sum(sums[0], 0, keepdims=True)
            qa[i, mp, 1:2, columns] = jnp.sum(sums[1], 0, keepdims=True)

        loop(width // TILE, one)
        sum_start(whole_sum, i)

    def grad_hidden(stat, hat_ref, norm, inv_ref, columns):
        gain = norm[0:1, columns] * inv_ref[:, columns]
        shift = stat[0:1, columns] / total_views
        slope = stat[1:2, columns] / total_views

        def tile(b):
            part = pl.ds(pl.multiple_of(b * rows, rows), rows)
            hat = hat_ref[b // 2, b % 2, :, columns].astype(jnp.float32)
            hat_ref[b // 2, b % 2, :, columns] = (
                gain * (wide[part, columns] - shift - hat * slope)
            ).astype(jnp.bfloat16)

        loop(blocks, tile)

    def small_grad(w, grads, act_ref):
        def one(n):
            columns = columns_at(n * TILE, TILE)
            right = act_ref[:, :, :, columns].reshape(views, TILE)
            value = tn_dot(ex[grads], right).astype(jnp.bfloat16)
            small[w, :, :, :, :, columns] = value.reshape(n0, n1, n2, small_rows, TILE)

        loop(width // TILE, one)

    def reduce_copies(kind, g, lane, phase):
        axis, second = ((1, 2), (2, 1))[lane]
        if kind == "up":
            columns = pl.ds(g * chunk + lane * TILE, TILE)
            send, recv = rs_s, rs_r
            source = lambda sel: tup.at[sel[0], sel[1], sel[2], :, columns]
            lands = (
                act2.at[:, :, :, columns],
                hat2.at[:, 0, :, columns],
                hat2.at[me[0], 1, :, columns],
            )
        else:
            columns = pl.ds(lane * half, half)
            send, recv = ss_s, ss_r
            source = lambda sel: small.at[3 - g, sel[0], sel[1], sel[2], :, columns]
            lands = (
                sr1.at[g, :, :, :, columns],
                sr2.at[g, :, :, columns],
                sr3.at[g, me[0], :, columns],
            )
        copies = []
        moves = range(1, n0) if phase == 2 else (1,)
        for k in moves:
            axis_now = (axis, second, 0)[phase]
            target = moved(axis_now, k)
            sel = [slice(None)] * 3
            if phase > 0:
                sel[axis] = me[axis]
            if phase > 1:
                sel[second] = me[second]
            sel[axis_now] = target[axis_now]
            copies.append(
                pltpu.make_async_remote_copy(
                    src_ref=source(sel),
                    dst_ref=lands[phase],
                    send_sem=send.at[g, lane, phase + k - 1],
                    recv_sem=recv.at[g, lane, phase + k - 1],
                    device_id=place(target),
                    device_id_type=MESH,
                )
            )
        return copies

    def reduce_step(kind, g, phase):
        for lane in range(2):
            if phase:
                for copy in reduce_copies(kind, g, lane, phase - 1):
                    copy.wait()
                reduce_add(kind, g, lane, phase)
            if phase < 3:
                for copy in reduce_copies(kind, g, lane, phase):
                    copy.start()

    def plus(first_op, second_op):
        return (first_op.astype(jnp.float32) + second_op.astype(jnp.float32)).astype(jnp.bfloat16)

    def reduce_add(kind, g, lane, phase):
        big = kind == "up"
        if big:
            columns = pl.ds(g * chunk + lane * TILE, TILE)
        else:
            columns = pl.ds(lane * half, half)
        if phase == 1:

            def add(j):
                z, i = j // 2, j % 2
                y, x = (me[1], i) if lane == 0 else (i, me[2])
                if big:
                    tup[z, y, x, :, columns] = plus(
                        tup[z, y, x, :, columns], act2[z, i, :, columns]
                    )
                else:
                    small[3 - g, z, y, x, :, columns] = plus(
                        small[3 - g, z, y, x, :, columns], sr1[g, z, i, :, columns]
                    )

            loop(n0 * 2, add)
        elif phase == 2:

            def add(z):
                if big:
                    tup[z, me[1], me[2], :, columns] = plus(
                        tup[z, me[1], me[2], :, columns], hat2[z, 0, :, columns]
                    )
                else:
                    small[3 - g, z, me[1], me[2], :, columns] = plus(
                        small[3 - g, z, me[1], me[2], :, columns], sr2[g, z, :, columns]
                    )

            loop(n0, add)
        else:
            if big:
                total = tup[me[0], me[1], me[2], :, columns].astype(jnp.float32)
                for k in range(1, n0):
                    total = total + hat2[(me[0] + k) % n0, 1, :, columns].astype(jnp.float32)
                gu_out[:, columns] = total
            else:
                total = small[3 - g, me[0], me[1], me[2], :, columns].astype(jnp.float32)
                for k in range(1, n0):
                    total = total + sr3[g, (me[0] + k) % n0, :, columns].astype(jnp.float32)
                gs_out[g, :, columns] = total

    back_norm(1, 2, 1, hat2, pred_norm)
    small_grad(3, 1, act2)
    reduce_step("small", 0, 0)
    sum_middle(whole_sum, 1)
    pred_stat[...] = sum_end(whole_sum, 1)
    loop(
        width // TILE,
        lambda n: grad_hidden(pred_stat, hat2, pred_norm, inv2, columns_at(n * TILE, TILE)),
    )
    ex[3] = nt_dot(hat2[...].reshape(views, width), weight(1, pl.ds(0, width))).astype(jnp.bfloat16)
    swap(3).start()
    small_grad(2, 0, hat2)
    reduce_step("small", 1, 0)
    reduce_step("small", 0, 1)
    swap_end(3)
    back_norm(2, 0, 3, hat1, proj_norm)
    sum_middle(scalar_sum, 1)
    small_grad(1, 3, act1)
    pl.semaphore_signal(ready, inc=1, device_id=other, device_id_type=MESH)
    reduce_step("small", 2, 0)
    reduce_step("small", 1, 1)
    reduce_step("small", 0, 2)
    sum_middle(whole_sum, 2)
    proj_stat[...] = sum_end(whole_sum, 2)

    def up_grad(g):
        for n in range(2):
            grad_hidden(proj_stat, hat1, proj_norm, inv1, pl.ds(g * chunk + n * TILE, TILE))
        columns = pl.ds(g * chunk, chunk)

        def one(z):
            left = feats[:, columns_at(z * plane * rows, plane * rows)]
            value = tn_dot(left, hat1[:, :, :, columns].reshape(views, chunk))
            tup[z, :, :, :, columns] = value.astype(jnp.bfloat16).reshape(n1, n2, rows, chunk)

        loop(n0, one)
        reduce_step("up", g, 0)

    parts = ig_s.shape[0]

    def input_copy(q):
        return pltpu.make_async_remote_copy(
            src_ref=act1.at[:, :, :, pl.ds(q * TILE, TILE)],
            dst_ref=act1.at[:, :, :, pl.ds((parts + q) * TILE, TILE)],
            send_sem=ig_s.at[q],
            recv_sem=ig_r.at[q],
            device_id=other,
            device_id_type=MESH,
        )

    def input_product(q, side):
        first = side * (n0 // 2) + q // n1
        matrix = up[first, q % n1].reshape(n2 * rows, width)
        return nt_dot(hat1[...].reshape(views, width), matrix)

    for g in range(4):
        up_grad(g)
        if g == 0:
            reduce_step("small", 2, 1)
            reduce_step("small", 1, 2)
        else:
            reduce_step("up", g - 1, 1)
        if g == 1:
            reduce_step("small", 0, 3)
            reduce_step("small", 2, 2)
        if g >= 2:
            reduce_step("up", g - 2, 2)
    pl.semaphore_wait(ready, 1)

    def send_part(q):
        act1[:, :, :, pl.ds(q * TILE, TILE)] = (
            input_product(q, 1 - core).astype(jnp.bfloat16).reshape(n0, 2, rows, TILE)
        )
        input_copy(q).start()

    def own_part(q):
        wide[:, pl.ds(q * TILE, TILE)] = input_product(q, core)

    for q in range(2):
        send_part(q)
    reduce_step("up", 3, 1)
    reduce_step("up", 2, 2)
    for q in range(2, parts):
        send_part(q)
    for q in range(parts):
        own_part(q)
    reduce_step("up", 3, 2)
    out_copies = []
    for q in range(parts):
        input_copy(q).wait()

        def add(b, q=q):
            part = pl.ds(pl.multiple_of(b * rows, rows), rows)
            wide[part, pl.ds(q * TILE, TILE)] += act1[
                b // 2, b % 2, :, pl.ds((parts + q) * TILE, TILE)
            ].astype(jnp.float32)

        loop(blocks, add)
    out_copy = pltpu.make_async_copy(
        wide.at[:, pl.ds(0, parts * TILE)], ig_hbm, load_sem.at[0]
    )
    out_copy.start()
    for g in (1, 2):
        reduce_step("small", g, 3)
    for g in range(4):
        reduce_step("up", g, 3)
    loss_out[...] = sum_end(scalar_sum, 1) / count[0]
    out_copy.wait()


def kernel_step(grid, total_views, features, keep, ups, downs, norms):
    n0, n1, n2 = grid
    plane = n1 * n2
    views, depth = features.shape
    rows, width = ups[0].shape
    small_rows = downs[0].shape[0]
    out = small_rows * n0 * plane
    parts = depth // 2 // TILE
    low, full = jnp.bfloat16, jnp.float32
    vm = pltpu.VMEM
    dma = pltpu.SemaphoreType.DMA
    anywhere = pl.BlockSpec(memory_space=pl.ANY)
    inside = pl.BlockSpec(memory_space=pltpu.VMEM)
    spread_shape = (n0, 2, rows, width)
    moves = 2 * (n0 - 1) + 2
    sum_moves = plane - 1 + n0 - 1
    return pl.pallas_call(
        functools.partial(step_kernel, grid, total_views),
        out_shape=(
            jax.ShapeDtypeStruct((views, depth // 2), full),
            jax.ShapeDtypeStruct((rows, width), full),
            jax.ShapeDtypeStruct((3, small_rows, width), full),
            jax.ShapeDtypeStruct((2, width), full),
            jax.ShapeDtypeStruct((2, width), full),
            jax.ShapeDtypeStruct((8, 128), full),
        ),
        in_specs=[anywhere] * 7 + [inside] * 4,
        out_specs=(anywhere,) + (inside,) * 5,
        scratch_shapes=[
            vm((views, depth), low),
            vm((n0, n1, n2, rows, width), low),
            vm((n0, n1, n2, rows, width), low),
            vm((4, n0, n1, n2, small_rows, width), low),
            vm(spread_shape, low),
            vm(spread_shape, low),
            vm(spread_shape, low),
            vm(spread_shape, low),
            vm((views, width), full),
            vm((n0, 2, rows, width // 4), low),
            vm((views, out), full),
            vm((4, views, out), low),
            vm((4, views, out), low),
            vm((3, n0, 2, small_rows, width), low),
            vm((3, n0, small_rows, width), low),
            vm((3, n0, small_rows, width), low),
            vm((1, width), full),
            vm((1, width), full),
            vm((1, width), full),
            vm((8, plane, 2, width // 4), full),
            vm((8, n0, 2, width // 4), full),
            vm((3, plane, 2, width), full),
            vm((3, n0, 2, width), full),
            vm((2, plane, 8, 128), full),
            vm((2, n0, 8, 128), full),
            dma((7,)),
            dma((10, 2, moves)),
            dma((10, 2, moves)),
            dma((8, sum_moves)),
            dma((8, sum_moves)),
            dma((3, sum_moves)),
            dma((3, sum_moves)),
            dma((2, sum_moves)),
            dma((2, sum_moves)),
            dma((4,)),
            dma((4,)),
            dma((4, 2, n0 + 1)),
            dma((4, 2, n0 + 1)),
            dma((3, 2, n0 + 1)),
            dma((3, 2, n0 + 1)),
            dma((parts,)),
            dma((parts,)),
            pltpu.SemaphoreType.REGULAR,
        ],
        compiler_params=pltpu.CompilerParams(
            collective_id=0, has_side_effects=True, vmem_limit_bytes=VMEM_LIMIT
        ),
    )(features, *ups, *downs, *norms, keep)


def step_body(grid, *args):
    (
        features,
        keep_mask,
        proj_up,
        proj_down,
        proj_norm,
        pred_up,
        pred_down,
        pred_norm,
        moment_proj_up,
        moment_proj_down,
        moment_proj_norm,
        moment_pred_up,
        moment_pred_down,
        moment_pred_norm,
        target_up,
        target_down,
        target_norm,
    ) = args
    if grid is None:
        return plain_body(*args)
    total_views = float(features.shape[0] * lax.axis_size("dp"))
    input_grad, shard_proj_up, shard_small, proj_stat, pred_stat, loss = kernel_step(
        grid,
        total_views,
        features,
        keep_mask.astype(jnp.float32).reshape(-1, 1),
        (proj_up, target_up),
        (proj_down, pred_up, pred_down, target_down),
        (proj_norm, pred_norm, target_norm),
    )
    shard_pred_down, shard_pred_up, shard_proj_down = shard_small[0], shard_small[1], shard_small[2]
    grad_proj_norm = proj_stat[::-1]
    grad_pred_norm = pred_stat[::-1]
    return finish(
        total_views,
        args,
        loss[0, 0],
        input_grad,
        shard_proj_up,
        shard_proj_down,
        grad_proj_norm,
        shard_pred_up,
        shard_pred_down,
        grad_pred_norm,
    )


def solution(mesh):
    placed = (
        P("dp", None),
        P("dp"),
        P("dp", "tensor"),
        P("dp", "tensor"),
        P(None, "tensor"),
        P("dp", "tensor"),
        P("dp", "tensor"),
        P(None, "tensor"),
        P("dp", "tensor"),
        P("dp", "tensor"),
        P(None, "tensor"),
        P("dp", "tensor"),
        P("dp", "tensor"),
        P(None, "tensor"),
        P("dp", "tensor"),
        P("dp", "tensor"),
        P(None, "tensor"),
    )
    return jax.shard_map(
        functools.partial(step_body, GRIDS.get(mesh.shape["dp"])),
        mesh=mesh,
        in_specs=placed,
        out_specs=(
            P(),
            P("dp", "tensor"),
            P("dp", "tensor"),
            P("dp", "tensor"),
            P("dp", "tensor"),
            P("dp", "tensor"),
            P("dp", "tensor"),
            P("dp", "tensor"),
            P(None, "tensor"),
            P(None, "tensor"),
            P(None, "tensor"),
            P("dp", "tensor"),
            P("dp", "tensor"),
            P("dp", "tensor"),
            P("dp", "tensor"),
            P("dp", "tensor"),
            P("dp", "tensor"),
            P(None, "tensor"),
            P(None, "tensor"),
            P(None, "tensor"),
            P("dp", "tensor"),
            P("dp", "tensor"),
            P(None, "tensor"),
        ),
        check_vma=False,
    )
```

```python
import functools
import math

import jax
import jax.numpy as jnp
from jax import lax
from jax.experimental import pallas as pl
from jax.experimental.pallas import tpu as pltpu
from jax.sharding import PartitionSpec as P

NORM_EPS = 1e-05
UNIT_EPS = 1e-06
RATE_PROJ_UP = 9.0
RATE_PROJ_DOWN = 1.2
RATE_PROJ_NORM = 40.0
RATE_PRED_UP = 18.0
RATE_PRED_DOWN = 0.9
RATE_PRED_NORM = 30.0


def across(matrix, weight):
    return lax.dot_general(
        matrix, weight, (((1,), (1,)), ((), ())), preferred_element_type=jnp.float32
    )


def outer_sum(first_op, second_op):
    return lax.dot_general(
        first_op, second_op, (((0,), (0,)), ((), ())), preferred_element_type=jnp.float32
    )


def standard(hidden, col_sum, col_square, total_views):
    middle_mean = col_sum / total_views
    inverse = lax.rsqrt(col_square / total_views - middle_mean * middle_mean + NORM_EPS)
    return ((hidden - middle_mean) * inverse, inverse)


def norm_back(grad_out, scaled, inverse, params, sum_grad, sum_cross, total_views):
    return (
        params[0]
        * inverse
        * (grad_out - sum_grad / total_views - scaled * (sum_cross / total_views))
    )


def unit_rows(values):
    return values * lax.rsqrt(jnp.sum(values * values, 1, keepdims=True) + UNIT_EPS)


def partner(values):
    width = values.shape[1]
    return values.reshape(-1, 2, width)[:, ::-1, :].reshape(-1, width)


def nesterov(weight, moment, grad, rate):
    fresh = 0.5 * moment + grad
    return (fresh, weight - rate * (grad + 0.5 * fresh))


def finish(
    total_views,
    args,
    loss,
    input_grad,
    shard_proj_up,
    shard_proj_down,
    grad_proj_norm,
    shard_pred_up,
    shard_pred_down,
    grad_pred_norm,
):
    (proj_up, proj_down, proj_norm, pred_up, pred_down, pred_norm) = args[2:8]
    (
        moment_proj_up,
        moment_proj_down,
        moment_proj_norm,
        moment_pred_up,
        moment_pred_down,
        moment_pred_norm,
        target_up,
        target_down,
        target_norm,
    ) = args[8:]
    scale = math.sqrt(total_views)
    mom_pu, next_pu = nesterov(proj_up, moment_proj_up, shard_proj_up, RATE_PROJ_UP * scale)
    mom_pd, next_pd = nesterov(proj_down, moment_proj_down, shard_proj_down, RATE_PROJ_DOWN * scale)
    mom_pn, next_pn = nesterov(proj_norm, moment_proj_norm, grad_proj_norm, RATE_PROJ_NORM * scale)
    mom_qu, next_qu = nesterov(pred_up, moment_pred_up, shard_pred_up, RATE_PRED_UP * scale)
    mom_qd, next_qd = nesterov(pred_down, moment_pred_down, shard_pred_down, RATE_PRED_DOWN * scale)
    mom_qn, next_qn = nesterov(pred_norm, moment_pred_norm, grad_pred_norm, RATE_PRED_NORM * scale)
    target_up_next = 0.5 * target_up + 0.5 * next_pu
    target_down_next = 0.5 * target_down + 0.5 * next_pd
    target_norm_next = 0.5 * target_norm + 0.5 * next_pn
    return (
        loss,
        input_grad,
        shard_proj_up,
        mom_pu,
        next_pu,
        shard_proj_down,
        mom_pd,
        next_pd,
        grad_proj_norm,
        mom_pn,
        next_pn,
        shard_pred_up,
        mom_qu,
        next_qu,
        shard_pred_down,
        mom_qd,
        next_qd,
        grad_pred_norm,
        mom_qn,
        next_qn,
        target_up_next,
        target_down_next,
        target_norm_next,
    )


def plain_body(
    features,
    keep_mask,
    proj_up,
    proj_down,
    proj_norm,
    pred_up,
    pred_down,
    pred_norm,
    moment_proj_up,
    moment_proj_down,
    moment_proj_norm,
    moment_pred_up,
    moment_pred_down,
    moment_pred_norm,
    target_up,
    target_down,
    target_norm,
):
    total_views = float(features.shape[0] * lax.axis_size("dp"))
    width = proj_up.shape[1]

    def gathered(parts):
        low = jnp.stack([part.astype(jnp.bfloat16) for part in parts])
        full = lax.all_gather(low, "dp", axis=1, tiled=True)
        return tuple(full[i] for i in range(len(parts)))

    (up_full, tup_full) = gathered((proj_up, target_up))
    (down_full, pup_full, pdown_full, tdown_full) = gathered(
        (proj_down, pred_up, pred_down, target_down)
    )
    keep_float = keep_mask.astype(jnp.float32)
    hidden1 = jnp.dot(features, up_full, preferred_element_type=jnp.float32)
    target_hidden = jnp.dot(features, tup_full, preferred_element_type=jnp.float32)
    sums = lax.psum(
        jnp.stack(
            [
                jnp.sum(hidden1, 0),
                jnp.sum(hidden1 * hidden1, 0),
                jnp.sum(target_hidden, 0),
                jnp.sum(target_hidden * target_hidden, 0),
                jnp.full((width,), jnp.sum(keep_float)),
            ]
        ),
        "dp",
    )
    sum_one, square_one, sum_target, square_target = sums[0], sums[1], sums[2], sums[3]
    count = sums[4, 0]
    scaled1, inverse1 = standard(hidden1, sum_one, square_one, total_views)
    action1, gelu_back1 = jax.vjp(jax.nn.gelu, scaled1 * proj_norm[0] + proj_norm[1])
    action1 = action1.astype(jnp.bfloat16)
    target_scaled, target_inverse = standard(target_hidden, sum_target, square_target, total_views)
    target_action = jax.nn.gelu(target_scaled * target_norm[0] + target_norm[1]).astype(
        jnp.bfloat16
    )
    middle, target_out = (
        lax.psum(across(action1, down_full).astype(jnp.bfloat16), "tensor").astype(jnp.float32),
        lax.psum(across(target_action, tdown_full).astype(jnp.bfloat16), "tensor").astype(
            jnp.float32
        ),
    )
    middle_low = middle.astype(jnp.bfloat16)
    hidden2 = jnp.dot(middle_low, pup_full, preferred_element_type=jnp.float32)
    sum_two, square_two = lax.psum(
        jnp.stack([jnp.sum(hidden2, 0), jnp.sum(hidden2 * hidden2, 0)]), "dp"
    )
    scaled2, inverse2 = standard(hidden2, sum_two, square_two, total_views)
    action2, gelu_back2 = jax.vjp(jax.nn.gelu, scaled2 * pred_norm[0] + pred_norm[1])
    action2 = action2.astype(jnp.bfloat16)
    query = lax.psum(across(action2, pdown_full).astype(jnp.bfloat16), "tensor").astype(jnp.float32)
    goal = partner(unit_rows(target_out))

    def loss_terms(values):
        return jnp.sum(keep_float * (2.0 - 2.0 * jnp.sum(unit_rows(values) * goal, 1)))

    local_loss, loss_back = jax.vjp(loss_terms, query)
    (grad_query,) = loss_back(1.0 / count)
    grad_query = grad_query.astype(jnp.bfloat16)
    grad_pred_down = outer_sum(grad_query, action2)
    (grad_norm2,) = gelu_back2(jnp.dot(grad_query, pdown_full, preferred_element_type=jnp.float32))
    back_sum2, back_cross2, loss_row = lax.psum(
        jnp.stack(
            [
                jnp.sum(grad_norm2, 0),
                jnp.sum(grad_norm2 * scaled2, 0),
                jnp.full((width,), local_loss),
            ]
        ),
        "dp",
    )
    loss_total = loss_row[0]
    grad_hidden2 = norm_back(
        grad_norm2, scaled2, inverse2, pred_norm, back_sum2, back_cross2, total_views
    ).astype(jnp.bfloat16)
    grad_pred_norm = jnp.stack([back_cross2, back_sum2])
    grad_pred_up = outer_sum(middle_low, grad_hidden2)
    grad_middle = lax.psum(across(grad_hidden2, pup_full).astype(jnp.bfloat16), "tensor")
    grad_proj_down = outer_sum(grad_middle, action1)
    (grad_norm1,) = gelu_back1(jnp.dot(grad_middle, down_full, preferred_element_type=jnp.float32))
    back_sum1, back_cross1 = lax.psum(
        jnp.stack([jnp.sum(grad_norm1, 0), jnp.sum(grad_norm1 * scaled1, 0)]), "dp"
    )
    grad_hidden1 = norm_back(
        grad_norm1, scaled1, inverse1, proj_norm, back_sum1, back_cross1, total_views
    ).astype(jnp.bfloat16)
    grad_proj_norm = jnp.stack([back_cross1, back_sum1])
    grad_proj_up = outer_sum(features, grad_hidden1)
    input_grad = lax.psum_scatter(
        across(grad_hidden1, up_full).astype(jnp.bfloat16),
        "tensor",
        scatter_dimension=1,
        tiled=True,
    ).astype(jnp.float32)
    shard_proj_up = lax.psum_scatter(
        grad_proj_up.astype(jnp.bfloat16), "dp", scatter_dimension=0, tiled=True
    ).astype(jnp.float32)
    small = lax.psum_scatter(
        jnp.stack([grad_proj_down, grad_pred_up, grad_pred_down]).astype(jnp.bfloat16),
        "dp",
        scatter_dimension=1,
        tiled=True,
    ).astype(jnp.float32)
    shard_proj_down, shard_pred_up, shard_pred_down = small[0], small[1], small[2]
    loss = loss_total / count
    return finish(
        total_views,
        (
            features,
            keep_mask,
            proj_up,
            proj_down,
            proj_norm,
            pred_up,
            pred_down,
            pred_norm,
            moment_proj_up,
            moment_proj_down,
            moment_proj_norm,
            moment_pred_up,
            moment_pred_down,
            moment_pred_norm,
            target_up,
            target_down,
            target_norm,
        ),
        loss,
        input_grad,
        shard_proj_up,
        shard_proj_down,
        grad_proj_norm,
        shard_pred_up,
        shard_pred_down,
        grad_pred_norm,
    )


MESH = pl.DeviceIdType.MESH
GRIDS = {16: (4, 2, 2)}
TILE = 256
GELU_A = math.sqrt(2.0 / math.pi)
GELU_B = 0.044715
LATE_PER_TICK = 2
VMEM_LIMIT = 63 * 1024 * 1024


def loop(count, step):
    def one(i, carry):
        step(i)
        return carry

    lax.fori_loop(0, count, one, 0)


def nt_dot(first_op, second_op):
    return lax.dot_general(
        first_op, second_op, (((1,), (1,)), ((), ())), preferred_element_type=jnp.float32
    )


def tn_dot(first_op, second_op):
    return lax.dot_general(
        first_op, second_op, (((0,), (0,)), ((), ())), preferred_element_type=jnp.float32
    )


def gelu_parts(value):
    square = value * value
    gate = 0.5 + 0.5 * jnp.tanh(value * (GELU_A + (GELU_A * GELU_B) * square))
    return gate, square


def gelu_slope(value, gate, square):
    bend = value * (2.0 * GELU_A + (6.0 * GELU_A * GELU_B) * square)
    return gate * (1.0 + (1.0 - gate) * bend)


def step_kernel(
    grid,
    total_views,
    x_hbm,
    pu_hbm,
    tu_hbm,
    pd_hbm,
    qu_hbm,
    qd_hbm,
    td_hbm,
    proj_norm,
    pred_norm,
    target_norm,
    keep,
    ig_hbm,
    gu_out,
    qd_out,
    qu_out,
    pd_out,
    proj_stat,
    pred_stat,
    loss_out,
    feats,
    up,
    tup,
    small,
    act1,
    hat1,
    act2,
    hat2,
    wide,
    tact,
    acc,
    ex,
    exr,
    slope1,
    sr1,
    sr2,
    sr3,
    inv1,
    inv2,
    means,
    pa,
    pb,
    qa,
    qb,
    ta,
    tb,
    load_sem,
    ag_s,
    ag_r,
    ps_s,
    ps_r,
    qs_s,
    qs_r,
    ts_s,
    ts_r,
    ex_s,
    ex_r,
    rs_s,
    rs_r,
    ss_s,
    ss_r,
    ig_s,
    ig_r,
    ready,
):
    n0, n1, n2 = grid
    plane = n1 * n2
    views, width = wide.shape
    rows = up.shape[3]
    small_rows = small.shape[4]
    blocks = views // rows
    chunk = width // 4
    half = width // 2
    dp = lax.axis_index("dp")
    core = lax.axis_index("tensor")
    me = (dp // plane, (dp // n2) % n1, dp % n2)
    mp = dp % plane
    other = (dp, 1 - core)

    def place(index):
        return ((index[0] * n1 + index[1]) * n2 + index[2], core)

    def moved(axis, k):
        target = list(me)
        target[axis] = (me[axis] + k) % grid[axis]
        return tuple(target)

    barrier = pltpu.get_barrier_semaphore()
    greet = [place(moved(0, k)) for k in range(1, n0)]
    greet += [(me[0] * plane + (mp + k) % plane, core) for k in range(1, plane)]
    greet.append(other)
    for device in greet:
        pl.semaphore_signal(barrier, inc=1, device_id=device, device_id_type=MESH)

    loads = [
        pltpu.make_async_copy(src, wide.at[pl.ds(start, src.shape[0])], load_sem.at[i])
        for i, (src, start) in enumerate(
            (
                (pd_hbm, 2 * rows),
                (qu_hbm, 2 * rows + small_rows),
                (qd_hbm, 2 * rows + 2 * small_rows),
                (td_hbm, 2 * rows + 3 * small_rows),
                (pu_hbm, 0),
                (tu_hbm, rows),
            )
        )
    ]
    loads.append(pltpu.make_async_copy(x_hbm, feats, load_sem.at[6]))
    for i in (4, 0, 1, 2, 3, 5, 6):
        loads[i].start()

    def take(load, buffer, start):
        load.wait()
        buffer[me[0], me[1], me[2]] = wide[pl.ds(start, rows), :].astype(jnp.bfloat16)

    def take_small():
        for w, load in enumerate(loads[:4]):
            load.wait()
            small[w, me[0], me[1], me[2]] = wide[
                pl.ds(2 * rows + w * small_rows, small_rows), :
            ].astype(jnp.bfloat16)

    take(loads[4], up, 0)
    pl.semaphore_wait(barrier, len(greet))

    hops = n0 - 1
    kinds = [("up", i) for i in range(4)] + [("small", 0)]
    kinds += [("target", i) for i in (0, 1, 3)]
    main = len(kinds)
    kinds += [("target", 2), ("small", 1)]
    late = [main + 1, main]

    def piece(c, lane, sel):
        kind, index = kinds[c]
        if kind == "small":
            return small.at[
                pl.ds(2 * index, 2), sel[0], sel[1], sel[2], :, pl.ds(lane * half, half)
            ]
        buffer = up if kind == "up" else tup
        return buffer.at[sel[0], sel[1], sel[2], :, pl.ds(index * chunk + lane * TILE, TILE)]

    def gather_copy(c, lane, ref, sem, target):
        return pltpu.make_async_remote_copy(
            src_ref=ref,
            dst_ref=ref,
            send_sem=ag_s.at[c, lane, sem],
            recv_sem=ag_r.at[c, lane, sem],
            device_id=place(target),
            device_id_type=MESH,
        )

    def inside_line(index):
        return jnp.logical_and(index >= 0, index < n0)

    def line_each(c, lane, hop, way, act):
        sel = [None, slice(None), slice(None)] if c in late else [None, me[1], me[2]]
        for bit, turn in enumerate((1, -1)):
            block = me[0] - turn * (hop if way == "send" else hop + 1)
            fits = inside_line(block)
            if way == "send":
                fits = jnp.logical_and(fits, inside_line(me[0] + turn))

            @pl.when(fits)
            def _(bit=bit, turn=turn, block=block):
                ref = piece(c, lane, [block] + sel[1:])
                target = (me[0] + (turn if way == "send" else -turn), me[1], me[2])
                act(gather_copy(c, lane, ref, 2 * hop + bit, target))

    def line_hop(c, lane, hop):
        if hop:
            line_each(c, lane, hop - 1, "recv", lambda copy: copy.wait_recv())
        line_each(c, lane, hop, "send", lambda copy: copy.start())

    def side_copy(c, lane, phase):
        axis, second = ((2, 1), (1, 2))[lane]
        sel = [me[0] if c in late else slice(None), me[1], me[2]]
        if phase:
            sel[axis] = slice(None)
        return gather_copy(
            c, lane, piece(c, lane, sel), 2 * hops + phase, moved((axis, second)[phase], 1)
        )

    def gather_line(c, hop):
        for lane in range(2):
            line_hop(c, lane, hop)

    def gather_side(c, phase):
        for lane in range(2):
            if phase:
                side_copy(c, lane, 0).wait_recv()
            elif c not in late:
                line_each(c, lane, hops - 1, "recv", lambda copy: copy.wait_recv())
            side_copy(c, lane, phase).start()

    def gather_end(c):
        for lane in range(2):
            if c in late:
                line_each(c, lane, hops - 1, "recv", lambda copy: copy.wait_recv())
            else:
                side_copy(c, lane, 1).wait_recv()

    late_items = [(c, lane, hop) for hop in range(hops) for c in late for lane in range(2)]

    def late_next():
        if late_items:
            c, lane, hop = late_items.pop(0)
            if hop == 0:
                side_copy(c, lane, 1).wait_recv()
            line_hop(c, lane, hop)

    def gather_sent():
        for c in range(len(kinds)):
            for lane in range(2):
                for hop in range(hops):
                    line_each(c, lane, hop, "send", lambda copy: copy.wait_send())
                for phase in range(2):
                    side_copy(c, lane, phase).wait_send()

    def sum_copies(buffers, i, stage):
        first, second, send, recv = buffers
        if stage == 0:
            ref = first.at[i, mp]
            return [
                pltpu.make_async_remote_copy(
                    src_ref=ref,
                    dst_ref=ref,
                    send_sem=send.at[i, k - 1],
                    recv_sem=recv.at[i, k - 1],
                    device_id=(me[0] * plane + (mp + k) % plane, core),
                    device_id_type=MESH,
                )
                for k in range(1, plane)
            ]
        ref = second.at[i, me[0]]
        return [
            pltpu.make_async_remote_copy(
                src_ref=ref,
                dst_ref=ref,
                send_sem=send.at[i, plane - 1 + k - 1],
                recv_sem=recv.at[i, plane - 1 + k - 1],
                device_id=place(moved(0, k)),
                device_id_type=MESH,
            )
            for k in range(1, n0)
        ]

    narrow_sum = (pa, pb, ps_s, ps_r)
    half_sum = (qa, qb, qs_s, qs_r)
    scalar_sum = (ta, tb, ts_s, ts_r)

    def sum_start(buffers, i):
        for copy in sum_copies(buffers, i, 0):
            copy.start()

    def sum_middle(buffers, i):
        for copy in sum_copies(buffers, i, 0):
            copy.wait()
        first, second = buffers[:2]
        total = first[i, 0]
        for j in range(1, plane):
            total = total + first[i, j]
        second[i, me[0]] = total
        for copy in sum_copies(buffers, i, 1):
            copy.start()

    def sum_end(buffers, i):
        for copy in sum_copies(buffers, i, 1):
            copy.wait()
        second = buffers[1]
        total = second[i, 0]
        for j in range(1, n0):
            total = total + second[i, j]
        return total

    def swap(i):
        return pltpu.make_async_remote_copy(
            src_ref=ex.at[i],
            dst_ref=exr.at[i % 2],
            send_sem=ex_s.at[i],
            recv_sem=ex_r.at[i],
            device_id=other,
            device_id_type=MESH,
        )

    def swap_end(i):
        swap(i).wait()

        def add(b):
            part = pl.ds(pl.multiple_of(b * rows, rows), rows)
            ex[i, part, :] = (
                ex[i, part, :].astype(jnp.float32) + exr[i % 2, part, :].astype(jnp.float32)
            ).astype(jnp.bfloat16)

        loop(blocks, add)

    def weight(w, columns):
        return small[w, :, :, :, :, columns].reshape(plane * n0 * small_rows, columns.size)

    def columns_at(start, size):
        return pl.ds(pl.multiple_of(start, TILE), size)

    def hidden_chunk(weights, i, slot):
        def one(lane):
            columns = columns_at(i * chunk + lane * TILE, TILE)
            matrix = weights[:, :, :, :, columns].reshape(n0 * plane * rows, TILE)
            values = jnp.dot(feats[...], matrix, preferred_element_type=jnp.float32)
            wide[:, columns] = values
            spot = columns_at(lane * TILE, TILE)
            pa[slot, mp, 0:1, spot] = jnp.sum(values, 0, keepdims=True)
            pa[slot, mp, 1:2, spot] = jnp.sum(values * values, 0, keepdims=True)

        loop(2, one)

    def spread(total):
        mean = total[0:1] / total_views
        return mean, lax.rsqrt(total[1:2] / total_views - mean * mean + NORM_EPS)

    def act_tile(start, mean, inverse, norm, act_ref, hat_ref, act_start):
        columns = pl.ds(start, TILE)
        targets = pl.ds(act_start, TILE)
        gain, shift = norm[0:1, columns], norm[1:2, columns]

        def one(b):
            part = pl.ds(pl.multiple_of(b * rows, rows), rows)
            hat = (wide[part, columns] - mean) * inverse
            value = hat * gain + shift
            gate, square = gelu_parts(value)
            act_ref[b // 2, b % 2, :, targets] = (value * gate).astype(jnp.bfloat16)
            if hat_ref is not None:
                hat_ref[b // 2, b % 2, :, targets] = hat.astype(jnp.bfloat16)
                slope1[b // 2, b % 2, :, targets] = gelu_slope(value, gate, square).astype(
                    jnp.bfloat16
                )

        loop(blocks, one)

    def act_online(i):
        mean, inverse = spread(sum_end(narrow_sum, i))
        inv1[:, pl.ds(i * chunk, chunk)] = inverse
        for n in range(chunk // TILE):
            start = i * chunk + n * TILE
            here = slice(n * TILE, (n + 1) * TILE)
            act_tile(start, mean[:, here], inverse[:, here], proj_norm, act1, hat1, start)

    def act_target(i):
        mean, inverse = spread(sum_end(narrow_sum, 4 + i))
        for n in range(chunk // TILE):
            start = i * chunk + n * TILE
            here = slice(n * TILE, (n + 1) * TILE)
            act_tile(start, mean[:, here], inverse[:, here], target_norm, tact, None, 0)
            product = nt_dot(tact[...].reshape(views, TILE), weight(3, pl.ds(start, TILE)))
            if start == 0:
                acc[...] = product
            else:
                acc[...] += product

    count = []

    def sum_rows(i, columns, first_row, second_row):
        qa[i, mp, 0:1, columns] = first_row
        qa[i, mp, 1:2, columns] = second_row

    def online_middle():
        ex[0] = nt_dot(act1[...].reshape(views, width), weight(0, pl.ds(0, width))).astype(
            jnp.bfloat16
        )
        swap(0).start()
        swap_end(0)
        for side in range(2):

            def one(n):
                columns = columns_at(side * half + n * TILE, TILE)
                values = jnp.dot(ex[0], weight(1, columns), preferred_element_type=jnp.float32)
                sum_rows(
                    side,
                    columns_at(n * TILE, TILE),
                    jnp.sum(values, 0, keepdims=True),
                    jnp.sum(values * values, 0, keepdims=True),
                )

            loop(half // TILE, one)
            sum_start(half_sum, side)

    def online_query():
        for side in range(2):
            mean, inverse = spread(sum_end(half_sum, side))
            inv2[:, pl.ds(side * half, half)] = inverse
            means[:, pl.ds(side * half, half)] = mean
        spare = pl.ds(3 * chunk, TILE)

        def one(n):
            columns = columns_at(n * TILE, TILE)
            wide[:, spare] = jnp.dot(
                ex[0], weight(1, columns), preferred_element_type=jnp.float32
            )
            mean_n, inverse_n = means[:, columns], inv2[:, columns]
            gain, shift = pred_norm[0:1, columns], pred_norm[1:2, columns]

            def tile(b):
                part = pl.ds(pl.multiple_of(b * rows, rows), rows)
                hat = (wide[part, spare] - mean_n) * inverse_n
                value = hat * gain + shift
                gate, _ = gelu_parts(value)
                act2[b // 2, b % 2, :, columns] = (value * gate).astype(jnp.bfloat16)
                hat2[b // 2, b % 2, :, columns] = hat.astype(jnp.bfloat16)

            loop(blocks, tile)

        loop(width // TILE, one)
        ex[1] = nt_dot(
            act2[...].reshape(views, width), weight(2, pl.ds(0, width))
        ).astype(jnp.bfloat16)
        swap(1).start()

    def forward(tick):
        gather_side(tick, 0)
        for ahead, hop in ((1, 2), (2, 1), (3, 0)):
            if tick + ahead < main:
                gather_line(tick + ahead, hop)
        if tick >= 1:
            for _ in range(LATE_PER_TICK):
                late_next()
            gather_side(tick - 1, 1)

    def hidden(slot):
        hidden_chunk(up if slot < 4 else tup, slot % 4, slot)
        sum_start(narrow_sum, slot)

    def after(tick):
        if tick == 2:
            loads[6].wait()
            kept = jnp.sum(jnp.sum(keep[...], 0, keepdims=True), 1, keepdims=True)
            ta[0, mp] = jnp.broadcast_to(kept, (8, 128))
            sum_start(scalar_sum, 0)
        if tick <= 5:
            hidden(tick - 2)
        if tick == 4:
            sum_middle(scalar_sum, 0)
        if 3 <= tick <= 6:
            sum_middle(narrow_sum, tick - 3)
        if tick >= 4:
            act_online(tick - 4)
        if tick == 6:
            count.append(sum_end(scalar_sum, 0))

    gather_line(0, 0)
    take_small()
    gather_side(late[0], 0)
    take(loads[5], tup, rows)
    gather_side(late[1], 0)
    gather_line(1, 0)
    gather_line(0, 1)
    gather_line(2, 0)
    gather_line(1, 1)
    gather_line(0, 2)
    for c in late:
        gather_side(c, 1)
    for tick in range(main - 1):
        forward(tick)
        if tick >= 2:
            gather_end(tick - 2)
            after(tick)
    forward(main - 1)
    after(main - 1)
    online_middle()
    gather_side(main - 1, 1)
    gather_end(main - 3)
    hidden(4)
    gather_end(main)
    hidden(6)
    sum_middle(half_sum, 0)
    sum_middle(half_sum, 1)
    sum_middle(narrow_sum, 4)
    gather_end(main - 2)
    hidden(5)
    gather_end(main + 1)
    online_query()
    act_target(0)
    sum_middle(narrow_sum, 6)
    sum_middle(narrow_sum, 5)
    gather_end(main - 1)
    hidden(7)
    swap_end(1)
    act_target(1)
    act_target(2)
    sum_middle(narrow_sum, 7)
    act_target(3)
    ex[2] = acc[...].astype(jnp.bfloat16)
    swap(2).start()
    gather_sent()
    swap(2).wait()

    scale = -2.0 / count[0][0:1, 0:1]

    def unit_scale(values):
        return lax.rsqrt(jnp.sum(values * values, 1, keepdims=True) + UNIT_EPS)

    even = (lax.broadcasted_iota(jnp.int32, (rows, acc.shape[1]), 0) % 2) == 0

    spot = lax.broadcasted_iota(jnp.int32, (rows, blocks), 1)

    def loss_tile(b, carry):
        part = pl.ds(pl.multiple_of(b * rows, rows), rows)
        query = ex[1, part, :].astype(jnp.float32)
        target = ex[2, part, :].astype(jnp.float32) + exr[0, part, :].astype(jnp.float32)
        target = target * unit_scale(target)
        goal = jnp.where(even, pltpu.roll(target, rows - 1, 0), pltpu.roll(target, 1, 0))
        back = unit_scale(query)
        unit = query * back
        cosine = jnp.sum(unit * goal, 1, keepdims=True)
        kept = jnp.sum(jnp.where(spot == b, keep[...], 0.0), 1, keepdims=True)
        ex[1, part, :] = ((scale * kept * back) * (goal - cosine * unit)).astype(jnp.bfloat16)
        return carry + kept * (2.0 - 2.0 * cosine)

    loss_rows = lax.fori_loop(0, blocks, loss_tile, jnp.zeros((rows, 1), jnp.float32))
    ta[1, mp] = jnp.broadcast_to(jnp.sum(loss_rows, 0, keepdims=True), (8, 128))
    sum_start(scalar_sum, 1)

    def back_norm(i, first, last, w, grads, hat_ref, norm, slope_ref):
        def one(n):
            columns = columns_at(n * TILE, TILE)
            wide[:, columns] = jnp.dot(
                ex[grads], weight(w, columns), preferred_element_type=jnp.float32
            )
            gain, shift = norm[0:1, columns], norm[1:2, columns]

            def tile(b, carry):
                part = pl.ds(pl.multiple_of(b * rows, rows), rows)
                hat = hat_ref[b // 2, b % 2, :, columns].astype(jnp.float32)
                if slope_ref is None:
                    value = hat * gain + shift
                    slope = gelu_slope(value, *gelu_parts(value))
                else:
                    slope = slope_ref[b // 2, b % 2, :, columns].astype(jnp.float32)
                grad = wide[part, columns] * slope
                wide[part, columns] = grad
                cross = grad * hat
                return (
                    carry[0] + jnp.sum(grad.reshape(rows // 8, 8, TILE), 0),
                    carry[1] + jnp.sum(cross.reshape(rows // 8, 8, TILE), 0),
                )

            zero = jnp.zeros((8, TILE), jnp.float32)
            sums = lax.fori_loop(0, blocks, tile, (zero, zero))
            sum_rows(
                i,
                columns_at((n % side_tiles) * TILE, TILE),
                jnp.sum(sums[0], 0, keepdims=True),
                jnp.sum(sums[1], 0, keepdims=True),
            )

        loop(last - first, lambda n: one(first + n))

    side_tiles = half // TILE

    def grad_hidden(stat, hat_ref, norm, inv_ref, columns):
        gain = norm[0:1, columns] * inv_ref[:, columns]
        shift = stat[0:1, columns] / total_views
        slope = stat[1:2, columns] / total_views

        def tile(b):
            part = pl.ds(pl.multiple_of(b * rows, rows), rows)
            hat = hat_ref[b // 2, b % 2, :, columns].astype(jnp.float32)
            hat_ref[b // 2, b % 2, :, columns] = (
                gain * (wide[part, columns] - shift - hat * slope)
            ).astype(jnp.bfloat16)

        loop(blocks, tile)

    def small_grad(w, grads, act_ref):
        def one(n):
            columns = columns_at(n * TILE, TILE)
            right = act_ref[:, :, :, columns].reshape(views, TILE)
            value = tn_dot(ex[grads], right).astype(jnp.bfloat16)
            small[w, :, :, :, :, columns] = value.reshape(n0, n1, n2, small_rows, TILE)

        loop(width // TILE, one)

    def plus(*terms):
        total = terms[0].astype(jnp.float32)
        for term in terms[1:]:
            total = total + term.astype(jnp.float32)
        return total

    def low_plus(*terms):
        return plus(*terms).astype(jnp.bfloat16)

    up_parts = [("line", 0, TILE // 2)]
    up_parts += [("side", TILE + g * chunk, TILE) for g in range(3)]
    up_parts += [("side", TILE + 3 * chunk, TILE // 2)]

    def reduce_copies(kind, g, lane, phase):
        axis, second = ((1, 2), (2, 1))[lane]
        style = up_parts[g][0] if kind == "up" else "side"
        order = (0, axis, second) if style == "line" else (axis, second, 0)
        sems = ((0, 3, 4) if style == "line" else (0, 1, 2))[phase]
        send, recv = (rs_s, rs_r) if kind == "up" else (ss_s, ss_r)
        axis_now = order[phase]
        copies = []
        for k in range(1, grid[axis_now]):
            target = moved(axis_now, k)
            sel = [slice(None)] * 3
            for done in order[:phase]:
                sel[done] = me[done]
            sel[axis_now] = target[axis_now]
            if kind == "small":
                columns = pl.ds(lane * half, half)
                source = small.at[3 - g, sel[0], sel[1], sel[2], :, columns]
                if phase == 0:
                    land = sr1.at[g, :, :, :, columns]
                elif phase == 1:
                    land = sr2.at[g, :, :, columns]
                else:
                    land = sr3.at[g, me[0], :, columns]
            else:
                _, start, size = up_parts[g]
                columns = pl.ds(start + lane * size, size)
                source = tup.at[sel[0], sel[1], sel[2], :, columns]
                if style == "line":
                    if phase == 0:
                        land = (act2 if k < 3 else hat2).at[
                            pl.ds(2 * ((k - 1) % 2), 2), :, :, columns
                        ]
                    elif phase == 1:
                        land = hat2.at[2, :, :, columns]
                    else:
                        land = hat2.at[3, 0, :, columns]
                elif phase == 0:
                    land = act2.at[:, :, :, columns]
                elif phase == 1:
                    land = hat2.at[:, 0, :, columns]
                else:
                    land = hat2.at[me[0], 1, :, columns]
            copies.append(
                pltpu.make_async_remote_copy(
                    src_ref=source,
                    dst_ref=land,
                    send_sem=send.at[g, lane, sems + k - 1],
                    recv_sem=recv.at[g, lane, sems + k - 1],
                    device_id=place(target),
                    device_id_type=MESH,
                )
            )
        return copies

    def reduce_step(kind, g, phase):
        for lane in range(2):
            if phase:
                for copy in reduce_copies(kind, g, lane, phase - 1):
                    copy.wait()
                if kind == "small":
                    small_add(g, lane, phase)
                elif up_parts[g][0] == "line":
                    line_add(g, lane, phase)
                else:
                    side_add(g, lane, phase)
            if phase < 3:
                for copy in reduce_copies(kind, g, lane, phase):
                    copy.start()

    def plane_spot(lane, i):
        return (me[1], i) if lane == 0 else (i, me[2])

    def small_add(g, lane, phase):
        columns = pl.ds(lane * half, half)
        w = 3 - g
        if phase == 1:

            def add(j):
                z, i = j // 2, j % 2
                y, x = plane_spot(lane, i)
                small[w, z, y, x, :, columns] = low_plus(
                    small[w, z, y, x, :, columns], sr1[g, z, i, :, columns]
                )

            loop(n0 * 2, add)
        elif phase == 2:

            def add(z):
                small[w, z, me[1], me[2], :, columns] = low_plus(
                    small[w, z, me[1], me[2], :, columns], sr2[g, z, :, columns]
                )

            loop(n0, add)
        else:
            (qd_out, qu_out, pd_out)[g][:, columns] = low_plus(
                small[w, me[0], me[1], me[2], :, columns],
                *[sr3[g, (me[0] + k) % n0, :, columns] for k in range(1, n0)],
            )

    def side_add(g, lane, phase):
        _, start, size = up_parts[g]
        columns = pl.ds(start + lane * size, size)
        if phase == 1:

            def add(j):
                z, i = j // 2, j % 2
                y, x = plane_spot(lane, i)
                tup[z, y, x, :, columns] = low_plus(
                    tup[z, y, x, :, columns], act2[z, i, :, columns]
                )

            loop(n0 * 2, add)
        elif phase == 2:

            def add(z):
                tup[z, me[1], me[2], :, columns] = low_plus(
                    tup[z, me[1], me[2], :, columns], hat2[z, 0, :, columns]
                )

            loop(n0, add)
        else:
            gu_out[:, columns] = low_plus(
                tup[me[0], me[1], me[2], :, columns],
                *[hat2[(me[0] + k) % n0, 1, :, columns] for k in range(1, n0)],
            )

    def line_add(g, lane, phase):
        _, start, size = up_parts[g]
        columns = pl.ds(start + lane * size, size)
        z = me[0]
        if phase == 1:

            def add(j):
                y, x = j // 2, j % 2
                tup[z, y, x, :, columns] = low_plus(
                    tup[z, y, x, :, columns],
                    act2[y, x, :, columns],
                    act2[2 + y, x, :, columns],
                    hat2[y, x, :, columns],
                )

            loop(plane, add)
        elif phase == 2:

            def add(i):
                y, x = plane_spot(lane, i)
                tup[z, y, x, :, columns] = low_plus(
                    tup[z, y, x, :, columns], hat2[2, i, :, columns]
                )

            loop(2, add)
        else:
            gu_out[:, columns] = low_plus(
                tup[z, me[1], me[2], :, columns], hat2[3, 0, :, columns]
            )

    def pred_half(side):
        pred_stat[:, pl.ds(side * half, half)] = sum_end(half_sum, 2 + side)

        def one(n):
            columns = columns_at(side * half + n * TILE, TILE)
            grad_hidden(pred_stat, hat2, pred_norm, inv2, columns)

        loop(side_tiles, one)
        columns = pl.ds(side * half, half)
        product = nt_dot(hat2[:, :, :, columns].reshape(views, half), weight(1, columns))
        if side == 0:
            acc[...] = product
        else:
            acc[...] += product

    middle_tile = side_tiles + side_tiles // 2
    pred_args = (2, 1, hat2, pred_norm, None)
    back_norm(2, 0, side_tiles, *pred_args)
    sum_start(half_sum, 2)
    back_norm(3, side_tiles, middle_tile, *pred_args)
    sum_middle(half_sum, 2)
    back_norm(3, middle_tile, 2 * side_tiles, *pred_args)
    sum_start(half_sum, 3)
    small_grad(3, 1, act2)
    sum_middle(half_sum, 3)
    reduce_step("small", 0, 0)
    pred_half(0)
    pred_half(1)
    ex[3] = acc[...].astype(jnp.bfloat16)
    swap(3).start()
    small_grad(2, 0, hat2)
    reduce_step("small", 1, 0)
    reduce_step("small", 0, 1)
    swap_end(3)
    proj_args = (0, 3, hat1, proj_norm, slope1)
    back_norm(4, 0, side_tiles, *proj_args)
    sum_start(half_sum, 4)
    back_norm(5, side_tiles, middle_tile, *proj_args)
    sum_middle(half_sum, 4)
    reduce_step("small", 1, 1)
    reduce_step("small", 0, 2)
    back_norm(5, middle_tile, 2 * side_tiles, *proj_args)
    sum_start(half_sum, 5)
    small_grad(1, 3, act1)
    pl.semaphore_signal(ready, inc=1, device_id=other, device_id_type=MESH)
    sum_middle(half_sum, 5)
    sum_middle(scalar_sum, 1)
    proj_stat[:, pl.ds(0, half)] = sum_end(half_sum, 4)

    def up_hidden(g):
        _, start, size = up_parts[g]
        for n in range(2 * size // TILE):
            grad_hidden(proj_stat, hat1, proj_norm, inv1, pl.ds(start + n * TILE, TILE))

    def up_grad(g):
        _, start, size = up_parts[g]
        columns = pl.ds(start, 2 * size)

        def one(z):
            left = feats[:, columns_at(z * plane * rows, plane * rows)]
            value = tn_dot(left, hat1[:, :, :, columns].reshape(views, 2 * size))
            tup[z, :, :, :, columns] = value.astype(jnp.bfloat16).reshape(n1, n2, rows, 2 * size)

        loop(n0, one)
        reduce_step("up", g, 0)

    parts = ig_s.shape[0]

    def input_copy(q):
        return pltpu.make_async_remote_copy(
            src_ref=act1.at[:, :, :, pl.ds(q * TILE, TILE)],
            dst_ref=act1.at[:, :, :, pl.ds((parts + q) * TILE, TILE)],
            send_sem=ig_s.at[q],
            recv_sem=ig_r.at[q],
            device_id=other,
            device_id_type=MESH,
        )

    def input_product(q, side):
        first = side * (n0 // 2) + q // n1
        matrix = up[first, q % n1].reshape(n2 * rows, width)
        return nt_dot(hat1[...].reshape(views, width), matrix)

    def send_part(q):
        act1[:, :, :, pl.ds(q * TILE, TILE)] = (
            input_product(q, 1 - core).astype(jnp.bfloat16).reshape(n0, 2, rows, TILE)
        )
        input_copy(q).start()

    def own_part(q):
        wide[:, pl.ds(q * TILE, TILE)] = input_product(q, core)

    up_hidden(0)
    up_grad(0)
    reduce_step("small", 2, 0)
    up_hidden(1)
    up_grad(1)
    proj_stat[:, pl.ds(half, half)] = sum_end(half_sum, 5)
    for g in (2, 3, 4):
        up_hidden(g)
    up_grad(2)
    reduce_step("small", 1, 2)
    reduce_step("small", 0, 3)
    pl.semaphore_wait(ready, 1)
    send_part(0)
    reduce_step("up", 1, 1)
    up_grad(3)
    reduce_step("small", 2, 1)
    send_part(1)
    send_part(2)
    reduce_step("up", 0, 1)
    reduce_step("up", 2, 1)
    up_grad(4)
    reduce_step("up", 1, 2)
    reduce_step("small", 2, 2)
    reduce_step("small", 1, 3)
    send_part(3)
    own_part(0)
    reduce_step("up", 0, 2)
    reduce_step("up", 3, 1)
    reduce_step("up", 2, 2)
    own_part(1)
    own_part(2)
    reduce_step("up", 4, 1)
    reduce_step("up", 3, 2)
    own_part(3)
    for q in range(parts):
        input_copy(q).wait()

        def add(b, q=q):
            part = pl.ds(pl.multiple_of(b * rows, rows), rows)
            theirs = act1[b // 2, b % 2, :, pl.ds((parts + q) * TILE, TILE)]
            act1[b // 2, b % 2, :, pl.ds(q * TILE, TILE)] = low_plus(
                wide[part, pl.ds(q * TILE, TILE)], theirs
            )

        loop(blocks, add)
    out_copy = pltpu.make_async_copy(
        act1.at[:, :, :, pl.ds(0, parts * TILE)], ig_hbm, load_sem.at[0]
    )
    out_copy.start()
    reduce_step("up", 4, 2)
    reduce_step("small", 2, 3)
    loss_out[...] = sum_end(scalar_sum, 1) / count[0]
    for g in range(5):
        reduce_step("up", g, 3)
    out_copy.wait()


def kernel_step(grid, total_views, features, keep, ups, downs, norms):
    n0, n1, n2 = grid
    plane = n1 * n2
    views, depth = features.shape
    rows, width = ups[0].shape
    small_rows = downs[0].shape[0]
    out = small_rows * n0 * plane
    parts = depth // 2 // TILE
    low, full = jnp.bfloat16, jnp.float32
    vm = pltpu.VMEM
    dma = pltpu.SemaphoreType.DMA
    anywhere = pl.BlockSpec(memory_space=pl.ANY)
    inside = pl.BlockSpec(memory_space=pltpu.VMEM)
    spread_shape = (n0, 2, rows, width)
    moves = 2 * (n0 - 1) + 2
    sum_moves = plane - 1 + n0 - 1
    return pl.pallas_call(
        functools.partial(step_kernel, grid, total_views),
        out_shape=(
            jax.ShapeDtypeStruct((n0, 2, rows, depth // 2), low),
            jax.ShapeDtypeStruct((rows, width), low),
            jax.ShapeDtypeStruct((small_rows, width), low),
            jax.ShapeDtypeStruct((small_rows, width), low),
            jax.ShapeDtypeStruct((small_rows, width), low),
            jax.ShapeDtypeStruct((2, width), full),
            jax.ShapeDtypeStruct((2, width), full),
            jax.ShapeDtypeStruct((8, 128), full),
        ),
        in_specs=[anywhere] * 7 + [inside] * 4,
        out_specs=(anywhere,) + (inside,) * 7,
        scratch_shapes=[
            vm((views, depth), low),
            vm((n0, n1, n2, rows, width), low),
            vm((n0, n1, n2, rows, width), low),
            vm((4, n0, n1, n2, small_rows, width), low),
            vm(spread_shape, low),
            vm(spread_shape, low),
            vm(spread_shape, low),
            vm(spread_shape, low),
            vm((views, width), full),
            vm((n0, 2, rows, TILE), low),
            vm((views, out), full),
            vm((4, views, out), low),
            vm((2, views, out), low),
            vm(spread_shape, low),
            vm((3, n0, 2, small_rows, width), low),
            vm((3, n0, small_rows, width), low),
            vm((3, n0, small_rows, width), low),
            vm((1, width), full),
            vm((1, width), full),
            vm((1, width), full),
            vm((8, plane, 2, width // 4), full),
            vm((8, n0, 2, width // 4), full),
            vm((6, plane, 2, width // 2), full),
            vm((6, n0, 2, width // 2), full),
            vm((2, plane, 8, 128), full),
            vm((2, n0, 8, 128), full),
            dma((7,)),
            dma((10, 2, moves)),
            dma((10, 2, moves)),
            dma((8, sum_moves)),
            dma((8, sum_moves)),
            dma((6, sum_moves)),
            dma((6, sum_moves)),
            dma((2, sum_moves)),
            dma((2, sum_moves)),
            dma((4,)),
            dma((4,)),
            dma((5, 2, n0 + 1)),
            dma((5, 2, n0 + 1)),
            dma((3, 2, n0 + 1)),
            dma((3, 2, n0 + 1)),
            dma((parts,)),
            dma((parts,)),
            pltpu.SemaphoreType.REGULAR,
        ],
        compiler_params=pltpu.CompilerParams(
            collective_id=0, has_side_effects=True, vmem_limit_bytes=VMEM_LIMIT
        ),
    )(features, *ups, *downs, *norms, keep)


def step_body(grid, *args):
    (
        features,
        keep_mask,
        proj_up,
        proj_down,
        proj_norm,
        pred_up,
        pred_down,
        pred_norm,
        moment_proj_up,
        moment_proj_down,
        moment_proj_norm,
        moment_pred_up,
        moment_pred_down,
        moment_pred_norm,
        target_up,
        target_down,
        target_norm,
    ) = args
    if grid is None:
        return plain_body(*args)
    total_views = float(features.shape[0] * lax.axis_size("dp"))
    (input_grad, *shards, proj_stat, pred_stat, loss) = kernel_step(
        grid,
        total_views,
        features,
        keep_mask.astype(jnp.float32).reshape(-1, proj_up.shape[0]).T,
        (proj_up, target_up),
        (proj_down, pred_up, pred_down, target_down),
        (proj_norm, pred_norm, target_norm),
    )
    shard_proj_up, shard_pred_down, shard_pred_up, shard_proj_down = (
        shard.astype(jnp.float32) for shard in shards
    )
    input_grad = input_grad.astype(jnp.float32).reshape(features.shape[0], -1)
    grad_proj_norm = proj_stat[::-1]
    grad_pred_norm = pred_stat[::-1]
    return finish(
        total_views,
        args,
        loss[0, 0],
        input_grad,
        shard_proj_up,
        shard_proj_down,
        grad_proj_norm,
        shard_pred_up,
        shard_pred_down,
        grad_pred_norm,
    )


def solution(mesh):
    placed = (
        P("dp", None),
        P("dp"),
        P("dp", "tensor"),
        P("dp", "tensor"),
        P(None, "tensor"),
        P("dp", "tensor"),
        P("dp", "tensor"),
        P(None, "tensor"),
        P("dp", "tensor"),
        P("dp", "tensor"),
        P(None, "tensor"),
        P("dp", "tensor"),
        P("dp", "tensor"),
        P(None, "tensor"),
        P("dp", "tensor"),
        P("dp", "tensor"),
        P(None, "tensor"),
    )
    return jax.shard_map(
        functools.partial(step_body, GRIDS.get(mesh.shape["dp"])),
        mesh=mesh,
        in_specs=placed,
        out_specs=(
            P(),
            P("dp", "tensor"),
            P("dp", "tensor"),
            P("dp", "tensor"),
            P("dp", "tensor"),
            P("dp", "tensor"),
            P("dp", "tensor"),
            P("dp", "tensor"),
            P(None, "tensor"),
            P(None, "tensor"),
            P(None, "tensor"),
            P("dp", "tensor"),
            P("dp", "tensor"),
            P("dp", "tensor"),
            P("dp", "tensor"),
            P("dp", "tensor"),
            P("dp", "tensor"),
            P(None, "tensor"),
            P(None, "tensor"),
            P(None, "tensor"),
            P("dp", "tensor"),
            P("dp", "tensor"),
            P(None, "tensor"),
        ),
        check_vma=False,
    )
```

```python
import functools
import math

import jax
import jax.numpy as jnp
from jax import lax
from jax.experimental import pallas as pl
from jax.experimental.pallas import tpu as pltpu
from jax.sharding import PartitionSpec as P

NORM_EPS = 1e-05
UNIT_EPS = 1e-06
RATE_PROJ_UP = 9.0
RATE_PROJ_DOWN = 1.2
RATE_PROJ_NORM = 40.0
RATE_PRED_UP = 18.0
RATE_PRED_DOWN = 0.9
RATE_PRED_NORM = 30.0


def across(matrix, weight):
    return lax.dot_general(
        matrix, weight, (((1,), (1,)), ((), ())), preferred_element_type=jnp.float32
    )


def outer_sum(first_op, second_op):
    return lax.dot_general(
        first_op, second_op, (((0,), (0,)), ((), ())), preferred_element_type=jnp.float32
    )


def standard(hidden, col_sum, col_square, total_views):
    middle_mean = col_sum / total_views
    inverse = lax.rsqrt(col_square / total_views - middle_mean * middle_mean + NORM_EPS)
    return ((hidden - middle_mean) * inverse, inverse)


def norm_back(grad_out, scaled, inverse, params, sum_grad, sum_cross, total_views):
    return (
        params[0]
        * inverse
        * (grad_out - sum_grad / total_views - scaled * (sum_cross / total_views))
    )


def unit_rows(values):
    return values * lax.rsqrt(jnp.sum(values * values, 1, keepdims=True) + UNIT_EPS)


def partner(values):
    width = values.shape[1]
    return values.reshape(-1, 2, width)[:, ::-1, :].reshape(-1, width)


def nesterov(weight, moment, grad, rate):
    fresh = 0.5 * moment + grad
    return (fresh, weight - rate * (grad + 0.5 * fresh))


def finish(
    total_views,
    args,
    loss,
    input_grad,
    shard_proj_up,
    shard_proj_down,
    grad_proj_norm,
    shard_pred_up,
    shard_pred_down,
    grad_pred_norm,
):
    (proj_up, proj_down, proj_norm, pred_up, pred_down, pred_norm) = args[2:8]
    (
        moment_proj_up,
        moment_proj_down,
        moment_proj_norm,
        moment_pred_up,
        moment_pred_down,
        moment_pred_norm,
        target_up,
        target_down,
        target_norm,
    ) = args[8:]
    scale = math.sqrt(total_views)
    mom_pu, next_pu = nesterov(proj_up, moment_proj_up, shard_proj_up, RATE_PROJ_UP * scale)
    mom_pd, next_pd = nesterov(proj_down, moment_proj_down, shard_proj_down, RATE_PROJ_DOWN * scale)
    mom_pn, next_pn = nesterov(proj_norm, moment_proj_norm, grad_proj_norm, RATE_PROJ_NORM * scale)
    mom_qu, next_qu = nesterov(pred_up, moment_pred_up, shard_pred_up, RATE_PRED_UP * scale)
    mom_qd, next_qd = nesterov(pred_down, moment_pred_down, shard_pred_down, RATE_PRED_DOWN * scale)
    mom_qn, next_qn = nesterov(pred_norm, moment_pred_norm, grad_pred_norm, RATE_PRED_NORM * scale)
    target_up_next = 0.5 * target_up + 0.5 * next_pu
    target_down_next = 0.5 * target_down + 0.5 * next_pd
    target_norm_next = 0.5 * target_norm + 0.5 * next_pn
    return (
        loss,
        input_grad,
        shard_proj_up,
        mom_pu,
        next_pu,
        shard_proj_down,
        mom_pd,
        next_pd,
        grad_proj_norm,
        mom_pn,
        next_pn,
        shard_pred_up,
        mom_qu,
        next_qu,
        shard_pred_down,
        mom_qd,
        next_qd,
        grad_pred_norm,
        mom_qn,
        next_qn,
        target_up_next,
        target_down_next,
        target_norm_next,
    )


def plain_body(
    features,
    keep_mask,
    proj_up,
    proj_down,
    proj_norm,
    pred_up,
    pred_down,
    pred_norm,
    moment_proj_up,
    moment_proj_down,
    moment_proj_norm,
    moment_pred_up,
    moment_pred_down,
    moment_pred_norm,
    target_up,
    target_down,
    target_norm,
):
    total_views = float(features.shape[0] * lax.axis_size("dp"))
    width = proj_up.shape[1]

    def gathered(parts):
        low = jnp.stack([part.astype(jnp.bfloat16) for part in parts])
        full = lax.all_gather(low, "dp", axis=1, tiled=True)
        return tuple(full[i] for i in range(len(parts)))

    (up_full, tup_full) = gathered((proj_up, target_up))
    (down_full, pup_full, pdown_full, tdown_full) = gathered(
        (proj_down, pred_up, pred_down, target_down)
    )
    keep_float = keep_mask.astype(jnp.float32)
    hidden1 = jnp.dot(features, up_full, preferred_element_type=jnp.float32)
    target_hidden = jnp.dot(features, tup_full, preferred_element_type=jnp.float32)
    sums = lax.psum(
        jnp.stack(
            [
                jnp.sum(hidden1, 0),
                jnp.sum(hidden1 * hidden1, 0),
                jnp.sum(target_hidden, 0),
                jnp.sum(target_hidden * target_hidden, 0),
                jnp.full((width,), jnp.sum(keep_float)),
            ]
        ),
        "dp",
    )
    sum_one, square_one, sum_target, square_target = sums[0], sums[1], sums[2], sums[3]
    count = sums[4, 0]
    scaled1, inverse1 = standard(hidden1, sum_one, square_one, total_views)
    action1, gelu_back1 = jax.vjp(jax.nn.gelu, scaled1 * proj_norm[0] + proj_norm[1])
    action1 = action1.astype(jnp.bfloat16)
    target_scaled, target_inverse = standard(target_hidden, sum_target, square_target, total_views)
    target_action = jax.nn.gelu(target_scaled * target_norm[0] + target_norm[1]).astype(
        jnp.bfloat16
    )
    middle, target_out = (
        lax.psum(across(action1, down_full).astype(jnp.bfloat16), "tensor").astype(jnp.float32),
        lax.psum(across(target_action, tdown_full).astype(jnp.bfloat16), "tensor").astype(
            jnp.float32
        ),
    )
    middle_low = middle.astype(jnp.bfloat16)
    hidden2 = jnp.dot(middle_low, pup_full, preferred_element_type=jnp.float32)
    sum_two, square_two = lax.psum(
        jnp.stack([jnp.sum(hidden2, 0), jnp.sum(hidden2 * hidden2, 0)]), "dp"
    )
    scaled2, inverse2 = standard(hidden2, sum_two, square_two, total_views)
    action2, gelu_back2 = jax.vjp(jax.nn.gelu, scaled2 * pred_norm[0] + pred_norm[1])
    action2 = action2.astype(jnp.bfloat16)
    query = lax.psum(across(action2, pdown_full).astype(jnp.bfloat16), "tensor").astype(jnp.float32)
    goal = partner(unit_rows(target_out))

    def loss_terms(values):
        return jnp.sum(keep_float * (2.0 - 2.0 * jnp.sum(unit_rows(values) * goal, 1)))

    local_loss, loss_back = jax.vjp(loss_terms, query)
    (grad_query,) = loss_back(1.0 / count)
    grad_query = grad_query.astype(jnp.bfloat16)
    grad_pred_down = outer_sum(grad_query, action2)
    (grad_norm2,) = gelu_back2(jnp.dot(grad_query, pdown_full, preferred_element_type=jnp.float32))
    back_sum2, back_cross2, loss_row = lax.psum(
        jnp.stack(
            [
                jnp.sum(grad_norm2, 0),
                jnp.sum(grad_norm2 * scaled2, 0),
                jnp.full((width,), local_loss),
            ]
        ),
        "dp",
    )
    loss_total = loss_row[0]
    grad_hidden2 = norm_back(
        grad_norm2, scaled2, inverse2, pred_norm, back_sum2, back_cross2, total_views
    ).astype(jnp.bfloat16)
    grad_pred_norm = jnp.stack([back_cross2, back_sum2])
    grad_pred_up = outer_sum(middle_low, grad_hidden2)
    grad_middle = lax.psum(across(grad_hidden2, pup_full).astype(jnp.bfloat16), "tensor")
    grad_proj_down = outer_sum(grad_middle, action1)
    (grad_norm1,) = gelu_back1(jnp.dot(grad_middle, down_full, preferred_element_type=jnp.float32))
    back_sum1, back_cross1 = lax.psum(
        jnp.stack([jnp.sum(grad_norm1, 0), jnp.sum(grad_norm1 * scaled1, 0)]), "dp"
    )
    grad_hidden1 = norm_back(
        grad_norm1, scaled1, inverse1, proj_norm, back_sum1, back_cross1, total_views
    ).astype(jnp.bfloat16)
    grad_proj_norm = jnp.stack([back_cross1, back_sum1])
    grad_proj_up = outer_sum(features, grad_hidden1)
    input_grad = lax.psum_scatter(
        across(grad_hidden1, up_full).astype(jnp.bfloat16),
        "tensor",
        scatter_dimension=1,
        tiled=True,
    ).astype(jnp.float32)
    shard_proj_up = lax.psum_scatter(
        grad_proj_up.astype(jnp.bfloat16), "dp", scatter_dimension=0, tiled=True
    ).astype(jnp.float32)
    small = lax.psum_scatter(
        jnp.stack([grad_proj_down, grad_pred_up, grad_pred_down]).astype(jnp.bfloat16),
        "dp",
        scatter_dimension=1,
        tiled=True,
    ).astype(jnp.float32)
    shard_proj_down, shard_pred_up, shard_pred_down = small[0], small[1], small[2]
    loss = loss_total / count
    return finish(
        total_views,
        (
            features,
            keep_mask,
            proj_up,
            proj_down,
            proj_norm,
            pred_up,
            pred_down,
            pred_norm,
            moment_proj_up,
            moment_proj_down,
            moment_proj_norm,
            moment_pred_up,
            moment_pred_down,
            moment_pred_norm,
            target_up,
            target_down,
            target_norm,
        ),
        loss,
        input_grad,
        shard_proj_up,
        shard_proj_down,
        grad_proj_norm,
        shard_pred_up,
        shard_pred_down,
        grad_pred_norm,
    )


MESH = pl.DeviceIdType.MESH
GRIDS = {16: (4, 2, 2)}
TILE = 256
GELU_A = math.sqrt(2.0 / math.pi)
GELU_B = 0.044715
LATE_STEPS = (1, 2, 2, 2, 2, 2, 1)
VMEM_LIMIT = 63 * 1024 * 1024


def loop(count, step):
    def one(i, carry):
        step(i)
        return carry

    lax.fori_loop(0, count, one, 0)


def nt_dot(first_op, second_op):
    return lax.dot_general(
        first_op, second_op, (((1,), (1,)), ((), ())), preferred_element_type=jnp.float32
    )


def tn_dot(first_op, second_op):
    return lax.dot_general(
        first_op, second_op, (((0,), (0,)), ((), ())), preferred_element_type=jnp.float32
    )


def gelu_parts(value):
    square = value * value
    gate = 0.5 + 0.5 * jnp.tanh(value * (GELU_A + (GELU_A * GELU_B) * square))
    return gate, square


def gelu_slope(value, gate, square):
    bend = value * (2.0 * GELU_A + (6.0 * GELU_A * GELU_B) * square)
    return gate * (1.0 + (1.0 - gate) * bend)


def step_kernel(
    grid,
    total_views,
    x_hbm,
    pu_hbm,
    tu_hbm,
    pd_hbm,
    qu_hbm,
    qd_hbm,
    td_hbm,
    proj_norm,
    pred_norm,
    target_norm,
    keep,
    ig_hbm,
    gu_out,
    qd_out,
    qu_out,
    pd_out,
    proj_stat,
    pred_stat,
    loss_out,
    feats,
    up,
    tup,
    small,
    act1,
    hat1,
    act2,
    hat2,
    wide,
    tact,
    acc,
    ex,
    exr,
    slope1,
    sr1,
    sr2,
    sr3,
    inv1,
    inv2,
    means,
    pa,
    pb,
    qa,
    qb,
    ta,
    tb,
    load_sem,
    ag_s,
    ag_r,
    ps_s,
    ps_r,
    qs_s,
    qs_r,
    ts_s,
    ts_r,
    ex_s,
    ex_r,
    rs_s,
    rs_r,
    ss_s,
    ss_r,
    ig_s,
    ig_r,
    ready,
):
    n0, n1, n2 = grid
    plane = n1 * n2
    views, width = wide.shape
    rows = up.shape[3]
    small_rows = small.shape[4]
    blocks = views // rows
    chunk = width // 4
    half = width // 2
    dp = lax.axis_index("dp")
    core = lax.axis_index("tensor")
    me = (dp // plane, (dp // n2) % n1, dp % n2)
    mp = dp % plane
    other = (dp, 1 - core)

    def place(index):
        return ((index[0] * n1 + index[1]) * n2 + index[2], core)

    def moved(axis, k):
        target = list(me)
        target[axis] = (me[axis] + k) % grid[axis]
        return tuple(target)

    barrier = pltpu.get_barrier_semaphore()
    greet = [place(moved(0, k)) for k in range(1, n0)]
    greet += [(me[0] * plane + (mp + k) % plane, core) for k in range(1, plane)]
    greet.append(other)
    for device in greet:
        pl.semaphore_signal(barrier, inc=1, device_id=device, device_id_type=MESH)

    loads = [
        pltpu.make_async_copy(src, wide.at[pl.ds(start, src.shape[0])], load_sem.at[i])
        for i, (src, start) in enumerate(
            (
                (pd_hbm, 2 * rows),
                (qu_hbm, 2 * rows + small_rows),
                (qd_hbm, 2 * rows + 2 * small_rows),
                (td_hbm, 2 * rows + 3 * small_rows),
                (pu_hbm, 0),
                (tu_hbm, rows),
            )
        )
    ]
    loads.append(pltpu.make_async_copy(x_hbm, feats, load_sem.at[6]))
    for i in (4, 0, 1, 2, 3, 5, 6):
        loads[i].start()

    def take(load, buffer, start):
        load.wait()
        buffer[me[0], me[1], me[2]] = wide[pl.ds(start, rows), :].astype(jnp.bfloat16)

    def take_small():
        for w, load in enumerate(loads[:4]):
            load.wait()
            small[w, me[0], me[1], me[2]] = wide[
                pl.ds(2 * rows + w * small_rows, small_rows), :
            ].astype(jnp.bfloat16)

    take(loads[4], up, 0)
    pl.semaphore_wait(barrier, len(greet))

    hops = n0 - 1
    kinds = [("up", i) for i in range(4)] + [("small", 0)]
    kinds += [("target", i) for i in (0, 1, 3)]
    main = len(kinds)
    kinds += [("target", 2), ("small", 1)]
    late = [main + 1, main]

    def piece(c, lane, sel):
        kind, index = kinds[c]
        if kind == "small":
            return small.at[
                pl.ds(2 * index, 2), sel[0], sel[1], sel[2], :, pl.ds(lane * half, half)
            ]
        buffer = up if kind == "up" else tup
        return buffer.at[sel[0], sel[1], sel[2], :, pl.ds(index * chunk + lane * TILE, TILE)]

    def gather_copy(c, lane, ref, sem, target):
        return pltpu.make_async_remote_copy(
            src_ref=ref,
            dst_ref=ref,
            send_sem=ag_s.at[c, lane, sem],
            recv_sem=ag_r.at[c, lane, sem],
            device_id=place(target),
            device_id_type=MESH,
        )

    def inside_line(index):
        return jnp.logical_and(index >= 0, index < n0)

    def line_each(c, lane, hop, way, act):
        sel = [None, slice(None), slice(None)] if c in late else [None, me[1], me[2]]
        for bit, turn in enumerate((1, -1)):
            block = me[0] - turn * (hop if way == "send" else hop + 1)
            fits = inside_line(block)
            if way == "send":
                fits = jnp.logical_and(fits, inside_line(me[0] + turn))

            @pl.when(fits)
            def _(bit=bit, turn=turn, block=block):
                ref = piece(c, lane, [block] + sel[1:])
                target = (me[0] + (turn if way == "send" else -turn), me[1], me[2])
                act(gather_copy(c, lane, ref, 2 * hop + bit, target))

    def line_hop(c, lane, hop):
        if hop:
            line_each(c, lane, hop - 1, "recv", lambda copy: copy.wait_recv())
        line_each(c, lane, hop, "send", lambda copy: copy.start())

    def side_copy(c, lane, phase):
        axis, second = ((2, 1), (1, 2))[lane]
        sel = [me[0] if c in late else slice(None), me[1], me[2]]
        if phase:
            sel[axis] = slice(None)
        return gather_copy(
            c, lane, piece(c, lane, sel), 2 * hops + phase, moved((axis, second)[phase], 1)
        )

    def gather_line(c, hop):
        for lane in range(2):
            line_hop(c, lane, hop)

    def gather_side(c, phase):
        for lane in range(2):
            if phase:
                side_copy(c, lane, 0).wait_recv()
            elif c not in late:
                line_each(c, lane, hops - 1, "recv", lambda copy: copy.wait_recv())
            side_copy(c, lane, phase).start()

    def gather_end(c):
        for lane in range(2):
            if c in late:
                line_each(c, lane, hops - 1, "recv", lambda copy: copy.wait_recv())
            else:
                side_copy(c, lane, 1).wait_recv()

    late_items = [(c, lane, hop) for hop in range(hops) for c in late for lane in range(2)]

    def late_next():
        if late_items:
            c, lane, hop = late_items.pop(0)
            if hop == 0:
                side_copy(c, lane, 1).wait_recv()
            line_hop(c, lane, hop)

    def gather_sent():
        for c in range(len(kinds)):
            for lane in range(2):
                for hop in range(hops):
                    line_each(c, lane, hop, "send", lambda copy: copy.wait_send())
                for phase in range(2):
                    side_copy(c, lane, phase).wait_send()

    def sum_copies(buffers, i, stage):
        first, second, send, recv = buffers
        if stage == 0:
            ref = first.at[i, mp]
            return [
                pltpu.make_async_remote_copy(
                    src_ref=ref,
                    dst_ref=ref,
                    send_sem=send.at[i, k - 1],
                    recv_sem=recv.at[i, k - 1],
                    device_id=(me[0] * plane + (mp + k) % plane, core),
                    device_id_type=MESH,
                )
                for k in range(1, plane)
            ]
        ref = second.at[i, me[0]]
        return [
            pltpu.make_async_remote_copy(
                src_ref=ref,
                dst_ref=ref,
                send_sem=send.at[i, plane - 1 + k - 1],
                recv_sem=recv.at[i, plane - 1 + k - 1],
                device_id=place(moved(0, k)),
                device_id_type=MESH,
            )
            for k in range(1, n0)
        ]

    narrow_sum = (pa, pb, ps_s, ps_r)
    half_sum = (qa, qb, qs_s, qs_r)
    scalar_sum = (ta, tb, ts_s, ts_r)

    def sum_start(buffers, i):
        for copy in sum_copies(buffers, i, 0):
            copy.start()

    def sum_middle(buffers, i):
        for copy in sum_copies(buffers, i, 0):
            copy.wait()
        first, second = buffers[:2]
        total = first[i, 0]
        for j in range(1, plane):
            total = total + first[i, j]
        second[i, me[0]] = total
        for copy in sum_copies(buffers, i, 1):
            copy.start()

    def sum_end(buffers, i):
        for copy in sum_copies(buffers, i, 1):
            copy.wait()
        second = buffers[1]
        total = second[i, 0]
        for j in range(1, n0):
            total = total + second[i, j]
        return total

    def swap(i):
        return pltpu.make_async_remote_copy(
            src_ref=ex.at[i],
            dst_ref=exr.at[i % 2],
            send_sem=ex_s.at[i],
            recv_sem=ex_r.at[i],
            device_id=other,
            device_id_type=MESH,
        )

    def swap_end(i):
        swap(i).wait()

        def add(b):
            part = pl.ds(pl.multiple_of(b * rows, rows), rows)
            ex[i, part, :] = (
                ex[i, part, :].astype(jnp.float32) + exr[i % 2, part, :].astype(jnp.float32)
            ).astype(jnp.bfloat16)

        loop(blocks, add)

    def weight(w, columns):
        return small[w, :, :, :, :, columns].reshape(plane * n0 * small_rows, columns.size)

    def columns_at(start, size):
        return pl.ds(pl.multiple_of(start, TILE), size)

    def hidden_chunk(weights, i, slot):
        def one(lane):
            columns = columns_at(i * chunk + lane * TILE, TILE)
            matrix = weights[:, :, :, :, columns].reshape(n0 * plane * rows, TILE)
            values = jnp.dot(feats[...], matrix, preferred_element_type=jnp.float32)
            wide[:, columns] = values
            spot = columns_at(lane * TILE, TILE)
            pa[slot, mp, 0:1, spot] = jnp.sum(values, 0, keepdims=True)
            pa[slot, mp, 1:2, spot] = jnp.sum(values * values, 0, keepdims=True)

        loop(2, one)

    def spread(total):
        mean = total[0:1] / total_views
        return mean, lax.rsqrt(total[1:2] / total_views - mean * mean + NORM_EPS)

    def act_tile(start, mean, inverse, norm, act_ref, hat_ref, act_start):
        columns = pl.ds(start, TILE)
        targets = pl.ds(act_start, TILE)
        gain, shift = norm[0:1, columns], norm[1:2, columns]

        def one(b):
            part = pl.ds(pl.multiple_of(b * rows, rows), rows)
            hat = (wide[part, columns] - mean) * inverse
            value = hat * gain + shift
            gate, square = gelu_parts(value)
            act_ref[b // 2, b % 2, :, targets] = (value * gate).astype(jnp.bfloat16)
            if hat_ref is not None:
                hat_ref[b // 2, b % 2, :, targets] = hat.astype(jnp.bfloat16)
                slope1[b // 2, b % 2, :, targets] = gelu_slope(value, gate, square).astype(
                    jnp.bfloat16
                )

        loop(blocks, one)

    def act_online(i):
        mean, inverse = spread(sum_end(narrow_sum, i))
        inv1[:, pl.ds(i * chunk, chunk)] = inverse
        for n in range(chunk // TILE):
            start = i * chunk + n * TILE
            here = slice(n * TILE, (n + 1) * TILE)
            act_tile(start, mean[:, here], inverse[:, here], proj_norm, act1, hat1, start)

    def act_target(i):
        mean, inverse = spread(sum_end(narrow_sum, 4 + i))
        for n in range(chunk // TILE):
            start = i * chunk + n * TILE
            here = slice(n * TILE, (n + 1) * TILE)
            act_tile(start, mean[:, here], inverse[:, here], target_norm, tact, None, 0)
            product = nt_dot(tact[...].reshape(views, TILE), weight(3, pl.ds(start, TILE)))
            if start == 0:
                acc[...] = product
            else:
                acc[...] += product

    count = []

    def sum_rows(i, columns, first_row, second_row):
        qa[i, mp, 0:1, columns] = first_row
        qa[i, mp, 1:2, columns] = second_row

    def online_middle():
        ex[0] = nt_dot(act1[...].reshape(views, width), weight(0, pl.ds(0, width))).astype(
            jnp.bfloat16
        )
        swap(0).start()
        swap_end(0)
        for side in range(2):

            def one(n):
                columns = columns_at(side * half + n * TILE, TILE)
                values = jnp.dot(ex[0], weight(1, columns), preferred_element_type=jnp.float32)
                sum_rows(
                    side,
                    columns_at(n * TILE, TILE),
                    jnp.sum(values, 0, keepdims=True),
                    jnp.sum(values * values, 0, keepdims=True),
                )

            loop(half // TILE, one)
            sum_start(half_sum, side)

    def online_query():
        for side in range(2):
            mean, inverse = spread(sum_end(half_sum, side))
            inv2[:, pl.ds(side * half, half)] = inverse
            means[:, pl.ds(side * half, half)] = mean
        spare = pl.ds(3 * chunk, TILE)

        def one(n):
            columns = columns_at(n * TILE, TILE)
            wide[:, spare] = jnp.dot(
                ex[0], weight(1, columns), preferred_element_type=jnp.float32
            )
            mean_n, inverse_n = means[:, columns], inv2[:, columns]
            gain, shift = pred_norm[0:1, columns], pred_norm[1:2, columns]

            def tile(b):
                part = pl.ds(pl.multiple_of(b * rows, rows), rows)
                hat = (wide[part, spare] - mean_n) * inverse_n
                value = hat * gain + shift
                gate, _ = gelu_parts(value)
                act2[b // 2, b % 2, :, columns] = (value * gate).astype(jnp.bfloat16)
                hat2[b // 2, b % 2, :, columns] = hat.astype(jnp.bfloat16)

            loop(blocks, tile)

        loop(width // TILE, one)
        ex[1] = nt_dot(
            act2[...].reshape(views, width), weight(2, pl.ds(0, width))
        ).astype(jnp.bfloat16)
        swap(1).start()

    def forward(tick):
        gather_side(tick, 0)
        for ahead, hop in ((1, 2), (2, 1), (3, 0)):
            if tick + ahead < main:
                gather_line(tick + ahead, hop)
        if tick >= 1:
            for _ in range(LATE_STEPS[tick - 1]):
                late_next()
            gather_side(tick - 1, 1)

    def hidden(slot):
        hidden_chunk(up if slot < 4 else tup, slot % 4, slot)
        sum_start(narrow_sum, slot)

    def after(tick):
        if tick == 2:
            loads[6].wait()
            kept = jnp.sum(jnp.sum(keep[...], 0, keepdims=True), 1, keepdims=True)
            ta[0, mp] = jnp.broadcast_to(kept, (8, 128))
            sum_start(scalar_sum, 0)
        if tick <= 5:
            hidden(tick - 2)
        if tick == 4:
            sum_middle(scalar_sum, 0)
        if 3 <= tick <= 6:
            sum_middle(narrow_sum, tick - 3)
        if tick >= 4:
            act_online(tick - 4)
        if tick == 6:
            count.append(sum_end(scalar_sum, 0))

    gather_line(0, 0)
    take_small()
    gather_side(late[0], 0)
    take(loads[5], tup, rows)
    gather_side(late[1], 0)
    gather_line(1, 0)
    gather_line(0, 1)
    gather_line(2, 0)
    gather_line(1, 1)
    gather_line(0, 2)
    for c in late:
        gather_side(c, 1)
    for tick in range(main - 1):
        forward(tick)
        if tick >= 2:
            gather_end(tick - 2)
            after(tick)
    forward(main - 1)
    after(main - 1)
    online_middle()
    gather_end(main - 3)
    hidden(4)
    gather_side(main - 1, 1)
    gather_end(main)
    hidden(6)
    sum_middle(half_sum, 0)
    sum_middle(half_sum, 1)
    sum_middle(narrow_sum, 4)
    gather_end(main - 2)
    hidden(5)
    gather_end(main + 1)
    online_query()
    act_target(0)
    gather_end(main - 1)
    sum_middle(narrow_sum, 6)
    sum_middle(narrow_sum, 5)
    hidden(7)
    swap_end(1)
    act_target(1)
    sum_middle(narrow_sum, 7)
    act_target(2)
    act_target(3)
    ex[2] = acc[...].astype(jnp.bfloat16)
    swap(2).start()
    gather_sent()
    swap(2).wait()

    scale = -2.0 / count[0][0:1, 0:1]

    def unit_scale(values):
        return lax.rsqrt(jnp.sum(values * values, 1, keepdims=True) + UNIT_EPS)

    even = (lax.broadcasted_iota(jnp.int32, (rows, acc.shape[1]), 0) % 2) == 0

    spot = lax.broadcasted_iota(jnp.int32, (rows, blocks), 1)

    def loss_tile(b, carry):
        part = pl.ds(pl.multiple_of(b * rows, rows), rows)
        query = ex[1, part, :].astype(jnp.float32)
        target = ex[2, part, :].astype(jnp.float32) + exr[0, part, :].astype(jnp.float32)
        target = target * unit_scale(target)
        goal = jnp.where(even, pltpu.roll(target, rows - 1, 0), pltpu.roll(target, 1, 0))
        back = unit_scale(query)
        unit = query * back
        cosine = jnp.sum(unit * goal, 1, keepdims=True)
        kept = jnp.sum(jnp.where(spot == b, keep[...], 0.0), 1, keepdims=True)
        ex[1, part, :] = ((scale * kept * back) * (goal - cosine * unit)).astype(jnp.bfloat16)
        return carry + kept * (2.0 - 2.0 * cosine)

    loss_rows = lax.fori_loop(0, blocks, loss_tile, jnp.zeros((rows, 1), jnp.float32))
    ta[1, mp] = jnp.broadcast_to(jnp.sum(loss_rows, 0, keepdims=True), (8, 128))
    sum_start(scalar_sum, 1)

    def back_norm(i, first, last, w, grads, hat_ref, norm, slope_ref):
        def one(n):
            columns = columns_at(n * TILE, TILE)
            wide[:, columns] = jnp.dot(
                ex[grads], weight(w, columns), preferred_element_type=jnp.float32
            )
            gain, shift = norm[0:1, columns], norm[1:2, columns]

            def tile(b, carry):
                part = pl.ds(pl.multiple_of(b * rows, rows), rows)
                hat = hat_ref[b // 2, b % 2, :, columns].astype(jnp.float32)
                if slope_ref is None:
                    value = hat * gain + shift
                    slope = gelu_slope(value, *gelu_parts(value))
                else:
                    slope = slope_ref[b // 2, b % 2, :, columns].astype(jnp.float32)
                grad = wide[part, columns] * slope
                wide[part, columns] = grad
                cross = grad * hat
                return (
                    carry[0] + jnp.sum(grad.reshape(rows // 8, 8, TILE), 0),
                    carry[1] + jnp.sum(cross.reshape(rows // 8, 8, TILE), 0),
                )

            zero = jnp.zeros((8, TILE), jnp.float32)
            sums = lax.fori_loop(0, blocks, tile, (zero, zero))
            sum_rows(
                i,
                columns_at((n % side_tiles) * TILE, TILE),
                jnp.sum(sums[0], 0, keepdims=True),
                jnp.sum(sums[1], 0, keepdims=True),
            )

        loop(last - first, lambda n: one(first + n))

    side_tiles = half // TILE

    def grad_hidden(stat, hat_ref, norm, inv_ref, columns):
        gain = norm[0:1, columns] * inv_ref[:, columns]
        shift = stat[0:1, columns] / total_views
        slope = stat[1:2, columns] / total_views

        def tile(b):
            part = pl.ds(pl.multiple_of(b * rows, rows), rows)
            hat = hat_ref[b // 2, b % 2, :, columns].astype(jnp.float32)
            hat_ref[b // 2, b % 2, :, columns] = (
                gain * (wide[part, columns] - shift - hat * slope)
            ).astype(jnp.bfloat16)

        loop(blocks, tile)

    def small_grad(w, grads, act_ref):
        def one(n):
            columns = columns_at(n * TILE, TILE)
            right = act_ref[:, :, :, columns].reshape(views, TILE)
            value = tn_dot(ex[grads], right).astype(jnp.bfloat16)
            small[w, :, :, :, :, columns] = value.reshape(n0, n1, n2, small_rows, TILE)

        loop(width // TILE, one)

    def plus(*terms):
        total = terms[0].astype(jnp.float32)
        for term in terms[1:]:
            total = total + term.astype(jnp.float32)
        return total

    def low_plus(*terms):
        return plus(*terms).astype(jnp.bfloat16)

    up_parts = [("line", 0, TILE // 2)]
    up_parts += [("side", TILE + g * chunk, TILE) for g in range(3)]
    up_parts += [("side", TILE + 3 * chunk, TILE // 2)]

    def reduce_copies(kind, g, lane, phase):
        axis, second = ((1, 2), (2, 1))[lane]
        style = up_parts[g][0] if kind == "up" else "side"
        order = (0, axis, second) if style == "line" else (axis, second, 0)
        sems = ((0, 3, 4) if style == "line" else (0, 1, 2))[phase]
        send, recv = (rs_s, rs_r) if kind == "up" else (ss_s, ss_r)
        axis_now = order[phase]
        copies = []
        for k in range(1, grid[axis_now]):
            target = moved(axis_now, k)
            sel = [slice(None)] * 3
            for done in order[:phase]:
                sel[done] = me[done]
            sel[axis_now] = target[axis_now]
            if kind == "small":
                columns = pl.ds(lane * half, half)
                source = small.at[3 - g, sel[0], sel[1], sel[2], :, columns]
                if phase == 0:
                    land = sr1.at[g, :, :, :, columns]
                elif phase == 1:
                    land = sr2.at[g, :, :, columns]
                else:
                    land = sr3.at[g, me[0], :, columns]
            else:
                _, start, size = up_parts[g]
                columns = pl.ds(start + lane * size, size)
                source = tup.at[sel[0], sel[1], sel[2], :, columns]
                if style == "line":
                    if phase == 0:
                        land = (act2 if k < 3 else hat2).at[
                            pl.ds(2 * ((k - 1) % 2), 2), :, :, columns
                        ]
                    elif phase == 1:
                        land = hat2.at[2, :, :, columns]
                    else:
                        land = hat2.at[3, 0, :, columns]
                elif phase == 0:
                    land = act2.at[:, :, :, columns]
                elif phase == 1:
                    land = hat2.at[:, 0, :, columns]
                else:
                    land = hat2.at[me[0], 1, :, columns]
            copies.append(
                pltpu.make_async_remote_copy(
                    src_ref=source,
                    dst_ref=land,
                    send_sem=send.at[g, lane, sems + k - 1],
                    recv_sem=recv.at[g, lane, sems + k - 1],
                    device_id=place(target),
                    device_id_type=MESH,
                )
            )
        return copies

    def reduce_step(kind, g, phase):
        for lane in range(2):
            if phase:
                for copy in reduce_copies(kind, g, lane, phase - 1):
                    copy.wait()
                if kind == "small":
                    small_add(g, lane, phase)
                elif up_parts[g][0] == "line":
                    line_add(g, lane, phase)
                else:
                    side_add(g, lane, phase)
            if phase < 3:
                for copy in reduce_copies(kind, g, lane, phase):
                    copy.start()

    def plane_spot(lane, i):
        return (me[1], i) if lane == 0 else (i, me[2])

    def small_add(g, lane, phase):
        columns = pl.ds(lane * half, half)
        w = 3 - g
        if phase == 1:

            def add(j):
                z, i = j // 2, j % 2
                y, x = plane_spot(lane, i)
                small[w, z, y, x, :, columns] = low_plus(
                    small[w, z, y, x, :, columns], sr1[g, z, i, :, columns]
                )

            loop(n0 * 2, add)
        elif phase == 2:

            def add(z):
                small[w, z, me[1], me[2], :, columns] = low_plus(
                    small[w, z, me[1], me[2], :, columns], sr2[g, z, :, columns]
                )

            loop(n0, add)
        else:
            (qd_out, qu_out, pd_out)[g][:, columns] = low_plus(
                small[w, me[0], me[1], me[2], :, columns],
                *[sr3[g, (me[0] + k) % n0, :, columns] for k in range(1, n0)],
            )

    def side_add(g, lane, phase):
        _, start, size = up_parts[g]
        columns = pl.ds(start + lane * size, size)
        if phase == 1:

            def add(j):
                z, i = j // 2, j % 2
                y, x = plane_spot(lane, i)
                tup[z, y, x, :, columns] = low_plus(
                    tup[z, y, x, :, columns], act2[z, i, :, columns]
                )

            loop(n0 * 2, add)
        elif phase == 2:

            def add(z):
                tup[z, me[1], me[2], :, columns] = low_plus(
                    tup[z, me[1], me[2], :, columns], hat2[z, 0, :, columns]
                )

            loop(n0, add)
        else:
            gu_out[:, columns] = low_plus(
                tup[me[0], me[1], me[2], :, columns],
                *[hat2[(me[0] + k) % n0, 1, :, columns] for k in range(1, n0)],
            )

    def line_add(g, lane, phase):
        _, start, size = up_parts[g]
        columns = pl.ds(start + lane * size, size)
        z = me[0]
        if phase == 1:

            def add(j):
                y, x = j // 2, j % 2
                tup[z, y, x, :, columns] = low_plus(
                    tup[z, y, x, :, columns],
                    act2[y, x, :, columns],
                    act2[2 + y, x, :, columns],
                    hat2[y, x, :, columns],
                )

            loop(plane, add)
        elif phase == 2:

            def add(i):
                y, x = plane_spot(lane, i)
                tup[z, y, x, :, columns] = low_plus(
                    tup[z, y, x, :, columns], hat2[2, i, :, columns]
                )

            loop(2, add)
        else:
            gu_out[:, columns] = low_plus(
                tup[z, me[1], me[2], :, columns], hat2[3, 0, :, columns]
            )

    def pred_half(side):
        pred_stat[:, pl.ds(side * half, half)] = sum_end(half_sum, 2 + side)

        def one(n):
            columns = columns_at(side * half + n * TILE, TILE)
            grad_hidden(pred_stat, hat2, pred_norm, inv2, columns)

        loop(side_tiles, one)
        columns = pl.ds(side * half, half)
        product = nt_dot(hat2[:, :, :, columns].reshape(views, half), weight(1, columns))
        if side == 0:
            acc[...] = product
        else:
            acc[...] += product

    middle_tile = side_tiles + side_tiles // 2
    pred_args = (2, 1, hat2, pred_norm, None)
    back_norm(2, 0, side_tiles, *pred_args)
    sum_start(half_sum, 2)
    back_norm(3, side_tiles, middle_tile, *pred_args)
    sum_middle(half_sum, 2)
    back_norm(3, middle_tile, 2 * side_tiles, *pred_args)
    sum_start(half_sum, 3)
    small_grad(3, 1, act2)
    sum_middle(half_sum, 3)
    reduce_step("small", 0, 0)
    pred_half(0)
    pred_half(1)
    ex[3] = acc[...].astype(jnp.bfloat16)
    swap(3).start()
    small_grad(2, 0, hat2)
    reduce_step("small", 1, 0)
    reduce_step("small", 0, 1)
    swap_end(3)
    proj_args = (0, 3, hat1, proj_norm, slope1)
    back_norm(4, 0, side_tiles, *proj_args)
    sum_start(half_sum, 4)
    back_norm(5, side_tiles, middle_tile, *proj_args)
    sum_middle(half_sum, 4)
    reduce_step("small", 1, 1)
    reduce_step("small", 0, 2)
    back_norm(5, middle_tile, 2 * side_tiles, *proj_args)
    sum_start(half_sum, 5)
    small_grad(1, 3, act1)
    pl.semaphore_signal(ready, inc=1, device_id=other, device_id_type=MESH)
    sum_middle(half_sum, 5)
    reduce_step("small", 2, 0)
    sum_middle(scalar_sum, 1)
    proj_stat[:, pl.ds(0, half)] = sum_end(half_sum, 4)

    def up_hidden(g):
        _, start, size = up_parts[g]
        for n in range(2 * size // TILE):
            grad_hidden(proj_stat, hat1, proj_norm, inv1, pl.ds(start + n * TILE, TILE))

    def up_grad(g):
        _, start, size = up_parts[g]
        columns = pl.ds(start, 2 * size)

        def one(z):
            left = feats[:, columns_at(z * plane * rows, plane * rows)]
            value = tn_dot(left, hat1[:, :, :, columns].reshape(views, 2 * size))
            tup[z, :, :, :, columns] = value.astype(jnp.bfloat16).reshape(n1, n2, rows, 2 * size)

        loop(n0, one)
        reduce_step("up", g, 0)

    parts = ig_s.shape[0]

    def input_copy(q):
        return pltpu.make_async_remote_copy(
            src_ref=act1.at[:, :, :, pl.ds(q * TILE, TILE)],
            dst_ref=act1.at[:, :, :, pl.ds((parts + q) * TILE, TILE)],
            send_sem=ig_s.at[q],
            recv_sem=ig_r.at[q],
            device_id=other,
            device_id_type=MESH,
        )

    def input_product(q, side):
        first = side * (n0 // 2) + q // n1
        matrix = up[first, q % n1].reshape(n2 * rows, width)
        return nt_dot(hat1[...].reshape(views, width), matrix)

    def send_part(q):
        act1[:, :, :, pl.ds(q * TILE, TILE)] = (
            input_product(q, 1 - core).astype(jnp.bfloat16).reshape(n0, 2, rows, TILE)
        )
        input_copy(q).start()

    def own_part(q):
        wide[:, pl.ds(q * TILE, TILE)] = input_product(q, core)

    up_hidden(0)
    up_grad(0)
    up_hidden(1)
    up_grad(1)
    proj_stat[:, pl.ds(half, half)] = sum_end(half_sum, 5)
    for g in (2, 3, 4):
        up_hidden(g)
    up_grad(2)
    reduce_step("small", 1, 2)
    reduce_step("small", 0, 3)
    pl.semaphore_wait(ready, 1)
    send_part(0)
    reduce_step("up", 1, 1)
    up_grad(3)
    reduce_step("small", 2, 1)
    send_part(1)
    send_part(2)
    reduce_step("up", 0, 1)
    reduce_step("up", 2, 1)
    up_grad(4)
    reduce_step("up", 1, 2)
    reduce_step("small", 2, 2)
    reduce_step("small", 1, 3)
    send_part(3)
    own_part(0)
    reduce_step("up", 0, 2)
    reduce_step("up", 3, 1)
    reduce_step("up", 2, 2)
    own_part(1)
    own_part(2)
    reduce_step("up", 4, 1)
    reduce_step("up", 3, 2)
    own_part(3)
    for q in range(parts):
        input_copy(q).wait()

        def add(b, q=q):
            part = pl.ds(pl.multiple_of(b * rows, rows), rows)
            theirs = act1[b // 2, b % 2, :, pl.ds((parts + q) * TILE, TILE)]
            act1[b // 2, b % 2, :, pl.ds(q * TILE, TILE)] = low_plus(
                wide[part, pl.ds(q * TILE, TILE)], theirs
            )

        loop(blocks, add)
    out_copy = pltpu.make_async_copy(
        act1.at[:, :, :, pl.ds(0, parts * TILE)], ig_hbm, load_sem.at[0]
    )
    out_copy.start()
    reduce_step("up", 4, 2)
    reduce_step("small", 2, 3)
    loss_out[...] = (sum_end(scalar_sum, 1) / count[0])[0:1, 0:1]
    for g in range(5):
        reduce_step("up", g, 3)
    out_copy.wait()


def kernel_step(grid, total_views, features, keep, ups, downs, norms):
    n0, n1, n2 = grid
    plane = n1 * n2
    views, depth = features.shape
    rows, width = ups[0].shape
    small_rows = downs[0].shape[0]
    out = small_rows * n0 * plane
    parts = depth // 2 // TILE
    low, full = jnp.bfloat16, jnp.float32
    vm = pltpu.VMEM
    dma = pltpu.SemaphoreType.DMA
    anywhere = pl.BlockSpec(memory_space=pl.ANY)
    inside = pl.BlockSpec(memory_space=pltpu.VMEM)
    spread_shape = (n0, 2, rows, width)
    moves = 2 * (n0 - 1) + 2
    sum_moves = plane - 1 + n0 - 1
    return pl.pallas_call(
        functools.partial(step_kernel, grid, total_views),
        out_shape=(
            jax.ShapeDtypeStruct((n0, 2, rows, depth // 2), low),
            jax.ShapeDtypeStruct((rows, width), low),
            jax.ShapeDtypeStruct((small_rows, width), low),
            jax.ShapeDtypeStruct((small_rows, width), low),
            jax.ShapeDtypeStruct((small_rows, width), low),
            jax.ShapeDtypeStruct((2, width), full),
            jax.ShapeDtypeStruct((2, width), full),
            jax.ShapeDtypeStruct((1, 1), full),
        ),
        in_specs=[anywhere] * 7 + [inside] * 4,
        out_specs=(anywhere,) + (inside,) * 7,
        scratch_shapes=[
            vm((views, depth), low),
            vm((n0, n1, n2, rows, width), low),
            vm((n0, n1, n2, rows, width), low),
            vm((4, n0, n1, n2, small_rows, width), low),
            vm(spread_shape, low),
            vm(spread_shape, low),
            vm(spread_shape, low),
            vm(spread_shape, low),
            vm((views, width), full),
            vm((n0, 2, rows, TILE), low),
            vm((views, out), full),
            vm((4, views, out), low),
            vm((2, views, out), low),
            vm(spread_shape, low),
            vm((3, n0, 2, small_rows, width), low),
            vm((3, n0, small_rows, width), low),
            vm((3, n0, small_rows, width), low),
            vm((1, width), full),
            vm((1, width), full),
            vm((1, width), full),
            vm((8, plane, 2, width // 4), full),
            vm((8, n0, 2, width // 4), full),
            vm((6, plane, 2, width // 2), full),
            vm((6, n0, 2, width // 2), full),
            vm((2, plane, 8, 128), full),
            vm((2, n0, 8, 128), full),
            dma((7,)),
            dma((10, 2, moves)),
            dma((10, 2, moves)),
            dma((8, sum_moves)),
            dma((8, sum_moves)),
            dma((6, sum_moves)),
            dma((6, sum_moves)),
            dma((2, sum_moves)),
            dma((2, sum_moves)),
            dma((4,)),
            dma((4,)),
            dma((5, 2, n0 + 1)),
            dma((5, 2, n0 + 1)),
            dma((3, 2, n0 + 1)),
            dma((3, 2, n0 + 1)),
            dma((parts,)),
            dma((parts,)),
            pltpu.SemaphoreType.REGULAR,
        ],
        compiler_params=pltpu.CompilerParams(
            collective_id=0, has_side_effects=True, vmem_limit_bytes=VMEM_LIMIT
        ),
    )(features, *ups, *downs, *norms, keep)


def step_body(grid, *args):
    (
        features,
        keep_mask,
        proj_up,
        proj_down,
        proj_norm,
        pred_up,
        pred_down,
        pred_norm,
        moment_proj_up,
        moment_proj_down,
        moment_proj_norm,
        moment_pred_up,
        moment_pred_down,
        moment_pred_norm,
        target_up,
        target_down,
        target_norm,
    ) = args
    if grid is None:
        return plain_body(*args)
    total_views = float(features.shape[0] * lax.axis_size("dp"))
    (input_grad, *shards, proj_stat, pred_stat, loss) = kernel_step(
        grid,
        total_views,
        features,
        keep_mask.astype(jnp.float32).reshape(-1, proj_up.shape[0]).T,
        (proj_up, target_up),
        (proj_down, pred_up, pred_down, target_down),
        (proj_norm, pred_norm, target_norm),
    )
    shard_proj_up, shard_pred_down, shard_pred_up, shard_proj_down = (
        shard.astype(jnp.float32) for shard in shards
    )
    input_grad = input_grad.astype(jnp.float32).reshape(features.shape[0], -1)
    grad_proj_norm = proj_stat[::-1]
    grad_pred_norm = pred_stat[::-1]
    return finish(
        total_views,
        args,
        loss.reshape(()),
        input_grad,
        shard_proj_up,
        shard_proj_down,
        grad_proj_norm,
        shard_pred_up,
        shard_pred_down,
        grad_pred_norm,
    )


def solution(mesh):
    placed = (
        P("dp", None),
        P("dp"),
        P("dp", "tensor"),
        P("dp", "tensor"),
        P(None, "tensor"),
        P("dp", "tensor"),
        P("dp", "tensor"),
        P(None, "tensor"),
        P("dp", "tensor"),
        P("dp", "tensor"),
        P(None, "tensor"),
        P("dp", "tensor"),
        P("dp", "tensor"),
        P(None, "tensor"),
        P("dp", "tensor"),
        P("dp", "tensor"),
        P(None, "tensor"),
    )
    return jax.shard_map(
        functools.partial(step_body, GRIDS.get(mesh.shape["dp"])),
        mesh=mesh,
        in_specs=placed,
        out_specs=(
            P(),
            P("dp", "tensor"),
            P("dp", "tensor"),
            P("dp", "tensor"),
            P("dp", "tensor"),
            P("dp", "tensor"),
            P("dp", "tensor"),
            P("dp", "tensor"),
            P(None, "tensor"),
            P(None, "tensor"),
            P(None, "tensor"),
            P("dp", "tensor"),
            P("dp", "tensor"),
            P("dp", "tensor"),
            P("dp", "tensor"),
            P("dp", "tensor"),
            P("dp", "tensor"),
            P(None, "tensor"),
            P(None, "tensor"),
            P(None, "tensor"),
            P("dp", "tensor"),
            P("dp", "tensor"),
            P(None, "tensor"),
        ),
        check_vma=False,
    )
```

```python
import functools
import math

import jax
import jax.numpy as jnp
from jax import lax
from jax.experimental import pallas as pl
from jax.experimental.pallas import tpu as pltpu
from jax.sharding import PartitionSpec as P

NORM_EPS = 1e-05
UNIT_EPS = 1e-06
RATE_PROJ_UP = 9.0
RATE_PROJ_DOWN = 1.2
RATE_PROJ_NORM = 40.0
RATE_PRED_UP = 18.0
RATE_PRED_DOWN = 0.9
RATE_PRED_NORM = 30.0


def across(matrix, weight):
    return lax.dot_general(
        matrix, weight, (((1,), (1,)), ((), ())), preferred_element_type=jnp.float32
    )


def outer_sum(first_op, second_op):
    return lax.dot_general(
        first_op, second_op, (((0,), (0,)), ((), ())), preferred_element_type=jnp.float32
    )


def standard(hidden, col_sum, col_square, total_views):
    middle_mean = col_sum / total_views
    inverse = lax.rsqrt(col_square / total_views - middle_mean * middle_mean + NORM_EPS)
    return ((hidden - middle_mean) * inverse, inverse)


def norm_back(grad_out, scaled, inverse, params, sum_grad, sum_cross, total_views):
    return (
        params[0]
        * inverse
        * (grad_out - sum_grad / total_views - scaled * (sum_cross / total_views))
    )


def unit_rows(values):
    return values * lax.rsqrt(jnp.sum(values * values, 1, keepdims=True) + UNIT_EPS)


def partner(values):
    width = values.shape[1]
    return values.reshape(-1, 2, width)[:, ::-1, :].reshape(-1, width)


def nesterov(weight, moment, grad, rate):
    fresh = 0.5 * moment + grad
    return (fresh, weight - rate * (grad + 0.5 * fresh))


def finish(
    total_views,
    args,
    loss,
    input_grad,
    shard_proj_up,
    shard_proj_down,
    grad_proj_norm,
    shard_pred_up,
    shard_pred_down,
    grad_pred_norm,
):
    (proj_up, proj_down, proj_norm, pred_up, pred_down, pred_norm) = args[2:8]
    (
        moment_proj_up,
        moment_proj_down,
        moment_proj_norm,
        moment_pred_up,
        moment_pred_down,
        moment_pred_norm,
        target_up,
        target_down,
        target_norm,
    ) = args[8:]
    scale = math.sqrt(total_views)
    mom_pu, next_pu = nesterov(proj_up, moment_proj_up, shard_proj_up, RATE_PROJ_UP * scale)
    mom_pd, next_pd = nesterov(proj_down, moment_proj_down, shard_proj_down, RATE_PROJ_DOWN * scale)
    mom_pn, next_pn = nesterov(proj_norm, moment_proj_norm, grad_proj_norm, RATE_PROJ_NORM * scale)
    mom_qu, next_qu = nesterov(pred_up, moment_pred_up, shard_pred_up, RATE_PRED_UP * scale)
    mom_qd, next_qd = nesterov(pred_down, moment_pred_down, shard_pred_down, RATE_PRED_DOWN * scale)
    mom_qn, next_qn = nesterov(pred_norm, moment_pred_norm, grad_pred_norm, RATE_PRED_NORM * scale)
    target_up_next = 0.5 * target_up + 0.5 * next_pu
    target_down_next = 0.5 * target_down + 0.5 * next_pd
    target_norm_next = 0.5 * target_norm + 0.5 * next_pn
    return (
        loss,
        input_grad,
        shard_proj_up,
        mom_pu,
        next_pu,
        shard_proj_down,
        mom_pd,
        next_pd,
        grad_proj_norm,
        mom_pn,
        next_pn,
        shard_pred_up,
        mom_qu,
        next_qu,
        shard_pred_down,
        mom_qd,
        next_qd,
        grad_pred_norm,
        mom_qn,
        next_qn,
        target_up_next,
        target_down_next,
        target_norm_next,
    )


def plain_body(
    features,
    keep_mask,
    proj_up,
    proj_down,
    proj_norm,
    pred_up,
    pred_down,
    pred_norm,
    moment_proj_up,
    moment_proj_down,
    moment_proj_norm,
    moment_pred_up,
    moment_pred_down,
    moment_pred_norm,
    target_up,
    target_down,
    target_norm,
):
    total_views = float(features.shape[0] * lax.axis_size("dp"))
    width = proj_up.shape[1]

    def gathered(parts):
        low = jnp.stack([part.astype(jnp.bfloat16) for part in parts])
        full = lax.all_gather(low, "dp", axis=1, tiled=True)
        return tuple(full[i] for i in range(len(parts)))

    (up_full, tup_full) = gathered((proj_up, target_up))
    (down_full, pup_full, pdown_full, tdown_full) = gathered(
        (proj_down, pred_up, pred_down, target_down)
    )
    keep_float = keep_mask.astype(jnp.float32)
    hidden1 = jnp.dot(features, up_full, preferred_element_type=jnp.float32)
    target_hidden = jnp.dot(features, tup_full, preferred_element_type=jnp.float32)
    sums = lax.psum(
        jnp.stack(
            [
                jnp.sum(hidden1, 0),
                jnp.sum(hidden1 * hidden1, 0),
                jnp.sum(target_hidden, 0),
                jnp.sum(target_hidden * target_hidden, 0),
                jnp.full((width,), jnp.sum(keep_float)),
            ]
        ),
        "dp",
    )
    sum_one, square_one, sum_target, square_target = sums[0], sums[1], sums[2], sums[3]
    count = sums[4, 0]
    scaled1, inverse1 = standard(hidden1, sum_one, square_one, total_views)
    action1, gelu_back1 = jax.vjp(jax.nn.gelu, scaled1 * proj_norm[0] + proj_norm[1])
    action1 = action1.astype(jnp.bfloat16)
    target_scaled, target_inverse = standard(target_hidden, sum_target, square_target, total_views)
    target_action = jax.nn.gelu(target_scaled * target_norm[0] + target_norm[1]).astype(
        jnp.bfloat16
    )
    middle, target_out = (
        lax.psum(across(action1, down_full).astype(jnp.bfloat16), "tensor").astype(jnp.float32),
        lax.psum(across(target_action, tdown_full).astype(jnp.bfloat16), "tensor").astype(
            jnp.float32
        ),
    )
    middle_low = middle.astype(jnp.bfloat16)
    hidden2 = jnp.dot(middle_low, pup_full, preferred_element_type=jnp.float32)
    sum_two, square_two = lax.psum(
        jnp.stack([jnp.sum(hidden2, 0), jnp.sum(hidden2 * hidden2, 0)]), "dp"
    )
    scaled2, inverse2 = standard(hidden2, sum_two, square_two, total_views)
    action2, gelu_back2 = jax.vjp(jax.nn.gelu, scaled2 * pred_norm[0] + pred_norm[1])
    action2 = action2.astype(jnp.bfloat16)
    query = lax.psum(across(action2, pdown_full).astype(jnp.bfloat16), "tensor").astype(jnp.float32)
    goal = partner(unit_rows(target_out))

    def loss_terms(values):
        return jnp.sum(keep_float * (2.0 - 2.0 * jnp.sum(unit_rows(values) * goal, 1)))

    local_loss, loss_back = jax.vjp(loss_terms, query)
    (grad_query,) = loss_back(1.0 / count)
    grad_query = grad_query.astype(jnp.bfloat16)
    grad_pred_down = outer_sum(grad_query, action2)
    (grad_norm2,) = gelu_back2(jnp.dot(grad_query, pdown_full, preferred_element_type=jnp.float32))
    back_sum2, back_cross2, loss_row = lax.psum(
        jnp.stack(
            [
                jnp.sum(grad_norm2, 0),
                jnp.sum(grad_norm2 * scaled2, 0),
                jnp.full((width,), local_loss),
            ]
        ),
        "dp",
    )
    loss_total = loss_row[0]
    grad_hidden2 = norm_back(
        grad_norm2, scaled2, inverse2, pred_norm, back_sum2, back_cross2, total_views
    ).astype(jnp.bfloat16)
    grad_pred_norm = jnp.stack([back_cross2, back_sum2])
    grad_pred_up = outer_sum(middle_low, grad_hidden2)
    grad_middle = lax.psum(across(grad_hidden2, pup_full).astype(jnp.bfloat16), "tensor")
    grad_proj_down = outer_sum(grad_middle, action1)
    (grad_norm1,) = gelu_back1(jnp.dot(grad_middle, down_full, preferred_element_type=jnp.float32))
    back_sum1, back_cross1 = lax.psum(
        jnp.stack([jnp.sum(grad_norm1, 0), jnp.sum(grad_norm1 * scaled1, 0)]), "dp"
    )
    grad_hidden1 = norm_back(
        grad_norm1, scaled1, inverse1, proj_norm, back_sum1, back_cross1, total_views
    ).astype(jnp.bfloat16)
    grad_proj_norm = jnp.stack([back_cross1, back_sum1])
    grad_proj_up = outer_sum(features, grad_hidden1)
    input_grad = lax.psum_scatter(
        across(grad_hidden1, up_full).astype(jnp.bfloat16),
        "tensor",
        scatter_dimension=1,
        tiled=True,
    ).astype(jnp.float32)
    shard_proj_up = lax.psum_scatter(
        grad_proj_up.astype(jnp.bfloat16), "dp", scatter_dimension=0, tiled=True
    ).astype(jnp.float32)
    small = lax.psum_scatter(
        jnp.stack([grad_proj_down, grad_pred_up, grad_pred_down]).astype(jnp.bfloat16),
        "dp",
        scatter_dimension=1,
        tiled=True,
    ).astype(jnp.float32)
    shard_proj_down, shard_pred_up, shard_pred_down = small[0], small[1], small[2]
    loss = loss_total / count
    return finish(
        total_views,
        (
            features,
            keep_mask,
            proj_up,
            proj_down,
            proj_norm,
            pred_up,
            pred_down,
            pred_norm,
            moment_proj_up,
            moment_proj_down,
            moment_proj_norm,
            moment_pred_up,
            moment_pred_down,
            moment_pred_norm,
            target_up,
            target_down,
            target_norm,
        ),
        loss,
        input_grad,
        shard_proj_up,
        shard_proj_down,
        grad_proj_norm,
        shard_pred_up,
        shard_pred_down,
        grad_pred_norm,
    )


MESH = pl.DeviceIdType.MESH
GRIDS = {16: (4, 2, 2)}
TILE = 256
GELU_A = math.sqrt(2.0 / math.pi)
GELU_B = 0.044715
LATE_STEPS = (1, 2, 2, 2, 2, 2, 1)
VMEM_LIMIT = 63 * 1024 * 1024


def loop(count, step):
    def one(i, carry):
        step(i)
        return carry

    lax.fori_loop(0, count, one, 0)


def nt_dot(first_op, second_op):
    return lax.dot_general(
        first_op, second_op, (((1,), (1,)), ((), ())), preferred_element_type=jnp.float32
    )


def tn_dot(first_op, second_op):
    return lax.dot_general(
        first_op, second_op, (((0,), (0,)), ((), ())), preferred_element_type=jnp.float32
    )


def gelu_parts(value):
    square = value * value
    gate = 0.5 + 0.5 * jnp.tanh(value * (GELU_A + (GELU_A * GELU_B) * square))
    return gate, square


def gelu_slope(value, gate, square):
    bend = value * (2.0 * GELU_A + (6.0 * GELU_A * GELU_B) * square)
    return gate * (1.0 + (1.0 - gate) * bend)


def step_kernel(
    grid,
    total_views,
    x_hbm,
    pu_hbm,
    tu_hbm,
    pd_hbm,
    qu_hbm,
    qd_hbm,
    td_hbm,
    proj_norm,
    pred_norm,
    target_norm,
    keep,
    ig_hbm,
    gu_out,
    qd_out,
    qu_out,
    pd_out,
    proj_stat,
    pred_stat,
    loss_out,
    feats,
    up,
    tup,
    small,
    act1,
    hat1,
    act2,
    hat2,
    wide,
    tact,
    acc,
    ex,
    exr,
    slope1,
    sr1,
    sr2,
    sr3,
    inv1,
    inv2,
    means,
    pa,
    pb,
    qa,
    qb,
    ta,
    tb,
    load_sem,
    ag_s,
    ag_r,
    ps_s,
    ps_r,
    qs_s,
    qs_r,
    ts_s,
    ts_r,
    ex_s,
    ex_r,
    rs_s,
    rs_r,
    ss_s,
    ss_r,
    ig_s,
    ig_r,
    ready,
):
    n0, n1, n2 = grid
    plane = n1 * n2
    views, width = wide.shape
    rows = up.shape[3]
    small_rows = small.shape[4]
    blocks = views // rows
    chunk = width // 4
    half = width // 2
    dp = lax.axis_index("dp")
    core = lax.axis_index("tensor")
    me = (dp // plane, (dp // n2) % n1, dp % n2)
    mp = dp % plane
    other = (dp, 1 - core)

    def place(index):
        return ((index[0] * n1 + index[1]) * n2 + index[2], core)

    def moved(axis, k):
        target = list(me)
        target[axis] = (me[axis] + k) % grid[axis]
        return tuple(target)

    barrier = pltpu.get_barrier_semaphore()
    greet = [place(moved(0, k)) for k in range(1, n0)]
    greet += [(me[0] * plane + (mp + k) % plane, core) for k in range(1, plane)]
    greet.append(other)
    for device in greet:
        pl.semaphore_signal(barrier, inc=1, device_id=device, device_id_type=MESH)

    loads = [
        pltpu.make_async_copy(src, wide.at[pl.ds(start, src.shape[0])], load_sem.at[i])
        for i, (src, start) in enumerate(
            (
                (pd_hbm, 2 * rows),
                (qu_hbm, 2 * rows + small_rows),
                (qd_hbm, 2 * rows + 2 * small_rows),
                (td_hbm, 2 * rows + 3 * small_rows),
                (pu_hbm, 0),
                (tu_hbm, rows),
            )
        )
    ]
    loads.append(pltpu.make_async_copy(x_hbm, feats, load_sem.at[6]))
    for i in (4, 0, 1, 2, 3, 5, 6):
        loads[i].start()

    def take(load, buffer, start):
        load.wait()
        buffer[me[0], me[1], me[2]] = wide[pl.ds(start, rows), :].astype(jnp.bfloat16)

    def take_small():
        for w, load in enumerate(loads[:4]):
            load.wait()
            small[w, me[0], me[1], me[2]] = wide[
                pl.ds(2 * rows + w * small_rows, small_rows), :
            ].astype(jnp.bfloat16)

    take(loads[4], up, 0)
    pl.semaphore_wait(barrier, len(greet))

    hops = n0 - 1
    kinds = [("up", i) for i in range(4)] + [("small", 0)]
    kinds += [("target", i) for i in (0, 1, 3)]
    main = len(kinds)
    kinds += [("target", 2), ("small", 1)]
    late = [main + 1, main]

    def piece(c, lane, sel):
        kind, index = kinds[c]
        if kind == "small":
            return small.at[
                pl.ds(2 * index, 2), sel[0], sel[1], sel[2], :, pl.ds(lane * half, half)
            ]
        buffer = up if kind == "up" else tup
        return buffer.at[sel[0], sel[1], sel[2], :, pl.ds(index * chunk + lane * TILE, TILE)]

    def gather_copy(c, lane, ref, sem, target):
        return pltpu.make_async_remote_copy(
            src_ref=ref,
            dst_ref=ref,
            send_sem=ag_s.at[c, lane, sem],
            recv_sem=ag_r.at[c, lane, sem],
            device_id=place(target),
            device_id_type=MESH,
        )

    def inside_line(index):
        return jnp.logical_and(index >= 0, index < n0)

    def line_each(c, lane, hop, way, act):
        sel = [None, slice(None), slice(None)] if c in late else [None, me[1], me[2]]
        for bit, turn in enumerate((1, -1)):
            block = me[0] - turn * (hop if way == "send" else hop + 1)
            fits = inside_line(block)
            if way == "send":
                fits = jnp.logical_and(fits, inside_line(me[0] + turn))

            @pl.when(fits)
            def _(bit=bit, turn=turn, block=block):
                ref = piece(c, lane, [block] + sel[1:])
                target = (me[0] + (turn if way == "send" else -turn), me[1], me[2])
                act(gather_copy(c, lane, ref, 2 * hop + bit, target))

    def line_hop(c, lane, hop):
        if hop:
            line_each(c, lane, hop - 1, "recv", lambda copy: copy.wait_recv())
        line_each(c, lane, hop, "send", lambda copy: copy.start())

    def side_copy(c, lane, phase):
        axis, second = ((2, 1), (1, 2))[lane]
        sel = [me[0] if c in late else slice(None), me[1], me[2]]
        if phase:
            sel[axis] = slice(None)
        return gather_copy(
            c, lane, piece(c, lane, sel), 2 * hops + phase, moved((axis, second)[phase], 1)
        )

    def gather_line(c, hop):
        for lane in range(2):
            line_hop(c, lane, hop)

    def gather_side(c, phase):
        for lane in range(2):
            if phase:
                side_copy(c, lane, 0).wait_recv()
            elif c not in late:
                line_each(c, lane, hops - 1, "recv", lambda copy: copy.wait_recv())
            side_copy(c, lane, phase).start()

    def gather_end(c):
        for lane in range(2):
            if c in late:
                line_each(c, lane, hops - 1, "recv", lambda copy: copy.wait_recv())
            else:
                side_copy(c, lane, 1).wait_recv()

    late_items = [(c, lane, hop) for hop in range(hops) for c in late for lane in range(2)]

    def late_next():
        if late_items:
            c, lane, hop = late_items.pop(0)
            if hop == 0:
                side_copy(c, lane, 1).wait_recv()
            line_hop(c, lane, hop)

    def gather_sent():
        for c in range(len(kinds)):
            for lane in range(2):
                for hop in range(hops):
                    line_each(c, lane, hop, "send", lambda copy: copy.wait_send())
                for phase in range(2):
                    side_copy(c, lane, phase).wait_send()

    def sum_copies(buffers, i, stage):
        first, second, send, recv = buffers
        if stage == 0:
            ref = first.at[i, mp]
            return [
                pltpu.make_async_remote_copy(
                    src_ref=ref,
                    dst_ref=ref,
                    send_sem=send.at[i, k - 1],
                    recv_sem=recv.at[i, k - 1],
                    device_id=(me[0] * plane + (mp + k) % plane, core),
                    device_id_type=MESH,
                )
                for k in range(1, plane)
            ]
        ref = second.at[i, me[0]]
        return [
            pltpu.make_async_remote_copy(
                src_ref=ref,
                dst_ref=ref,
                send_sem=send.at[i, plane - 1 + k - 1],
                recv_sem=recv.at[i, plane - 1 + k - 1],
                device_id=place(moved(0, k)),
                device_id_type=MESH,
            )
            for k in range(1, n0)
        ]

    narrow_sum = (pa, pb, ps_s, ps_r)
    half_sum = (qa, qb, qs_s, qs_r)
    scalar_sum = (ta, tb, ts_s, ts_r)

    def sum_start(buffers, i):
        for copy in sum_copies(buffers, i, 0):
            copy.start()

    def sum_middle(buffers, i):
        for copy in sum_copies(buffers, i, 0):
            copy.wait()
        first, second = buffers[:2]
        total = first[i, 0]
        for j in range(1, plane):
            total = total + first[i, j]
        second[i, me[0]] = total
        for copy in sum_copies(buffers, i, 1):
            copy.start()

    def sum_end(buffers, i):
        for copy in sum_copies(buffers, i, 1):
            copy.wait()
        second = buffers[1]
        total = second[i, 0]
        for j in range(1, n0):
            total = total + second[i, j]
        return total

    def swap(i):
        return pltpu.make_async_remote_copy(
            src_ref=ex.at[i],
            dst_ref=exr.at[i % 2],
            send_sem=ex_s.at[i],
            recv_sem=ex_r.at[i],
            device_id=other,
            device_id_type=MESH,
        )

    def swap_end(i):
        swap(i).wait()

        def add(b):
            part = pl.ds(pl.multiple_of(b * rows, rows), rows)
            ex[i, part, :] = (
                ex[i, part, :].astype(jnp.float32) + exr[i % 2, part, :].astype(jnp.float32)
            ).astype(jnp.bfloat16)

        loop(blocks, add)

    def weight(w, columns):
        return small[w, :, :, :, :, columns].reshape(plane * n0 * small_rows, columns.size)

    def columns_at(start, size):
        return pl.ds(pl.multiple_of(start, TILE), size)

    def hidden_chunk(weights, i, slot):
        def one(lane):
            columns = columns_at(i * chunk + lane * TILE, TILE)
            matrix = weights[:, :, :, :, columns].reshape(n0 * plane * rows, TILE)
            values = jnp.dot(feats[...], matrix, preferred_element_type=jnp.float32)
            wide[:, columns] = values
            spot = columns_at(lane * TILE, TILE)
            pa[slot, mp, 0:1, spot] = jnp.sum(values, 0, keepdims=True)
            pa[slot, mp, 1:2, spot] = jnp.sum(values * values, 0, keepdims=True)

        loop(2, one)

    def spread(total):
        mean = total[0:1] / total_views
        return mean, lax.rsqrt(total[1:2] / total_views - mean * mean + NORM_EPS)

    def act_tile(start, mean, inverse, norm, act_ref, hat_ref, act_start):
        columns = pl.ds(start, TILE)
        targets = pl.ds(act_start, TILE)
        gain, shift = norm[0:1, columns], norm[1:2, columns]

        def one(b):
            part = pl.ds(pl.multiple_of(b * rows, rows), rows)
            hat = (wide[part, columns] - mean) * inverse
            value = hat * gain + shift
            value = value.astype(jnp.bfloat16)
            gate, square = gelu_parts(value)
            act_ref[b // 2, b % 2, :, targets] = value * gate
            if hat_ref is not None:
                hat_ref[b // 2, b % 2, :, targets] = hat.astype(jnp.bfloat16)
                slope1[b // 2, b % 2, :, targets] = gelu_slope(value, gate, square)

        loop(blocks, one)

    def act_online(i):
        mean, inverse = spread(sum_end(narrow_sum, i))
        inv1[:, pl.ds(i * chunk, chunk)] = inverse
        for n in range(chunk // TILE):
            start = i * chunk + n * TILE
            here = slice(n * TILE, (n + 1) * TILE)
            act_tile(start, mean[:, here], inverse[:, here], proj_norm, act1, hat1, start)

    def act_target(i):
        mean, inverse = spread(sum_end(narrow_sum, 4 + i))
        for n in range(chunk // TILE):
            start = i * chunk + n * TILE
            here = slice(n * TILE, (n + 1) * TILE)
            act_tile(start, mean[:, here], inverse[:, here], target_norm, tact, None, 0)
            product = nt_dot(tact[...].reshape(views, TILE), weight(3, pl.ds(start, TILE)))
            if start == 0:
                acc[...] = product
            else:
                acc[...] += product

    count = []

    def sum_rows(i, columns, first_row, second_row):
        qa[i, mp, 0:1, columns] = first_row
        qa[i, mp, 1:2, columns] = second_row

    def online_middle():
        ex[0] = nt_dot(act1[...].reshape(views, width), weight(0, pl.ds(0, width))).astype(
            jnp.bfloat16
        )
        swap(0).start()
        swap_end(0)
        for side in range(2):

            def one(n):
                columns = columns_at(side * half + n * TILE, TILE)
                values = jnp.dot(ex[0], weight(1, columns), preferred_element_type=jnp.float32)
                sum_rows(
                    side,
                    columns_at(n * TILE, TILE),
                    jnp.sum(values, 0, keepdims=True),
                    jnp.sum(values * values, 0, keepdims=True),
                )

            loop(half // TILE, one)
            sum_start(half_sum, side)

    def online_query():
        for side in range(2):
            mean, inverse = spread(sum_end(half_sum, side))
            inv2[:, pl.ds(side * half, half)] = inverse
            means[:, pl.ds(side * half, half)] = mean
        spare = pl.ds(3 * chunk, TILE)

        def one(n):
            columns = columns_at(n * TILE, TILE)
            wide[:, spare] = jnp.dot(
                ex[0], weight(1, columns), preferred_element_type=jnp.float32
            )
            mean_n, inverse_n = means[:, columns], inv2[:, columns]
            gain, shift = pred_norm[0:1, columns], pred_norm[1:2, columns]

            def tile(b):
                part = pl.ds(pl.multiple_of(b * rows, rows), rows)
                hat = (wide[part, spare] - mean_n) * inverse_n
                value = hat * gain + shift
                value = value.astype(jnp.bfloat16)
                gate, _ = gelu_parts(value)
                act2[b // 2, b % 2, :, columns] = value * gate
                hat2[b // 2, b % 2, :, columns] = hat.astype(jnp.bfloat16)

            loop(blocks, tile)

        loop(width // TILE, one)
        ex[1] = nt_dot(
            act2[...].reshape(views, width), weight(2, pl.ds(0, width))
        ).astype(jnp.bfloat16)
        swap(1).start()

    def forward(tick):
        gather_side(tick, 0)
        for ahead, hop in ((1, 2), (2, 1), (3, 0)):
            if tick + ahead < main:
                gather_line(tick + ahead, hop)
        if tick >= 1:
            for _ in range(LATE_STEPS[tick - 1]):
                late_next()
            gather_side(tick - 1, 1)

    def hidden(slot):
        hidden_chunk(up if slot < 4 else tup, slot % 4, slot)
        sum_start(narrow_sum, slot)

    def after(tick):
        if tick == 2:
            loads[6].wait()
            kept = jnp.sum(jnp.sum(keep[...], 0, keepdims=True), 1, keepdims=True)
            ta[0, mp] = jnp.broadcast_to(kept, (8, 128))
            sum_start(scalar_sum, 0)
        if tick <= 5:
            hidden(tick - 2)
        if tick == 4:
            sum_middle(scalar_sum, 0)
        if 3 <= tick <= 6:
            sum_middle(narrow_sum, tick - 3)
        if tick >= 4:
            act_online(tick - 4)
        if tick == 6:
            count.append(sum_end(scalar_sum, 0))

    gather_line(0, 0)
    take_small()
    gather_side(late[0], 0)
    take(loads[5], tup, rows)
    gather_side(late[1], 0)
    gather_line(1, 0)
    gather_line(0, 1)
    gather_line(2, 0)
    gather_line(1, 1)
    gather_line(0, 2)
    for c in late:
        gather_side(c, 1)
    for tick in range(main - 1):
        forward(tick)
        if tick >= 2:
            gather_end(tick - 2)
            after(tick)
    forward(main - 1)
    after(main - 1)
    online_middle()
    gather_end(main - 3)
    hidden(4)
    gather_side(main - 1, 1)
    gather_end(main)
    hidden(6)
    sum_middle(half_sum, 0)
    sum_middle(half_sum, 1)
    sum_middle(narrow_sum, 4)
    gather_end(main - 2)
    hidden(5)
    gather_end(main + 1)
    online_query()
    act_target(0)
    gather_end(main - 1)
    sum_middle(narrow_sum, 6)
    sum_middle(narrow_sum, 5)
    hidden(7)
    swap_end(1)
    act_target(1)
    sum_middle(narrow_sum, 7)
    act_target(2)
    act_target(3)
    ex[2] = acc[...].astype(jnp.bfloat16)
    swap(2).start()
    gather_sent()
    swap(2).wait()

    scale = -2.0 / count[0][0:1, 0:1]

    def unit_scale(values):
        return lax.rsqrt(jnp.sum(values * values, 1, keepdims=True) + UNIT_EPS)

    even = (lax.broadcasted_iota(jnp.int32, (rows, acc.shape[1]), 0) % 2) == 0

    spot = lax.broadcasted_iota(jnp.int32, (rows, blocks), 1)

    def loss_tile(b, carry):
        part = pl.ds(pl.multiple_of(b * rows, rows), rows)
        query = ex[1, part, :].astype(jnp.float32)
        target = ex[2, part, :].astype(jnp.float32) + exr[0, part, :].astype(jnp.float32)
        target = target * unit_scale(target)
        goal = jnp.where(even, pltpu.roll(target, rows - 1, 0), pltpu.roll(target, 1, 0))
        back = unit_scale(query)
        unit = query * back
        cosine = jnp.sum(unit * goal, 1, keepdims=True)
        kept = jnp.sum(jnp.where(spot == b, keep[...], 0.0), 1, keepdims=True)
        ex[1, part, :] = ((scale * kept * back) * (goal - cosine * unit)).astype(jnp.bfloat16)
        return carry + kept * (2.0 - 2.0 * cosine)

    loss_rows = lax.fori_loop(0, blocks, loss_tile, jnp.zeros((rows, 1), jnp.float32))
    ta[1, mp] = jnp.broadcast_to(jnp.sum(loss_rows, 0, keepdims=True), (8, 128))
    sum_start(scalar_sum, 1)

    def back_norm(i, first, last, w, grads, hat_ref, norm, slope_ref):
        def one(n):
            columns = columns_at(n * TILE, TILE)
            wide[:, columns] = jnp.dot(
                ex[grads], weight(w, columns), preferred_element_type=jnp.float32
            )
            gain, shift = norm[0:1, columns], norm[1:2, columns]

            def tile(b, carry):
                part = pl.ds(pl.multiple_of(b * rows, rows), rows)
                hat = hat_ref[b // 2, b % 2, :, columns].astype(jnp.float32)
                if slope_ref is None:
                    value = hat * gain + shift
                    slope = gelu_slope(value, *gelu_parts(value))
                else:
                    slope = slope_ref[b // 2, b % 2, :, columns].astype(jnp.float32)
                grad = wide[part, columns] * slope
                wide[part, columns] = grad
                cross = grad * hat
                return (
                    carry[0] + jnp.sum(grad.reshape(rows // 8, 8, TILE), 0),
                    carry[1] + jnp.sum(cross.reshape(rows // 8, 8, TILE), 0),
                )

            zero = jnp.zeros((8, TILE), jnp.float32)
            sums = lax.fori_loop(0, blocks, tile, (zero, zero))
            sum_rows(
                i,
                columns_at((n % side_tiles) * TILE, TILE),
                jnp.sum(sums[0], 0, keepdims=True),
                jnp.sum(sums[1], 0, keepdims=True),
            )

        loop(last - first, lambda n: one(first + n))

    side_tiles = half // TILE

    def grad_hidden(stat, hat_ref, norm, inv_ref, columns):
        gain = norm[0:1, columns] * inv_ref[:, columns]
        shift = stat[0:1, columns] / total_views
        slope = stat[1:2, columns] / total_views

        def tile(b):
            part = pl.ds(pl.multiple_of(b * rows, rows), rows)
            hat = hat_ref[b // 2, b % 2, :, columns].astype(jnp.float32)
            hat_ref[b // 2, b % 2, :, columns] = (
                gain * (wide[part, columns] - shift - hat * slope)
            ).astype(jnp.bfloat16)

        loop(blocks, tile)

    def small_grad(w, grads, act_ref):
        def one(n):
            columns = columns_at(n * TILE, TILE)
            right = act_ref[:, :, :, columns].reshape(views, TILE)
            value = tn_dot(ex[grads], right).astype(jnp.bfloat16)
            small[w, :, :, :, :, columns] = value.reshape(n0, n1, n2, small_rows, TILE)

        loop(width // TILE, one)

    def plus(*terms):
        total = terms[0].astype(jnp.float32)
        for term in terms[1:]:
            total = total + term.astype(jnp.float32)
        return total

    def low_plus(*terms):
        return plus(*terms).astype(jnp.bfloat16)

    up_parts = [("line", 0, TILE // 2)]
    up_parts += [("side", TILE + g * chunk, TILE) for g in range(3)]
    up_parts += [("side", TILE + 3 * chunk, TILE // 2)]

    def reduce_copies(kind, g, lane, phase):
        axis, second = ((1, 2), (2, 1))[lane]
        style = up_parts[g][0] if kind == "up" else "side"
        order = (0, axis, second) if style == "line" else (axis, second, 0)
        sems = ((0, 3, 4) if style == "line" else (0, 1, 2))[phase]
        send, recv = (rs_s, rs_r) if kind == "up" else (ss_s, ss_r)
        axis_now = order[phase]
        copies = []
        for k in range(1, grid[axis_now]):
            target = moved(axis_now, k)
            sel = [slice(None)] * 3
            for done in order[:phase]:
                sel[done] = me[done]
            sel[axis_now] = target[axis_now]
            if kind == "small":
                columns = pl.ds(lane * half, half)
                source = small.at[3 - g, sel[0], sel[1], sel[2], :, columns]
                if phase == 0:
                    land = sr1.at[g, :, :, :, columns]
                elif phase == 1:
                    land = sr2.at[g, :, :, columns]
                else:
                    land = sr3.at[g, me[0], :, columns]
            else:
                _, start, size = up_parts[g]
                columns = pl.ds(start + lane * size, size)
                source = tup.at[sel[0], sel[1], sel[2], :, columns]
                if style == "line":
                    if phase == 0:
                        land = (act2 if k < 3 else hat2).at[
                            pl.ds(2 * ((k - 1) % 2), 2), :, :, columns
                        ]
                    elif phase == 1:
                        land = hat2.at[2, :, :, columns]
                    else:
                        land = hat2.at[3, 0, :, columns]
                elif phase == 0:
                    land = act2.at[:, :, :, columns]
                elif phase == 1:
                    land = hat2.at[:, 0, :, columns]
                else:
                    land = hat2.at[me[0], 1, :, columns]
            copies.append(
                pltpu.make_async_remote_copy(
                    src_ref=source,
                    dst_ref=land,
                    send_sem=send.at[g, lane, sems + k - 1],
                    recv_sem=recv.at[g, lane, sems + k - 1],
                    device_id=place(target),
                    device_id_type=MESH,
                )
            )
        return copies

    def reduce_step(kind, g, phase):
        for lane in range(2):
            if phase:
                for copy in reduce_copies(kind, g, lane, phase - 1):
                    copy.wait()
                if kind == "small":
                    small_add(g, lane, phase)
                elif up_parts[g][0] == "line":
                    line_add(g, lane, phase)
                else:
                    side_add(g, lane, phase)
            if phase < 3:
                for copy in reduce_copies(kind, g, lane, phase):
                    copy.start()

    def plane_spot(lane, i):
        return (me[1], i) if lane == 0 else (i, me[2])

    def small_add(g, lane, phase):
        columns = pl.ds(lane * half, half)
        w = 3 - g
        if phase == 1:

            def add(j):
                z, i = j // 2, j % 2
                y, x = plane_spot(lane, i)
                small[w, z, y, x, :, columns] = low_plus(
                    small[w, z, y, x, :, columns], sr1[g, z, i, :, columns]
                )

            loop(n0 * 2, add)
        elif phase == 2:

            def add(z):
                small[w, z, me[1], me[2], :, columns] = low_plus(
                    small[w, z, me[1], me[2], :, columns], sr2[g, z, :, columns]
                )

            loop(n0, add)
        else:
            (qd_out, qu_out, pd_out)[g][:, columns] = low_plus(
                small[w, me[0], me[1], me[2], :, columns],
                *[sr3[g, (me[0] + k) % n0, :, columns] for k in range(1, n0)],
            )

    def side_add(g, lane, phase):
        _, start, size = up_parts[g]
        columns = pl.ds(start + lane * size, size)
        if phase == 1:

            def add(j):
                z, i = j // 2, j % 2
                y, x = plane_spot(lane, i)
                tup[z, y, x, :, columns] = low_plus(
                    tup[z, y, x, :, columns], act2[z, i, :, columns]
                )

            loop(n0 * 2, add)
        elif phase == 2:

            def add(z):
                tup[z, me[1], me[2], :, columns] = low_plus(
                    tup[z, me[1], me[2], :, columns], hat2[z, 0, :, columns]
                )

            loop(n0, add)
        else:
            gu_out[:, columns] = low_plus(
                tup[me[0], me[1], me[2], :, columns],
                *[hat2[(me[0] + k) % n0, 1, :, columns] for k in range(1, n0)],
            )

    def line_add(g, lane, phase):
        _, start, size = up_parts[g]
        columns = pl.ds(start + lane * size, size)
        z = me[0]
        if phase == 1:

            def add(j):
                y, x = j // 2, j % 2
                tup[z, y, x, :, columns] = low_plus(
                    tup[z, y, x, :, columns],
                    act2[y, x, :, columns],
                    act2[2 + y, x, :, columns],
                    hat2[y, x, :, columns],
                )

            loop(plane, add)
        elif phase == 2:

            def add(i):
                y, x = plane_spot(lane, i)
                tup[z, y, x, :, columns] = low_plus(
                    tup[z, y, x, :, columns], hat2[2, i, :, columns]
                )

            loop(2, add)
        else:
            gu_out[:, columns] = low_plus(
                tup[z, me[1], me[2], :, columns], hat2[3, 0, :, columns]
            )

    def pred_half(side):
        pred_stat[:, pl.ds(side * half, half)] = sum_end(half_sum, 2 + side)

        def one(n):
            columns = columns_at(side * half + n * TILE, TILE)
            grad_hidden(pred_stat, hat2, pred_norm, inv2, columns)

        loop(side_tiles, one)
        columns = pl.ds(side * half, half)
        product = nt_dot(hat2[:, :, :, columns].reshape(views, half), weight(1, columns))
        if side == 0:
            acc[...] = product
        else:
            acc[...] += product

    middle_tile = side_tiles + side_tiles // 2
    pred_args = (2, 1, hat2, pred_norm, None)
    back_norm(2, 0, side_tiles, *pred_args)
    sum_start(half_sum, 2)
    back_norm(3, side_tiles, middle_tile, *pred_args)
    sum_middle(half_sum, 2)
    back_norm(3, middle_tile, 2 * side_tiles, *pred_args)
    sum_start(half_sum, 3)
    small_grad(3, 1, act2)
    sum_middle(half_sum, 3)
    reduce_step("small", 0, 0)
    pred_half(0)
    pred_half(1)
    ex[3] = acc[...].astype(jnp.bfloat16)
    swap(3).start()
    small_grad(2, 0, hat2)
    reduce_step("small", 1, 0)
    reduce_step("small", 0, 1)
    swap_end(3)
    proj_args = (0, 3, hat1, proj_norm, slope1)
    back_norm(4, 0, side_tiles, *proj_args)
    sum_start(half_sum, 4)
    back_norm(5, side_tiles, middle_tile, *proj_args)
    sum_middle(half_sum, 4)
    reduce_step("small", 1, 1)
    reduce_step("small", 0, 2)
    back_norm(5, middle_tile, 2 * side_tiles, *proj_args)
    sum_start(half_sum, 5)
    small_grad(1, 3, act1)
    pl.semaphore_signal(ready, inc=1, device_id=other, device_id_type=MESH)
    sum_middle(half_sum, 5)
    reduce_step("small", 2, 0)
    sum_middle(scalar_sum, 1)
    proj_stat[:, pl.ds(0, half)] = sum_end(half_sum, 4)

    def up_hidden(g):
        _, start, size = up_parts[g]
        for n in range(2 * size // TILE):
            grad_hidden(proj_stat, hat1, proj_norm, inv1, pl.ds(start + n * TILE, TILE))

    def up_grad(g):
        _, start, size = up_parts[g]
        columns = pl.ds(start, 2 * size)

        def one(z):
            left = feats[:, columns_at(z * plane * rows, plane * rows)]
            value = tn_dot(left, hat1[:, :, :, columns].reshape(views, 2 * size))
            tup[z, :, :, :, columns] = value.astype(jnp.bfloat16).reshape(n1, n2, rows, 2 * size)

        loop(n0, one)
        reduce_step("up", g, 0)

    parts = ig_s.shape[0]

    def input_copy(q):
        return pltpu.make_async_remote_copy(
            src_ref=act1.at[:, :, :, pl.ds(q * TILE, TILE)],
            dst_ref=act1.at[:, :, :, pl.ds((parts + q) * TILE, TILE)],
            send_sem=ig_s.at[q],
            recv_sem=ig_r.at[q],
            device_id=other,
            device_id_type=MESH,
        )

    def input_product(q, side):
        first = side * (n0 // 2) + q // n1
        matrix = up[first, q % n1].reshape(n2 * rows, width)
        return nt_dot(hat1[...].reshape(views, width), matrix)

    def send_part(q):
        act1[:, :, :, pl.ds(q * TILE, TILE)] = (
            input_product(q, 1 - core).astype(jnp.bfloat16).reshape(n0, 2, rows, TILE)
        )
        input_copy(q).start()

    def own_part(q):
        wide[:, pl.ds(q * TILE, TILE)] = input_product(q, core)

    up_hidden(0)
    up_grad(0)
    up_hidden(1)
    up_grad(1)
    proj_stat[:, pl.ds(half, half)] = sum_end(half_sum, 5)
    for g in (2, 3, 4):
        up_hidden(g)
    up_grad(2)
    reduce_step("small", 2, 1)
    reduce_step("small", 1, 2)
    reduce_step("small", 0, 3)
    pl.semaphore_wait(ready, 1)
    send_part(0)
    reduce_step("up", 1, 1)
    up_grad(3)
    send_part(1)
    send_part(2)
    reduce_step("up", 0, 1)
    reduce_step("up", 2, 1)
    up_grad(4)
    reduce_step("up", 1, 2)
    reduce_step("small", 2, 2)
    reduce_step("small", 1, 3)
    send_part(3)
    own_part(0)
    reduce_step("up", 0, 2)
    reduce_step("up", 3, 1)
    reduce_step("up", 2, 2)
    own_part(1)
    own_part(2)
    reduce_step("up", 4, 1)
    reduce_step("up", 3, 2)
    own_part(3)
    for q in range(parts):
        input_copy(q).wait()

        def add(b, q=q):
            part = pl.ds(pl.multiple_of(b * rows, rows), rows)
            theirs = act1[b // 2, b % 2, :, pl.ds((parts + q) * TILE, TILE)]
            act1[b // 2, b % 2, :, pl.ds(q * TILE, TILE)] = low_plus(
                wide[part, pl.ds(q * TILE, TILE)], theirs
            )

        loop(blocks, add)
    out_copy = pltpu.make_async_copy(
        act1.at[:, :, :, pl.ds(0, parts * TILE)], ig_hbm, load_sem.at[0]
    )
    out_copy.start()
    reduce_step("up", 4, 2)
    reduce_step("small", 2, 3)
    loss_out[...] = (sum_end(scalar_sum, 1) / count[0])[0:1, 0:1]
    for g in range(5):
        reduce_step("up", g, 3)
    out_copy.wait()


def kernel_step(grid, total_views, features, keep, ups, downs, norms):
    n0, n1, n2 = grid
    plane = n1 * n2
    views, depth = features.shape
    rows, width = ups[0].shape
    small_rows = downs[0].shape[0]
    out = small_rows * n0 * plane
    parts = depth // 2 // TILE
    low, full = jnp.bfloat16, jnp.float32
    vm = pltpu.VMEM
    dma = pltpu.SemaphoreType.DMA
    anywhere = pl.BlockSpec(memory_space=pl.ANY)
    inside = pl.BlockSpec(memory_space=pltpu.VMEM)
    spread_shape = (n0, 2, rows, width)
    moves = 2 * (n0 - 1) + 2
    sum_moves = plane - 1 + n0 - 1
    return pl.pallas_call(
        functools.partial(step_kernel, grid, total_views),
        out_shape=(
            jax.ShapeDtypeStruct((n0, 2, rows, depth // 2), low),
            jax.ShapeDtypeStruct((rows, width), low),
            jax.ShapeDtypeStruct((small_rows, width), low),
            jax.ShapeDtypeStruct((small_rows, width), low),
            jax.ShapeDtypeStruct((small_rows, width), low),
            jax.ShapeDtypeStruct((2, width), full),
            jax.ShapeDtypeStruct((2, width), full),
            jax.ShapeDtypeStruct((1, 1), full),
        ),
        in_specs=[anywhere] * 7 + [inside] * 4,
        out_specs=(anywhere,) + (inside,) * 7,
        scratch_shapes=[
            vm((views, depth), low),
            vm((n0, n1, n2, rows, width), low),
            vm((n0, n1, n2, rows, width), low),
            vm((4, n0, n1, n2, small_rows, width), low),
            vm(spread_shape, low),
            vm(spread_shape, low),
            vm(spread_shape, low),
            vm(spread_shape, low),
            vm((views, width), full),
            vm((n0, 2, rows, TILE), low),
            vm((views, out), full),
            vm((4, views, out), low),
            vm((2, views, out), low),
            vm(spread_shape, low),
            vm((3, n0, 2, small_rows, width), low),
            vm((3, n0, small_rows, width), low),
            vm((3, n0, small_rows, width), low),
            vm((1, width), full),
            vm((1, width), full),
            vm((1, width), full),
            vm((8, plane, 2, width // 4), full),
            vm((8, n0, 2, width // 4), full),
            vm((6, plane, 2, width // 2), full),
            vm((6, n0, 2, width // 2), full),
            vm((2, plane, 8, 128), full),
            vm((2, n0, 8, 128), full),
            dma((7,)),
            dma((10, 2, moves)),
            dma((10, 2, moves)),
            dma((8, sum_moves)),
            dma((8, sum_moves)),
            dma((6, sum_moves)),
            dma((6, sum_moves)),
            dma((2, sum_moves)),
            dma((2, sum_moves)),
            dma((4,)),
            dma((4,)),
            dma((5, 2, n0 + 1)),
            dma((5, 2, n0 + 1)),
            dma((3, 2, n0 + 1)),
            dma((3, 2, n0 + 1)),
            dma((parts,)),
            dma((parts,)),
            pltpu.SemaphoreType.REGULAR,
        ],
        compiler_params=pltpu.CompilerParams(
            collective_id=0, has_side_effects=True, vmem_limit_bytes=VMEM_LIMIT
        ),
    )(features, *ups, *downs, *norms, keep)


def step_body(grid, *args):
    (
        features,
        keep_mask,
        proj_up,
        proj_down,
        proj_norm,
        pred_up,
        pred_down,
        pred_norm,
        moment_proj_up,
        moment_proj_down,
        moment_proj_norm,
        moment_pred_up,
        moment_pred_down,
        moment_pred_norm,
        target_up,
        target_down,
        target_norm,
    ) = args
    if grid is None:
        return plain_body(*args)
    total_views = float(features.shape[0] * lax.axis_size("dp"))
    (input_grad, *shards, proj_stat, pred_stat, loss) = kernel_step(
        grid,
        total_views,
        features,
        keep_mask.astype(jnp.float32).reshape(-1, proj_up.shape[0]).T,
        (proj_up, target_up),
        (proj_down, pred_up, pred_down, target_down),
        (proj_norm, pred_norm, target_norm),
    )
    shard_proj_up, shard_pred_down, shard_pred_up, shard_proj_down = (
        shard.astype(jnp.float32) for shard in shards
    )
    input_grad = input_grad.astype(jnp.float32).reshape(features.shape[0], -1)
    grad_proj_norm = proj_stat[::-1]
    grad_pred_norm = pred_stat[::-1]
    return finish(
        total_views,
        args,
        loss.reshape(()),
        input_grad,
        shard_proj_up,
        shard_proj_down,
        grad_proj_norm,
        shard_pred_up,
        shard_pred_down,
        grad_pred_norm,
    )


def solution(mesh):
    placed = (
        P("dp", None),
        P("dp"),
        P("dp", "tensor"),
        P("dp", "tensor"),
        P(None, "tensor"),
        P("dp", "tensor"),
        P("dp", "tensor"),
        P(None, "tensor"),
        P("dp", "tensor"),
        P("dp", "tensor"),
        P(None, "tensor"),
        P("dp", "tensor"),
        P("dp", "tensor"),
        P(None, "tensor"),
        P("dp", "tensor"),
        P("dp", "tensor"),
        P(None, "tensor"),
    )
    return jax.shard_map(
        functools.partial(step_body, GRIDS.get(mesh.shape["dp"])),
        mesh=mesh,
        in_specs=placed,
        out_specs=(
            P(),
            P("dp", "tensor"),
            P("dp", "tensor"),
            P("dp", "tensor"),
            P("dp", "tensor"),
            P("dp", "tensor"),
            P("dp", "tensor"),
            P("dp", "tensor"),
            P(None, "tensor"),
            P(None, "tensor"),
            P(None, "tensor"),
            P("dp", "tensor"),
            P("dp", "tensor"),
            P("dp", "tensor"),
            P("dp", "tensor"),
            P("dp", "tensor"),
            P("dp", "tensor"),
            P(None, "tensor"),
            P(None, "tensor"),
            P(None, "tensor"),
            P("dp", "tensor"),
            P("dp", "tensor"),
            P(None, "tensor"),
        ),
        check_vma=False,
    )
```

```python
import functools
import math

import jax
import jax.numpy as jnp
from jax import lax
from jax.experimental import pallas as pl
from jax.experimental.pallas import tpu as pltpu
from jax.sharding import PartitionSpec as P

NORM_EPS = 1e-05
UNIT_EPS = 1e-06
RATE_PROJ_UP = 9.0
RATE_PROJ_DOWN = 1.2
RATE_PROJ_NORM = 40.0
RATE_PRED_UP = 18.0
RATE_PRED_DOWN = 0.9
RATE_PRED_NORM = 30.0


def across(matrix, weight):
    return lax.dot_general(
        matrix, weight, (((1,), (1,)), ((), ())), preferred_element_type=jnp.float32
    )


def outer_sum(first_op, second_op):
    return lax.dot_general(
        first_op, second_op, (((0,), (0,)), ((), ())), preferred_element_type=jnp.float32
    )


def standard(hidden, col_sum, col_square, total_views):
    middle_mean = col_sum / total_views
    inverse = lax.rsqrt(col_square / total_views - middle_mean * middle_mean + NORM_EPS)
    return ((hidden - middle_mean) * inverse, inverse)


def norm_back(grad_out, scaled, inverse, params, sum_grad, sum_cross, total_views):
    return (
        params[0]
        * inverse
        * (grad_out - sum_grad / total_views - scaled * (sum_cross / total_views))
    )


def unit_rows(values):
    return values * lax.rsqrt(jnp.sum(values * values, 1, keepdims=True) + UNIT_EPS)


def partner(values):
    width = values.shape[1]
    return values.reshape(-1, 2, width)[:, ::-1, :].reshape(-1, width)


def nesterov(weight, moment, grad, rate):
    fresh = 0.5 * moment + grad
    return (fresh, weight - rate * (grad + 0.5 * fresh))


def finish(
    total_views,
    args,
    loss,
    input_grad,
    shard_proj_up,
    shard_proj_down,
    grad_proj_norm,
    shard_pred_up,
    shard_pred_down,
    grad_pred_norm,
):
    (proj_up, proj_down, proj_norm, pred_up, pred_down, pred_norm) = args[2:8]
    (
        moment_proj_up,
        moment_proj_down,
        moment_proj_norm,
        moment_pred_up,
        moment_pred_down,
        moment_pred_norm,
        target_up,
        target_down,
        target_norm,
    ) = args[8:]
    scale = math.sqrt(total_views)
    mom_pu, next_pu = nesterov(proj_up, moment_proj_up, shard_proj_up, RATE_PROJ_UP * scale)
    mom_pd, next_pd = nesterov(proj_down, moment_proj_down, shard_proj_down, RATE_PROJ_DOWN * scale)
    mom_pn, next_pn = nesterov(proj_norm, moment_proj_norm, grad_proj_norm, RATE_PROJ_NORM * scale)
    mom_qu, next_qu = nesterov(pred_up, moment_pred_up, shard_pred_up, RATE_PRED_UP * scale)
    mom_qd, next_qd = nesterov(pred_down, moment_pred_down, shard_pred_down, RATE_PRED_DOWN * scale)
    mom_qn, next_qn = nesterov(pred_norm, moment_pred_norm, grad_pred_norm, RATE_PRED_NORM * scale)
    target_up_next = 0.5 * target_up + 0.5 * next_pu
    target_down_next = 0.5 * target_down + 0.5 * next_pd
    target_norm_next = 0.5 * target_norm + 0.5 * next_pn
    return (
        loss,
        input_grad,
        shard_proj_up,
        mom_pu,
        next_pu,
        shard_proj_down,
        mom_pd,
        next_pd,
        grad_proj_norm,
        mom_pn,
        next_pn,
        shard_pred_up,
        mom_qu,
        next_qu,
        shard_pred_down,
        mom_qd,
        next_qd,
        grad_pred_norm,
        mom_qn,
        next_qn,
        target_up_next,
        target_down_next,
        target_norm_next,
    )


def plain_body(
    features,
    keep_mask,
    proj_up,
    proj_down,
    proj_norm,
    pred_up,
    pred_down,
    pred_norm,
    moment_proj_up,
    moment_proj_down,
    moment_proj_norm,
    moment_pred_up,
    moment_pred_down,
    moment_pred_norm,
    target_up,
    target_down,
    target_norm,
):
    total_views = float(features.shape[0] * lax.axis_size("dp"))
    width = proj_up.shape[1]

    def gathered(parts):
        low = jnp.stack([part.astype(jnp.bfloat16) for part in parts])
        full = lax.all_gather(low, "dp", axis=1, tiled=True)
        return tuple(full[i] for i in range(len(parts)))

    (up_full, tup_full) = gathered((proj_up, target_up))
    (down_full, pup_full, pdown_full, tdown_full) = gathered(
        (proj_down, pred_up, pred_down, target_down)
    )
    keep_float = keep_mask.astype(jnp.float32)
    hidden1 = jnp.dot(features, up_full, preferred_element_type=jnp.float32)
    target_hidden = jnp.dot(features, tup_full, preferred_element_type=jnp.float32)
    sums = lax.psum(
        jnp.stack(
            [
                jnp.sum(hidden1, 0),
                jnp.sum(hidden1 * hidden1, 0),
                jnp.sum(target_hidden, 0),
                jnp.sum(target_hidden * target_hidden, 0),
                jnp.full((width,), jnp.sum(keep_float)),
            ]
        ),
        "dp",
    )
    sum_one, square_one, sum_target, square_target = sums[0], sums[1], sums[2], sums[3]
    count = sums[4, 0]
    scaled1, inverse1 = standard(hidden1, sum_one, square_one, total_views)
    action1, gelu_back1 = jax.vjp(jax.nn.gelu, scaled1 * proj_norm[0] + proj_norm[1])
    action1 = action1.astype(jnp.bfloat16)
    target_scaled, target_inverse = standard(target_hidden, sum_target, square_target, total_views)
    target_action = jax.nn.gelu(target_scaled * target_norm[0] + target_norm[1]).astype(
        jnp.bfloat16
    )
    middle, target_out = (
        lax.psum(across(action1, down_full).astype(jnp.bfloat16), "tensor").astype(jnp.float32),
        lax.psum(across(target_action, tdown_full).astype(jnp.bfloat16), "tensor").astype(
            jnp.float32
        ),
    )
    middle_low = middle.astype(jnp.bfloat16)
    hidden2 = jnp.dot(middle_low, pup_full, preferred_element_type=jnp.float32)
    sum_two, square_two = lax.psum(
        jnp.stack([jnp.sum(hidden2, 0), jnp.sum(hidden2 * hidden2, 0)]), "dp"
    )
    scaled2, inverse2 = standard(hidden2, sum_two, square_two, total_views)
    action2, gelu_back2 = jax.vjp(jax.nn.gelu, scaled2 * pred_norm[0] + pred_norm[1])
    action2 = action2.astype(jnp.bfloat16)
    query = lax.psum(across(action2, pdown_full).astype(jnp.bfloat16), "tensor").astype(jnp.float32)
    goal = partner(unit_rows(target_out))

    def loss_terms(values):
        return jnp.sum(keep_float * (2.0 - 2.0 * jnp.sum(unit_rows(values) * goal, 1)))

    local_loss, loss_back = jax.vjp(loss_terms, query)
    (grad_query,) = loss_back(1.0 / count)
    grad_query = grad_query.astype(jnp.bfloat16)
    grad_pred_down = outer_sum(grad_query, action2)
    (grad_norm2,) = gelu_back2(jnp.dot(grad_query, pdown_full, preferred_element_type=jnp.float32))
    back_sum2, back_cross2, loss_row = lax.psum(
        jnp.stack(
            [
                jnp.sum(grad_norm2, 0),
                jnp.sum(grad_norm2 * scaled2, 0),
                jnp.full((width,), local_loss),
            ]
        ),
        "dp",
    )
    loss_total = loss_row[0]
    grad_hidden2 = norm_back(
        grad_norm2, scaled2, inverse2, pred_norm, back_sum2, back_cross2, total_views
    ).astype(jnp.bfloat16)
    grad_pred_norm = jnp.stack([back_cross2, back_sum2])
    grad_pred_up = outer_sum(middle_low, grad_hidden2)
    grad_middle = lax.psum(across(grad_hidden2, pup_full).astype(jnp.bfloat16), "tensor")
    grad_proj_down = outer_sum(grad_middle, action1)
    (grad_norm1,) = gelu_back1(jnp.dot(grad_middle, down_full, preferred_element_type=jnp.float32))
    back_sum1, back_cross1 = lax.psum(
        jnp.stack([jnp.sum(grad_norm1, 0), jnp.sum(grad_norm1 * scaled1, 0)]), "dp"
    )
    grad_hidden1 = norm_back(
        grad_norm1, scaled1, inverse1, proj_norm, back_sum1, back_cross1, total_views
    ).astype(jnp.bfloat16)
    grad_proj_norm = jnp.stack([back_cross1, back_sum1])
    grad_proj_up = outer_sum(features, grad_hidden1)
    input_grad = lax.psum_scatter(
        across(grad_hidden1, up_full).astype(jnp.bfloat16),
        "tensor",
        scatter_dimension=1,
        tiled=True,
    ).astype(jnp.float32)
    shard_proj_up = lax.psum_scatter(
        grad_proj_up.astype(jnp.bfloat16), "dp", scatter_dimension=0, tiled=True
    ).astype(jnp.float32)
    small = lax.psum_scatter(
        jnp.stack([grad_proj_down, grad_pred_up, grad_pred_down]).astype(jnp.bfloat16),
        "dp",
        scatter_dimension=1,
        tiled=True,
    ).astype(jnp.float32)
    shard_proj_down, shard_pred_up, shard_pred_down = small[0], small[1], small[2]
    loss = loss_total / count
    return finish(
        total_views,
        (
            features,
            keep_mask,
            proj_up,
            proj_down,
            proj_norm,
            pred_up,
            pred_down,
            pred_norm,
            moment_proj_up,
            moment_proj_down,
            moment_proj_norm,
            moment_pred_up,
            moment_pred_down,
            moment_pred_norm,
            target_up,
            target_down,
            target_norm,
        ),
        loss,
        input_grad,
        shard_proj_up,
        shard_proj_down,
        grad_proj_norm,
        shard_pred_up,
        shard_pred_down,
        grad_pred_norm,
    )


MESH = pl.DeviceIdType.MESH
GRIDS = {16: (4, 2, 2)}
TILE = 256
GELU_A = math.sqrt(2.0 / math.pi)
GELU_B = 0.044715
LATE_STEPS = (1, 2, 2, 2, 2, 2, 1)
VMEM_LIMIT = 63 * 1024 * 1024


def loop(count, step):
    def one(i, carry):
        step(i)
        return carry

    lax.fori_loop(0, count, one, 0)


def nt_dot(first_op, second_op):
    return lax.dot_general(
        first_op, second_op, (((1,), (1,)), ((), ())), preferred_element_type=jnp.float32
    )


def tn_dot(first_op, second_op):
    return lax.dot_general(
        first_op, second_op, (((0,), (0,)), ((), ())), preferred_element_type=jnp.float32
    )


def gelu_parts(value):
    square = value * value
    gate = 0.5 + 0.5 * jnp.tanh(value * (GELU_A + (GELU_A * GELU_B) * square))
    return gate, square


def gelu_slope(value, gate, square):
    bend = value * (2.0 * GELU_A + (6.0 * GELU_A * GELU_B) * square)
    return gate * (1.0 + (1.0 - gate) * bend)


def step_kernel(
    grid,
    total_views,
    x_hbm,
    pu_hbm,
    tu_hbm,
    pd_hbm,
    qu_hbm,
    qd_hbm,
    td_hbm,
    proj_norm,
    pred_norm,
    target_norm,
    keep,
    ig_hbm,
    gu_out,
    qd_out,
    qu_out,
    pd_out,
    proj_stat,
    pred_stat,
    loss_out,
    feats,
    up,
    tup,
    small,
    act1,
    hat1,
    act2,
    hat2,
    wide,
    tact,
    acc,
    ex,
    exr,
    slope1,
    sr1,
    sr2,
    sr3,
    inv1,
    inv2,
    means,
    pa,
    pb,
    qa,
    qb,
    ta,
    tb,
    load_sem,
    ag_s,
    ag_r,
    ps_s,
    ps_r,
    qs_s,
    qs_r,
    ts_s,
    ts_r,
    ex_s,
    ex_r,
    rs_s,
    rs_r,
    ss_s,
    ss_r,
    ig_s,
    ig_r,
    ready,
):
    n0, n1, n2 = grid
    plane = n1 * n2
    views, width = wide.shape
    rows = up.shape[3]
    small_rows = small.shape[4]
    blocks = views // rows
    chunk = width // 4
    half = width // 2
    dp = lax.axis_index("dp")
    core = lax.axis_index("tensor")
    me = (dp // plane, (dp // n2) % n1, dp % n2)
    mp = dp % plane
    other = (dp, 1 - core)

    def place(index):
        return ((index[0] * n1 + index[1]) * n2 + index[2], core)

    def moved(axis, k):
        target = list(me)
        target[axis] = (me[axis] + k) % grid[axis]
        return tuple(target)

    barrier = pltpu.get_barrier_semaphore()
    greet = [place(moved(0, k)) for k in range(1, n0)]
    greet += [(me[0] * plane + (mp + k) % plane, core) for k in range(1, plane)]
    greet.append(other)
    for device in greet:
        pl.semaphore_signal(barrier, inc=1, device_id=device, device_id_type=MESH)

    loads = [
        pltpu.make_async_copy(src, wide.at[pl.ds(start, src.shape[0])], load_sem.at[i])
        for i, (src, start) in enumerate(
            (
                (pd_hbm, 2 * rows),
                (qu_hbm, 2 * rows + small_rows),
                (qd_hbm, 2 * rows + 2 * small_rows),
                (td_hbm, 2 * rows + 3 * small_rows),
                (pu_hbm, 0),
                (tu_hbm, rows),
            )
        )
    ]
    loads.append(pltpu.make_async_copy(x_hbm, feats, load_sem.at[6]))
    for i in (4, 0, 1, 2, 3, 5, 6):
        loads[i].start()

    def take(load, buffer, start):
        load.wait()
        buffer[me[0], me[1], me[2]] = wide[pl.ds(start, rows), :].astype(jnp.bfloat16)

    def take_small():
        for w, load in enumerate(loads[:4]):
            load.wait()
            small[w, me[0], me[1], me[2]] = wide[
                pl.ds(2 * rows + w * small_rows, small_rows), :
            ].astype(jnp.bfloat16)

    take(loads[4], up, 0)
    pl.semaphore_wait(barrier, len(greet))

    hops = n0 - 1
    kinds = [("up", i) for i in range(4)] + [("small", 0)]
    kinds += [("target", i) for i in (0, 1, 3)]
    main = len(kinds)
    kinds += [("target", 2), ("small", 1)]
    late = [main + 1, main]

    def piece(c, lane, sel):
        kind, index = kinds[c]
        if kind == "small":
            return small.at[
                pl.ds(2 * index, 2), sel[0], sel[1], sel[2], :, pl.ds(lane * half, half)
            ]
        buffer = up if kind == "up" else tup
        return buffer.at[sel[0], sel[1], sel[2], :, pl.ds(index * chunk + lane * TILE, TILE)]

    def gather_copy(c, lane, ref, sem, target):
        return pltpu.make_async_remote_copy(
            src_ref=ref,
            dst_ref=ref,
            send_sem=ag_s.at[c, lane, sem],
            recv_sem=ag_r.at[c, lane, sem],
            device_id=place(target),
            device_id_type=MESH,
        )

    def inside_line(index):
        return jnp.logical_and(index >= 0, index < n0)

    def line_each(c, lane, hop, way, act):
        sel = [None, slice(None), slice(None)] if c in late else [None, me[1], me[2]]
        for bit, turn in enumerate((1, -1)):
            block = me[0] - turn * (hop if way == "send" else hop + 1)
            fits = inside_line(block)
            if way == "send":
                fits = jnp.logical_and(fits, inside_line(me[0] + turn))

            @pl.when(fits)
            def _(bit=bit, turn=turn, block=block):
                ref = piece(c, lane, [block] + sel[1:])
                target = (me[0] + (turn if way == "send" else -turn), me[1], me[2])
                act(gather_copy(c, lane, ref, 2 * hop + bit, target))

    def line_hop(c, lane, hop):
        if hop:
            line_each(c, lane, hop - 1, "recv", lambda copy: copy.wait_recv())
        line_each(c, lane, hop, "send", lambda copy: copy.start())

    def side_copy(c, lane, phase):
        axis, second = ((2, 1), (1, 2))[lane]
        sel = [me[0] if c in late else slice(None), me[1], me[2]]
        if phase:
            sel[axis] = slice(None)
        return gather_copy(
            c, lane, piece(c, lane, sel), 2 * hops + phase, moved((axis, second)[phase], 1)
        )

    def gather_line(c, hop):
        for lane in range(2):
            line_hop(c, lane, hop)

    def gather_side(c, phase):
        for lane in range(2):
            if phase:
                side_copy(c, lane, 0).wait_recv()
            elif c not in late:
                line_each(c, lane, hops - 1, "recv", lambda copy: copy.wait_recv())
            side_copy(c, lane, phase).start()

    def gather_end(c):
        for lane in range(2):
            if c in late:
                line_each(c, lane, hops - 1, "recv", lambda copy: copy.wait_recv())
            else:
                side_copy(c, lane, 1).wait_recv()

    late_items = [(c, lane, hop) for hop in range(hops) for c in late for lane in range(2)]

    def late_next():
        if late_items:
            c, lane, hop = late_items.pop(0)
            if hop == 0:
                side_copy(c, lane, 1).wait_recv()
            line_hop(c, lane, hop)

    def gather_sent():
        for c in range(len(kinds)):
            for lane in range(2):
                for hop in range(hops):
                    line_each(c, lane, hop, "send", lambda copy: copy.wait_send())
                for phase in range(2):
                    side_copy(c, lane, phase).wait_send()

    def sum_copies(buffers, i, stage):
        first, second, send, recv = buffers
        if stage == 0:
            ref = first.at[i, mp]
            return [
                pltpu.make_async_remote_copy(
                    src_ref=ref,
                    dst_ref=ref,
                    send_sem=send.at[i, k - 1],
                    recv_sem=recv.at[i, k - 1],
                    device_id=(me[0] * plane + (mp + k) % plane, core),
                    device_id_type=MESH,
                )
                for k in range(1, plane)
            ]
        ref = second.at[i, me[0]]
        return [
            pltpu.make_async_remote_copy(
                src_ref=ref,
                dst_ref=ref,
                send_sem=send.at[i, plane - 1 + k - 1],
                recv_sem=recv.at[i, plane - 1 + k - 1],
                device_id=place(moved(0, k)),
                device_id_type=MESH,
            )
            for k in range(1, n0)
        ]

    narrow_sum = (pa, pb, ps_s, ps_r)
    half_sum = (qa, qb, qs_s, qs_r)
    scalar_sum = (ta, tb, ts_s, ts_r)

    def sum_start(buffers, i):
        for copy in sum_copies(buffers, i, 0):
            copy.start()

    def sum_middle(buffers, i):
        for copy in sum_copies(buffers, i, 0):
            copy.wait()
        first, second = buffers[:2]
        total = first[i, 0]
        for j in range(1, plane):
            total = total + first[i, j]
        second[i, me[0]] = total
        for copy in sum_copies(buffers, i, 1):
            copy.start()

    def sum_end(buffers, i):
        for copy in sum_copies(buffers, i, 1):
            copy.wait()
        second = buffers[1]
        total = second[i, 0]
        for j in range(1, n0):
            total = total + second[i, j]
        return total

    def swap(i):
        return pltpu.make_async_remote_copy(
            src_ref=ex.at[i],
            dst_ref=exr.at[i % 2],
            send_sem=ex_s.at[i],
            recv_sem=ex_r.at[i],
            device_id=other,
            device_id_type=MESH,
        )

    def swap_end(i):
        swap(i).wait()

        def add(b):
            part = pl.ds(pl.multiple_of(b * rows, rows), rows)
            ex[i, part, :] = (
                ex[i, part, :].astype(jnp.float32) + exr[i % 2, part, :].astype(jnp.float32)
            ).astype(jnp.bfloat16)

        loop(blocks, add)

    def weight(w, columns):
        return small[w, :, :, :, :, columns].reshape(plane * n0 * small_rows, columns.size)

    def columns_at(start, size):
        return pl.ds(pl.multiple_of(start, TILE), size)

    def hidden_chunk(weights, i, slot):
        def one(lane):
            columns = columns_at(i * chunk + lane * TILE, TILE)
            matrix = weights[:, :, :, :, columns].reshape(n0 * plane * rows, TILE)
            values = jnp.dot(feats[...], matrix, preferred_element_type=jnp.float32)
            wide[:, columns] = values
            spot = columns_at(lane * TILE, TILE)
            pa[slot, mp, 0:1, spot] = jnp.sum(values, 0, keepdims=True)
            pa[slot, mp, 1:2, spot] = jnp.sum(values * values, 0, keepdims=True)

        loop(2, one)

    def spread(total):
        mean = total[0:1] / total_views
        return mean, lax.rsqrt(total[1:2] / total_views - mean * mean + NORM_EPS)

    def act_tile(start, mean, inverse, norm, act_ref, hat_ref, act_start):
        columns = pl.ds(start, TILE)
        targets = pl.ds(act_start, TILE)
        gain, shift = norm[0:1, columns], norm[1:2, columns]

        def one(b):
            part = pl.ds(pl.multiple_of(b * rows, rows), rows)
            hat = (wide[part, columns] - mean) * inverse
            value = hat * gain + shift
            value = value.astype(jnp.bfloat16)
            gate, square = gelu_parts(value)
            act_ref[b // 2, b % 2, :, targets] = value * gate
            if hat_ref is not None:
                hat_ref[b // 2, b % 2, :, targets] = hat.astype(jnp.bfloat16)
                slope1[b // 2, b % 2, :, targets] = gelu_slope(value, gate, square)

        loop(blocks, one)

    def act_online(i):
        mean, inverse = spread(sum_end(narrow_sum, i))
        inv1[:, pl.ds(i * chunk, chunk)] = inverse
        for n in range(chunk // TILE):
            start = i * chunk + n * TILE
            here = slice(n * TILE, (n + 1) * TILE)
            act_tile(start, mean[:, here], inverse[:, here], proj_norm, act1, hat1, start)

    def act_target(i):
        mean, inverse = spread(sum_end(narrow_sum, 4 + i))
        for n in range(chunk // TILE):
            start = i * chunk + n * TILE
            here = slice(n * TILE, (n + 1) * TILE)
            act_tile(start, mean[:, here], inverse[:, here], target_norm, tact, None, 0)
            product = nt_dot(tact[...].reshape(views, TILE), weight(3, pl.ds(start, TILE)))
            if start == 0:
                acc[...] = product
            else:
                acc[...] += product

    count = []

    def sum_rows(i, columns, first_row, second_row):
        qa[i, mp, 0:1, columns] = first_row
        qa[i, mp, 1:2, columns] = second_row

    def online_middle():
        ex[0] = nt_dot(act1[...].reshape(views, width), weight(0, pl.ds(0, width))).astype(
            jnp.bfloat16
        )
        swap(0).start()
        swap_end(0)
        for side in range(2):

            def one(n):
                columns = columns_at(side * half + n * TILE, TILE)
                values = jnp.dot(ex[0], weight(1, columns), preferred_element_type=jnp.float32)
                sum_rows(
                    side,
                    columns_at(n * TILE, TILE),
                    jnp.sum(values, 0, keepdims=True),
                    jnp.sum(values * values, 0, keepdims=True),
                )

            loop(half // TILE, one)
            sum_start(half_sum, side)

    def online_query():
        for side in range(2):
            mean, inverse = spread(sum_end(half_sum, side))
            inv2[:, pl.ds(side * half, half)] = inverse
            means[:, pl.ds(side * half, half)] = mean
        spare = pl.ds(3 * chunk, TILE)

        def one(n):
            columns = columns_at(n * TILE, TILE)
            wide[:, spare] = jnp.dot(
                ex[0], weight(1, columns), preferred_element_type=jnp.float32
            )
            mean_n, inverse_n = means[:, columns], inv2[:, columns]
            gain, shift = pred_norm[0:1, columns], pred_norm[1:2, columns]

            def tile(b):
                part = pl.ds(pl.multiple_of(b * rows, rows), rows)
                hat = (wide[part, spare] - mean_n) * inverse_n
                value = hat * gain + shift
                value = value.astype(jnp.bfloat16)
                gate, _ = gelu_parts(value)
                act2[b // 2, b % 2, :, columns] = value * gate
                hat2[b // 2, b % 2, :, columns] = hat.astype(jnp.bfloat16)

            loop(blocks, tile)

        loop(width // TILE, one)
        ex[1] = nt_dot(
            act2[...].reshape(views, width), weight(2, pl.ds(0, width))
        ).astype(jnp.bfloat16)
        swap(1).start()

    def forward(tick):
        gather_side(tick, 0)
        for ahead, hop in ((1, 2), (2, 1), (3, 0)):
            if tick + ahead < main:
                gather_line(tick + ahead, hop)
        if tick >= 1:
            for _ in range(LATE_STEPS[tick - 1]):
                late_next()
            gather_side(tick - 1, 1)

    def hidden(slot):
        hidden_chunk(up if slot < 4 else tup, slot % 4, slot)
        sum_start(narrow_sum, slot)

    def after(tick):
        if tick == 2:
            loads[6].wait()
            kept = jnp.sum(jnp.sum(keep[...], 0, keepdims=True), 1, keepdims=True)
            ta[0, mp] = jnp.broadcast_to(kept, (8, 128))
            sum_start(scalar_sum, 0)
        if tick <= 5:
            hidden(tick - 2)
        if tick == 4:
            sum_middle(scalar_sum, 0)
        if 3 <= tick <= 6:
            sum_middle(narrow_sum, tick - 3)
        if tick >= 4:
            act_online(tick - 4)
        if tick == 6:
            count.append(sum_end(scalar_sum, 0))

    gather_line(0, 0)
    take_small()
    gather_side(late[0], 0)
    take(loads[5], tup, rows)
    gather_side(late[1], 0)
    gather_line(1, 0)
    gather_line(0, 1)
    gather_line(2, 0)
    gather_line(1, 1)
    gather_line(0, 2)
    for c in late:
        gather_side(c, 1)
    for tick in range(main - 1):
        forward(tick)
        if tick >= 2:
            gather_end(tick - 2)
            after(tick)
    forward(main - 1)
    after(main - 1)
    online_middle()
    gather_end(main - 3)
    hidden(4)
    gather_side(main - 1, 1)
    gather_end(main)
    hidden(6)
    sum_middle(half_sum, 0)
    sum_middle(half_sum, 1)
    sum_middle(narrow_sum, 4)
    gather_end(main - 2)
    hidden(5)
    gather_end(main + 1)
    online_query()
    act_target(0)
    gather_end(main - 1)
    sum_middle(narrow_sum, 6)
    sum_middle(narrow_sum, 5)
    hidden(7)
    swap_end(1)
    act_target(1)
    sum_middle(narrow_sum, 7)
    act_target(2)
    act_target(3)
    ex[2] = acc[...].astype(jnp.bfloat16)
    swap(2).start()
    gather_sent()
    swap(2).wait()

    scale = -2.0 / count[0][0:1, 0:1]

    def unit_scale(values):
        return lax.rsqrt(jnp.sum(values * values, 1, keepdims=True) + UNIT_EPS)

    even = (lax.broadcasted_iota(jnp.int32, (rows, acc.shape[1]), 0) % 2) == 0

    spot = lax.broadcasted_iota(jnp.int32, (rows, blocks), 1)

    def loss_tile(b, carry):
        part = pl.ds(pl.multiple_of(b * rows, rows), rows)
        query = ex[1, part, :].astype(jnp.float32)
        target = ex[2, part, :].astype(jnp.float32) + exr[0, part, :].astype(jnp.float32)
        target = target * unit_scale(target)
        goal = jnp.where(even, pltpu.roll(target, rows - 1, 0), pltpu.roll(target, 1, 0))
        back = unit_scale(query)
        unit = query * back
        cosine = jnp.sum(unit * goal, 1, keepdims=True)
        kept = jnp.sum(jnp.where(spot == b, keep[...], 0.0), 1, keepdims=True)
        ex[1, part, :] = ((scale * kept * back) * (goal - cosine * unit)).astype(jnp.bfloat16)
        return carry + kept * (2.0 - 2.0 * cosine)

    loss_rows = lax.fori_loop(0, blocks, loss_tile, jnp.zeros((rows, 1), jnp.float32))
    ta[1, mp] = jnp.broadcast_to(jnp.sum(loss_rows, 0, keepdims=True), (8, 128))
    sum_start(scalar_sum, 1)

    def back_norm(i, first, last, w, grads, hat_ref, norm, slope_ref):
        def one(n):
            columns = columns_at(n * TILE, TILE)
            wide[:, columns] = jnp.dot(
                ex[grads], weight(w, columns), preferred_element_type=jnp.float32
            )
            gain, shift = norm[0:1, columns], norm[1:2, columns]

            def tile(b, carry):
                part = pl.ds(pl.multiple_of(b * rows, rows), rows)
                hat = hat_ref[b // 2, b % 2, :, columns].astype(jnp.float32)
                if slope_ref is None:
                    value = hat * gain + shift
                    slope = gelu_slope(value, *gelu_parts(value))
                else:
                    slope = slope_ref[b // 2, b % 2, :, columns].astype(jnp.float32)
                grad = wide[part, columns] * slope
                wide[part, columns] = grad
                cross = grad * hat
                return (
                    carry[0] + jnp.sum(grad.reshape(rows // 8, 8, TILE), 0),
                    carry[1] + jnp.sum(cross.reshape(rows // 8, 8, TILE), 0),
                )

            zero = jnp.zeros((8, TILE), jnp.float32)
            sums = lax.fori_loop(0, blocks, tile, (zero, zero))
            sum_rows(
                i,
                columns_at((n % side_tiles) * TILE, TILE),
                jnp.sum(sums[0], 0, keepdims=True),
                jnp.sum(sums[1], 0, keepdims=True),
            )

        loop(last - first, lambda n: one(first + n))

    side_tiles = half // TILE

    def grad_hidden(stat, hat_ref, norm, inv_ref, columns):
        gain = norm[0:1, columns] * inv_ref[:, columns]
        shift = stat[0:1, columns] / total_views
        slope = stat[1:2, columns] / total_views

        def tile(b):
            part = pl.ds(pl.multiple_of(b * rows, rows), rows)
            hat = hat_ref[b // 2, b % 2, :, columns].astype(jnp.float32)
            hat_ref[b // 2, b % 2, :, columns] = (
                gain * (wide[part, columns] - shift - hat * slope)
            ).astype(jnp.bfloat16)

        loop(blocks, tile)

    def small_grad(w, grads, act_ref):
        def one(n):
            columns = columns_at(n * TILE, TILE)
            right = act_ref[:, :, :, columns].reshape(views, TILE)
            value = tn_dot(ex[grads], right).astype(jnp.bfloat16)
            small[w, :, :, :, :, columns] = value.reshape(n0, n1, n2, small_rows, TILE)

        loop(width // TILE, one)

    def plus(*terms):
        total = terms[0].astype(jnp.float32)
        for term in terms[1:]:
            total = total + term.astype(jnp.float32)
        return total

    def low_plus(*terms):
        return plus(*terms).astype(jnp.bfloat16)

    up_parts = [("line", 0, TILE // 2)]
    up_parts += [("side", TILE + g * chunk, TILE) for g in range(3)]
    up_parts += [("side", TILE + 3 * chunk, TILE // 2)]

    def reduce_copies(kind, g, lane, phase):
        axis, second = ((1, 2), (2, 1))[lane]
        style = up_parts[g][0] if kind == "up" else "side"
        order = (0, axis, second) if style == "line" else (axis, second, 0)
        sems = ((0, 3, 4) if style == "line" else (0, 1, 2))[phase]
        send, recv = (rs_s, rs_r) if kind == "up" else (ss_s, ss_r)
        axis_now = order[phase]
        copies = []
        for k in range(1, grid[axis_now]):
            target = moved(axis_now, k)
            sel = [slice(None)] * 3
            for done in order[:phase]:
                sel[done] = me[done]
            sel[axis_now] = target[axis_now]
            if kind == "small":
                columns = pl.ds(lane * half, half)
                source = small.at[3 - g, sel[0], sel[1], sel[2], :, columns]
                if phase == 0:
                    land = sr1.at[g, :, :, :, columns]
                elif phase == 1:
                    land = sr2.at[g, :, :, columns]
                else:
                    land = sr3.at[g, me[0], :, columns]
            else:
                _, start, size = up_parts[g]
                columns = pl.ds(start + lane * size, size)
                source = tup.at[sel[0], sel[1], sel[2], :, columns]
                if style == "line":
                    if phase == 0:
                        land = (act2 if k < 3 else hat2).at[
                            pl.ds(2 * ((k - 1) % 2), 2), :, :, columns
                        ]
                    elif phase == 1:
                        land = hat2.at[2, :, :, columns]
                    else:
                        land = hat2.at[3, 0, :, columns]
                elif phase == 0:
                    land = act2.at[:, :, :, columns]
                elif phase == 1:
                    land = hat2.at[:, 0, :, columns]
                else:
                    land = hat2.at[me[0], 1, :, columns]
            copies.append(
                pltpu.make_async_remote_copy(
                    src_ref=source,
                    dst_ref=land,
                    send_sem=send.at[g, lane, sems + k - 1],
                    recv_sem=recv.at[g, lane, sems + k - 1],
                    device_id=place(target),
                    device_id_type=MESH,
                )
            )
        return copies

    def reduce_step(kind, g, phase):
        for lane in range(2):
            if phase:
                for copy in reduce_copies(kind, g, lane, phase - 1):
                    copy.wait()
                if kind == "small":
                    small_add(g, lane, phase)
                elif up_parts[g][0] == "line":
                    line_add(g, lane, phase)
                else:
                    side_add(g, lane, phase)
            if phase < 3:
                for copy in reduce_copies(kind, g, lane, phase):
                    copy.start()

    def plane_spot(lane, i):
        return (me[1], i) if lane == 0 else (i, me[2])

    def small_add(g, lane, phase):
        columns = pl.ds(lane * half, half)
        w = 3 - g
        if phase == 1:

            def add(j):
                z, i = j // 2, j % 2
                y, x = plane_spot(lane, i)
                small[w, z, y, x, :, columns] = low_plus(
                    small[w, z, y, x, :, columns], sr1[g, z, i, :, columns]
                )

            loop(n0 * 2, add)
        elif phase == 2:

            def add(z):
                small[w, z, me[1], me[2], :, columns] = low_plus(
                    small[w, z, me[1], me[2], :, columns], sr2[g, z, :, columns]
                )

            loop(n0, add)
        else:
            (qd_out, qu_out, pd_out)[g][:, columns] = low_plus(
                small[w, me[0], me[1], me[2], :, columns],
                *[sr3[g, (me[0] + k) % n0, :, columns] for k in range(1, n0)],
            )

    def side_add(g, lane, phase):
        _, start, size = up_parts[g]
        columns = pl.ds(start + lane * size, size)
        if phase == 1:

            def add(j):
                z, i = j // 2, j % 2
                y, x = plane_spot(lane, i)
                tup[z, y, x, :, columns] = low_plus(
                    tup[z, y, x, :, columns], act2[z, i, :, columns]
                )

            loop(n0 * 2, add)
        elif phase == 2:

            def add(z):
                tup[z, me[1], me[2], :, columns] = low_plus(
                    tup[z, me[1], me[2], :, columns], hat2[z, 0, :, columns]
                )

            loop(n0, add)
        else:
            gu_out[:, columns] = low_plus(
                tup[me[0], me[1], me[2], :, columns],
                *[hat2[(me[0] + k) % n0, 1, :, columns] for k in range(1, n0)],
            )

    def line_add(g, lane, phase):
        _, start, size = up_parts[g]
        columns = pl.ds(start + lane * size, size)
        z = me[0]
        if phase == 1:

            def add(j):
                y, x = j // 2, j % 2
                tup[z, y, x, :, columns] = low_plus(
                    tup[z, y, x, :, columns],
                    act2[y, x, :, columns],
                    act2[2 + y, x, :, columns],
                    hat2[y, x, :, columns],
                )

            loop(plane, add)
        elif phase == 2:

            def add(i):
                y, x = plane_spot(lane, i)
                tup[z, y, x, :, columns] = low_plus(
                    tup[z, y, x, :, columns], hat2[2, i, :, columns]
                )

            loop(2, add)
        else:
            gu_out[:, columns] = low_plus(
                tup[z, me[1], me[2], :, columns], hat2[3, 0, :, columns]
            )

    def pred_half(side):
        pred_stat[:, pl.ds(side * half, half)] = sum_end(half_sum, 2 + side)

        def one(n):
            columns = columns_at(side * half + n * TILE, TILE)
            grad_hidden(pred_stat, hat2, pred_norm, inv2, columns)

        loop(side_tiles, one)
        columns = pl.ds(side * half, half)
        product = nt_dot(hat2[:, :, :, columns].reshape(views, half), weight(1, columns))
        if side == 0:
            acc[...] = product
        else:
            acc[...] += product

    middle_tile = side_tiles + side_tiles // 2
    pred_args = (2, 1, hat2, pred_norm, None)
    back_norm(2, 0, side_tiles, *pred_args)
    sum_start(half_sum, 2)
    back_norm(3, side_tiles, middle_tile, *pred_args)
    sum_middle(half_sum, 2)
    back_norm(3, middle_tile, 2 * side_tiles, *pred_args)
    sum_start(half_sum, 3)
    small_grad(3, 1, act2)
    sum_middle(half_sum, 3)
    reduce_step("small", 0, 0)
    pred_half(0)
    pred_half(1)
    ex[3] = acc[...].astype(jnp.bfloat16)
    swap(3).start()
    small_grad(2, 0, hat2)
    reduce_step("small", 1, 0)
    reduce_step("small", 0, 1)
    swap_end(3)
    proj_args = (0, 3, hat1, proj_norm, slope1)
    back_norm(4, 0, side_tiles, *proj_args)
    sum_start(half_sum, 4)
    back_norm(5, side_tiles, middle_tile, *proj_args)
    sum_middle(half_sum, 4)
    reduce_step("small", 1, 1)
    reduce_step("small", 0, 2)
    back_norm(5, middle_tile, 2 * side_tiles, *proj_args)
    sum_start(half_sum, 5)
    small_grad(1, 3, act1)
    pl.semaphore_signal(ready, inc=1, device_id=other, device_id_type=MESH)
    sum_middle(half_sum, 5)
    reduce_step("small", 2, 0)
    sum_middle(scalar_sum, 1)
    proj_stat[:, pl.ds(0, half)] = sum_end(half_sum, 4)

    def up_hidden(g):
        _, start, size = up_parts[g]
        for n in range(2 * size // TILE):
            grad_hidden(proj_stat, hat1, proj_norm, inv1, pl.ds(start + n * TILE, TILE))

    def up_grad(g):
        _, start, size = up_parts[g]
        columns = pl.ds(start, 2 * size)

        def one(z):
            left = feats[:, columns_at(z * plane * rows, plane * rows)]
            value = tn_dot(left, hat1[:, :, :, columns].reshape(views, 2 * size))
            tup[z, :, :, :, columns] = value.astype(jnp.bfloat16).reshape(n1, n2, rows, 2 * size)

        loop(n0, one)
        reduce_step("up", g, 0)

    parts = ig_s.shape[0]

    def input_copy(q):
        return pltpu.make_async_remote_copy(
            src_ref=act1.at[:, :, :, pl.ds(q * TILE, TILE)],
            dst_ref=act1.at[:, :, :, pl.ds((parts + q) * TILE, TILE)],
            send_sem=ig_s.at[q],
            recv_sem=ig_r.at[q],
            device_id=other,
            device_id_type=MESH,
        )

    def input_product(q, side):
        first = side * (n0 // 2) + q // n1
        matrix = up[first, q % n1].reshape(n2 * rows, width)
        return nt_dot(hat1[...].reshape(views, width), matrix)

    def send_part(q):
        act1[:, :, :, pl.ds(q * TILE, TILE)] = (
            input_product(q, 1 - core).astype(jnp.bfloat16).reshape(n0, 2, rows, TILE)
        )
        input_copy(q).start()

    def own_part(q):
        wide[:, pl.ds(q * TILE, TILE)] = input_product(q, core)

    up_hidden(0)
    up_grad(0)
    up_hidden(1)
    up_grad(1)
    proj_stat[:, pl.ds(half, half)] = sum_end(half_sum, 5)
    for g in (2, 3, 4):
        up_hidden(g)
    up_grad(2)
    reduce_step("small", 2, 1)
    reduce_step("small", 1, 2)
    reduce_step("small", 0, 3)
    pl.semaphore_wait(ready, 1)
    send_part(0)
    reduce_step("up", 1, 1)
    up_grad(3)
    send_part(1)
    reduce_step("up", 2, 1)
    up_grad(4)
    reduce_step("up", 0, 1)
    send_part(2)
    reduce_step("up", 1, 2)
    reduce_step("small", 2, 2)
    reduce_step("small", 1, 3)
    send_part(3)
    own_part(0)
    reduce_step("up", 0, 2)
    reduce_step("up", 3, 1)
    reduce_step("up", 2, 2)
    own_part(1)
    own_part(2)
    reduce_step("up", 4, 1)
    reduce_step("up", 3, 2)
    own_part(3)
    for q in range(parts):
        input_copy(q).wait()

        def add(b, q=q):
            part = pl.ds(pl.multiple_of(b * rows, rows), rows)
            theirs = act1[b // 2, b % 2, :, pl.ds((parts + q) * TILE, TILE)]
            act1[b // 2, b % 2, :, pl.ds(q * TILE, TILE)] = low_plus(
                wide[part, pl.ds(q * TILE, TILE)], theirs
            )

        loop(blocks, add)
    out_copy = pltpu.make_async_copy(
        act1.at[:, :, :, pl.ds(0, parts * TILE)], ig_hbm, load_sem.at[0]
    )
    out_copy.start()
    reduce_step("up", 4, 2)
    reduce_step("small", 2, 3)
    loss_out[...] = (sum_end(scalar_sum, 1) / count[0])[0:1, 0:1]
    for g in range(5):
        reduce_step("up", g, 3)
    out_copy.wait()


def kernel_step(grid, total_views, features, keep, ups, downs, norms):
    n0, n1, n2 = grid
    plane = n1 * n2
    views, depth = features.shape
    rows, width = ups[0].shape
    small_rows = downs[0].shape[0]
    out = small_rows * n0 * plane
    parts = depth // 2 // TILE
    low, full = jnp.bfloat16, jnp.float32
    vm = pltpu.VMEM
    dma = pltpu.SemaphoreType.DMA
    anywhere = pl.BlockSpec(memory_space=pl.ANY)
    inside = pl.BlockSpec(memory_space=pltpu.VMEM)
    spread_shape = (n0, 2, rows, width)
    moves = 2 * (n0 - 1) + 2
    sum_moves = plane - 1 + n0 - 1
    return pl.pallas_call(
        functools.partial(step_kernel, grid, total_views),
        out_shape=(
            jax.ShapeDtypeStruct((n0, 2, rows, depth // 2), low),
            jax.ShapeDtypeStruct((rows, width), low),
            jax.ShapeDtypeStruct((small_rows, width), low),
            jax.ShapeDtypeStruct((small_rows, width), low),
            jax.ShapeDtypeStruct((small_rows, width), low),
            jax.ShapeDtypeStruct((2, width), full),
            jax.ShapeDtypeStruct((2, width), full),
            jax.ShapeDtypeStruct((1, 1), full),
        ),
        in_specs=[anywhere] * 7 + [inside] * 4,
        out_specs=(anywhere,) + (inside,) * 7,
        scratch_shapes=[
            vm((views, depth), low),
            vm((n0, n1, n2, rows, width), low),
            vm((n0, n1, n2, rows, width), low),
            vm((4, n0, n1, n2, small_rows, width), low),
            vm(spread_shape, low),
            vm(spread_shape, low),
            vm(spread_shape, low),
            vm(spread_shape, low),
            vm((views, width), full),
            vm((n0, 2, rows, TILE), low),
            vm((views, out), full),
            vm((4, views, out), low),
            vm((2, views, out), low),
            vm(spread_shape, low),
            vm((3, n0, 2, small_rows, width), low),
            vm((3, n0, small_rows, width), low),
            vm((3, n0, small_rows, width), low),
            vm((1, width), full),
            vm((1, width), full),
            vm((1, width), full),
            vm((8, plane, 2, width // 4), full),
            vm((8, n0, 2, width // 4), full),
            vm((6, plane, 2, width // 2), full),
            vm((6, n0, 2, width // 2), full),
            vm((2, plane, 8, 128), full),
            vm((2, n0, 8, 128), full),
            dma((7,)),
            dma((10, 2, moves)),
            dma((10, 2, moves)),
            dma((8, sum_moves)),
            dma((8, sum_moves)),
            dma((6, sum_moves)),
            dma((6, sum_moves)),
            dma((2, sum_moves)),
            dma((2, sum_moves)),
            dma((4,)),
            dma((4,)),
            dma((5, 2, n0 + 1)),
            dma((5, 2, n0 + 1)),
            dma((3, 2, n0 + 1)),
            dma((3, 2, n0 + 1)),
            dma((parts,)),
            dma((parts,)),
            pltpu.SemaphoreType.REGULAR,
        ],
        compiler_params=pltpu.CompilerParams(
            collective_id=0, has_side_effects=True, vmem_limit_bytes=VMEM_LIMIT
        ),
    )(features, *ups, *downs, *norms, keep)


def step_body(grid, *args):
    (
        features,
        keep_mask,
        proj_up,
        proj_down,
        proj_norm,
        pred_up,
        pred_down,
        pred_norm,
        moment_proj_up,
        moment_proj_down,
        moment_proj_norm,
        moment_pred_up,
        moment_pred_down,
        moment_pred_norm,
        target_up,
        target_down,
        target_norm,
    ) = args
    if grid is None:
        return plain_body(*args)
    total_views = float(features.shape[0] * lax.axis_size("dp"))
    (input_grad, *shards, proj_stat, pred_stat, loss) = kernel_step(
        grid,
        total_views,
        features,
        keep_mask.astype(jnp.float32).reshape(-1, proj_up.shape[0]).T,
        (proj_up, target_up),
        (proj_down, pred_up, pred_down, target_down),
        (proj_norm, pred_norm, target_norm),
    )
    shard_proj_up, shard_pred_down, shard_pred_up, shard_proj_down = (
        shard.astype(jnp.float32) for shard in shards
    )
    input_grad = input_grad.astype(jnp.float32).reshape(features.shape[0], -1)
    grad_proj_norm = proj_stat[::-1]
    grad_pred_norm = pred_stat[::-1]
    return finish(
        total_views,
        args,
        loss.reshape(()),
        input_grad,
        shard_proj_up,
        shard_proj_down,
        grad_proj_norm,
        shard_pred_up,
        shard_pred_down,
        grad_pred_norm,
    )


def solution(mesh):
    placed = (
        P("dp", None),
        P("dp"),
        P("dp", "tensor"),
        P("dp", "tensor"),
        P(None, "tensor"),
        P("dp", "tensor"),
        P("dp", "tensor"),
        P(None, "tensor"),
        P("dp", "tensor"),
        P("dp", "tensor"),
        P(None, "tensor"),
        P("dp", "tensor"),
        P("dp", "tensor"),
        P(None, "tensor"),
        P("dp", "tensor"),
        P("dp", "tensor"),
        P(None, "tensor"),
    )
    return jax.shard_map(
        functools.partial(step_body, GRIDS.get(mesh.shape["dp"])),
        mesh=mesh,
        in_specs=placed,
        out_specs=(
            P(),
            P("dp", "tensor"),
            P("dp", "tensor"),
            P("dp", "tensor"),
            P("dp", "tensor"),
            P("dp", "tensor"),
            P("dp", "tensor"),
            P("dp", "tensor"),
            P(None, "tensor"),
            P(None, "tensor"),
            P(None, "tensor"),
            P("dp", "tensor"),
            P("dp", "tensor"),
            P("dp", "tensor"),
            P("dp", "tensor"),
            P("dp", "tensor"),
            P("dp", "tensor"),
            P(None, "tensor"),
            P(None, "tensor"),
            P(None, "tensor"),
            P("dp", "tensor"),
            P("dp", "tensor"),
            P(None, "tensor"),
        ),
        check_vma=False,
    )
```
